32 devices in a mesh: dp: 32 (over z, y, x, core).
Axes of the slice: x: 2, y: 2, z: 4, core: 2. Of those that a mesh axis runs over, the one named last changes fastest.
Arguments:
- mel_input: float32 [32, 160, 1024], P('dp'), may hold values from -6 to 6
- lengths: int32 [32], P('dp'), may hold values from 200 to 1000, as said below
- norm_bias: float32 [2, 160], replicated, may hold values from -3 to 3
- norm_logs: float32 [2, 160], replicated, may hold values from -1.75 to 1.75
- mix_weight: float32 [2, 4, 4], replicated, as said below
- start_weight: float32 [2, 192, 80], replicated, may hold values from -0.625 to 0.625
- start_bias: float32 [2, 192], replicated, may hold values from -3 to 3
- conv_weight: float32 [2, 4, 384, 960], replicated, may hold values from -0.1875 to 0.1875
- conv_bias: float32 [2, 4, 384], replicated, may hold values from -3 to 3
- res_weight: float32 [2, 3, 384, 192], replicated, may hold values from -0.4375 to 0.4375
- res_bias: float32 [2, 3, 384], replicated, may hold values from -1.75 to 1.75
- last_weight: float32 [2, 192, 192], replicated, may hold values from -0.4375 to 0.4375
- last_bias: float32 [2, 192], replicated, may hold values from -1.75 to 1.75
- end_weight: float32 [2, 160, 192], replicated, may hold values from -0.3125 to 0.3125
- end_bias: float32 [2, 160], replicated, may hold values from -1.25 to 1.25
- grad_out: float32 [32, 160, 1024], P('dp'), may hold values from -6 to 6
- grad_logdet: float32 [32], P('dp'), may hold values from -6 to 6
Outputs:
- flowed: float32 [32, 160, 1024], P('dp')
- logdet_frame: float32 [32], P('dp')
- grad_input: float32 [32, 160, 1024], P('dp')
- grad_norm_bias: float32 [2, 160], replicated
- grad_norm_logs: float32 [2, 160], replicated
- grad_mix_weight: float32 [2, 4, 4], replicated
- grad_start_weight: float32 [2, 192, 80], replicated
- grad_start_bias: float32 [2, 192], replicated
- grad_conv_weight: float32 [2, 4, 384, 960], replicated
- grad_conv_bias: float32 [2, 4, 384], replicated
- grad_res_weight: float32 [2, 3, 384, 192], replicated
- grad_res_bias: float32 [2, 3, 384], replicated
- grad_last_weight: float32 [2, 192, 192], replicated
- grad_last_bias: float32 [2, 192], replicated
- grad_end_weight: float32 [2, 160, 192], replicated
- grad_end_bias: float32 [2, 160], replicated
The draws below stay inside these ranges and needn't reach their ends.
Inputs may be any that keep to these rules, and one draw needn't show every extreme that they name: `lengths`: some utterance has exactly 1000 frames. `mix_weight`: in every matrix each diagonal entry is positive and larger than the sum of magnitudes of the other entries of its row.
All inputs are finite; a program needn't handle non-finite values.
Results may differ from the reference program's by a relative error of at most 0.0003.
Values sent between devices are 32-bit elements; how exact they have to be, the bound alone decides.
A program may use at most 256 MiB of HBM per device.

```python
import jax
import jax.numpy as jnp
from jax import lax

C = 160
HALF = 80
H = 192
KERNEL = 5
GROUP = 4
LAYERS = 4
BLOCKS = 2
SLOT = 1024
LONGEST = 1000
UTTS = 32


def draw_lengths(key, part):
    key = jax.random.fold_in(key, 11)
    first_key, second_key = jax.random.split(key)
    values = jax.random.randint(first_key, (UTTS,), LONGEST // 5, LONGEST + 1)
    chosen = jax.random.randint(second_key, (), 0, UTTS)
    return jnp.where(jnp.arange(UTTS) == chosen, LONGEST, values).astype(jnp.int32)


def draw_mix_weight(key, part):
    key = jax.random.fold_in(key, 5)
    first_key, second_key = jax.random.split(key)
    diagonal = jax.random.uniform(first_key, (BLOCKS, GROUP), jnp.float32, 0.8, 1.2)
    offdiag = jax.random.uniform(second_key, (BLOCKS, GROUP, GROUP), jnp.float32, -0.25, 0.25)
    identity = jnp.eye(GROUP, dtype=jnp.float32)
    return offdiag * (1.0 - identity) + diagonal[:, :, None] * identity


def block_levels(key, dims, cuts, smallest, top_value):
    loudness = 1.0
    for dim, blocks in cuts:
        draws = jax.random.uniform(jax.random.fold_in(jax.random.fold_in(key, 6), dim), (blocks,), jnp.float32, smallest / len(cuts), top_value / len(cuts))
        loudness = loudness * jnp.repeat(jnp.exp(draws), dims[dim] // blocks).reshape((-1,) + (1,) * (len(dims) - 1 - dim))
    return loudness


def noise(rng, dims, deviation, bound, cuts=(), held_as=jnp.bfloat16):
    result = deviation * jax.random.normal(rng, dims, jnp.float32)
    if cuts:
        result = result * block_levels(rng, dims, cuts, -0.22, 0.18)
    return jnp.clip(result, -bound, bound).astype(held_as)


def setup_inputs(seed: int = 0) -> dict:
    seeds = jax.random.split(jax.random.key(seed), 18)
    return {
        "mel_input": noise(seeds[0], (UTTS, C, SLOT), 1.0, 6.0, ((0, 32),), jnp.float32),
        "lengths": draw_lengths(jax.random.fold_in(seeds[17], 71), 0),
        "norm_bias": noise(seeds[2], (BLOCKS, C), 0.5, 3.0, (), jnp.float32),
        "norm_logs": noise(seeds[3], (BLOCKS, C), 0.3, 1.75, (), jnp.float32),
        "mix_weight": draw_mix_weight(jax.random.fold_in(seeds[17], 71), 0),
        "start_weight": noise(seeds[5], (BLOCKS, H, HALF), HALF ** -0.5, 0.625, (), jnp.float32),
        "start_bias": noise(seeds[6], (BLOCKS, H), 0.5, 3.0, (), jnp.float32),
        "conv_weight": noise(seeds[7], (BLOCKS, LAYERS, 2 * H, KERNEL * H), (KERNEL * H) ** -0.5, 0.1875, (), jnp.float32),
        "conv_bias": noise(seeds[8], (BLOCKS, LAYERS, 2 * H), 0.5, 3.0, (), jnp.float32),
        "res_weight": noise(seeds[9], (BLOCKS, LAYERS - 1, 2 * H, H), H ** -0.5, 0.4375, (), jnp.float32),
        "res_bias": noise(seeds[10], (BLOCKS, LAYERS - 1, 2 * H), 0.3, 1.75, (), jnp.float32),
        "last_weight": noise(seeds[11], (BLOCKS, H, H), H ** -0.5, 0.4375, (), jnp.float32),
        "last_bias": noise(seeds[12], (BLOCKS, H), 0.3, 1.75, (), jnp.float32),
        "end_weight": noise(seeds[13], (BLOCKS, C, H), (2 * H) ** -0.5, 0.3125, (), jnp.float32),
        "end_bias": noise(seeds[14], (BLOCKS, C), 0.2, 1.25, (), jnp.float32),
        "grad_out": noise(seeds[15], (UTTS, C, SLOT), 1.0, 6.0, ((0, 32),), jnp.float32),
        "grad_logdet": noise(seeds[16], (UTTS,), 1.0, 6.0, ((0, 32),), jnp.float32),
    }


precise = lax.Precision.HIGHEST

@jax.custom_vjp
def low(v):
    return lax.optimization_barrier(v.astype(jnp.bfloat16)).astype(jnp.float32)

@jax.custom_vjp
def low_back(v):
    return v

def low_keep(v):
    return (low(v), None)

def low_pass(kept, grad):
    return (grad,)

def back_keep(v):
    return (v, None)

def back_low(kept, grad):
    return (low(grad),)
low.defvjp(low_keep, low_pass)
low_back.defvjp(back_keep, back_low)

def apply(weight, inputs):
    return jnp.einsum('oc,ucs->uos', weight, inputs, precision=precise)

def grouped(inputs):
    utterances, channels, frames = inputs.shape
    reshaped = inputs.reshape(utterances, 2, channels // 4, 2, frames)
    return jnp.transpose(reshaped, (0, 1, 3, 2, 4)).reshape(utterances, 4, channels // 4, frames)

def ungrouped(inputs):
    utterances, members, quarter, frames = inputs.shape
    reshaped = inputs.reshape(utterances, 2, 2, quarter, frames)
    return jnp.transpose(reshaped, (0, 1, 3, 2, 4)).reshape(utterances, 4 * quarter, frames)

def shifted(hidden, kernel):
    reach_len = kernel // 2
    frames = hidden.shape[2]
    padded = jnp.pad(hidden, ((0, 0), (0, 0), (reach_len, reach_len)))
    return jnp.concatenate([padded[:, :, offset:offset + frames] for offset in range(kernel)], axis=1)

def flow_block(params, inputs, frame_mask, lengths_f):
    norm_bias, norm_logs, mix_weight, start_weight, start_bias, conv_weight, conv_bias, res_weight, res_bias, last_weight, last_bias, end_weight, end_bias = params
    mask_col = frame_mask[:, None, :]
    normed = (norm_bias[None, :, None] + jnp.exp(norm_logs)[None, :, None] * inputs) * mask_col
    channels = inputs.shape[1]
    half_c = channels // 2
    mixed = ungrouped(jnp.einsum('ij,ujcs->uics', mix_weight, grouped(normed), precision=precise))
    passed = mixed[:, :half_c]
    changed = mixed[:, half_c:]
    hidden_size = start_weight.shape[0]
    kernel = conv_weight.shape[2] // hidden_size
    hidden = (apply(start_weight, passed) + start_bias[None, :, None]) * mask_col
    skipped = jnp.zeros_like(hidden)
    for layer_idx in range(LAYERS):
        conv_out = apply(conv_weight[layer_idx], shifted(hidden, kernel)) + conv_bias[layer_idx][None, :, None]
        gated = jnp.tanh(conv_out[:, :hidden_size]) * jax.nn.sigmoid(conv_out[:, hidden_size:])
        if layer_idx < LAYERS - 1:
            res_out = apply(res_weight[layer_idx], gated) + res_bias[layer_idx][None, :, None]
            hidden = (hidden + res_out[:, :hidden_size]) * mask_col
            skipped = skipped + res_out[:, hidden_size:]
        else:
            skipped = skipped + apply(last_weight, gated) + last_bias[None, :, None]
    wavenet = skipped * mask_col
    out_proj = apply(end_weight, wavenet) + end_bias[None, :, None]
    log_scale = out_proj[:, half_c:]
    moved = (out_proj[:, :half_c] + jnp.exp(log_scale) * changed) * mask_col
    det_part = jnp.sum(norm_logs) * lengths_f
    det_part = det_part + jnp.log(jnp.linalg.det(mix_weight)) * (channels // 4) * lengths_f
    det_part = det_part + lax.optimization_barrier(jnp.sum(log_scale * mask_col, axis=(1, 2)))
    return (jnp.concatenate([passed, moved], axis=1), det_part)

def reference(mel_input, lengths, norm_bias, norm_logs, mix_weight, start_weight, start_bias, conv_weight, conv_bias, res_weight, res_bias, last_weight, last_bias, end_weight, end_bias, grad_out, grad_logdet):
    params = (norm_bias, norm_logs, mix_weight, start_weight, start_bias, conv_weight, conv_bias, res_weight, res_bias, last_weight, last_bias, end_weight, end_bias)
    batches = UTTS // 4
    frame_index = jnp.arange(SLOT, dtype=jnp.int32)

    def forward(weights, data_in, frame_mask, lengths_f):
        flowing = data_in
        det_sum = jnp.zeros((data_in.shape[0],), jnp.float32)
        for block_idx in range(BLOCKS):
            flowing, det_part = flow_block(tuple((weight_arr[block_idx] for weight_arr in weights)), flowing, frame_mask, lengths_f)
            det_sum = det_sum + det_part
        return (flowing, det_sum / lengths_f)

    def group_step(totals, element):
        data_in, lens_group, cot_out, cot_det = element
        frame_mask = (frame_index[None, :] < lens_group[:, None]).astype(jnp.float32)
        lengths_f = lens_group.astype(jnp.float32)
        (flowing, det_frame), pullback = jax.vjp(lambda weights, values: forward(weights, values, frame_mask, lengths_f), params, data_in)
        grads_w, grads_in = pullback((cot_out, cot_det))
        totals = jax.tree.map(lambda earlier, later: earlier + later, totals, grads_w)
        return (totals, (flowing, det_frame, grads_in))
    zero_grads = jax.tree.map(jnp.zeros_like, params)
    elements = (mel_input.reshape(batches, 4, C, SLOT), lengths.reshape(batches, 4), grad_out.reshape(batches, 4, C, SLOT), grad_logdet.reshape(batches, 4))
    totals, (flowing, det_frame, grads_in) = lax.scan(group_step, zero_grads, elements)
    return (flowing.reshape(UTTS, C, SLOT), det_frame.reshape(UTTS), grads_in.reshape(UTTS, C, SLOT), totals[0], totals[1], totals[2], totals[3], totals[4], totals[5], totals[6], totals[7], totals[8], totals[9], totals[10], totals[11], totals[12])
```

```python
import functools

import jax
import jax.numpy as jnp
from jax import lax
from jax.experimental import pallas as pl
from jax.experimental.pallas import tpu as pltpu
from jax.sharding import PartitionSpec as P

f32, bf16 = jnp.float32, jnp.bfloat16
NN = (((1,), (0,)), ((), ()))
NT = (((1,), (1,)), ((), ()))
TN = (((0,), (0,)), ((), ()))
VMEM_LIMIT = 60 * 2**20


def dot(left, right, form=NN):
    return lax.dot_general(left, right, form, preferred_element_type=f32)


def split(value):
    high = value.astype(bf16)
    return high, (value - high.astype(f32)).astype(bf16)


def dot3(left, right, form=NN):
    (left_high, left_low), (right_high, right_low) = left, right
    return (
        dot(left_high, right_high, form)
        + dot(left_high, right_low, form)
        + dot(left_low, right_high, form)
    )


def mix_matrix(mix_ref, block, channels):
    half = channels // 2
    rows = lax.broadcasted_iota(jnp.int32, (channels, channels), 0)
    cols = lax.broadcasted_iota(jnp.int32, (channels, channels), 1)
    row_top, col_top = rows < half, cols < half
    row_in = jnp.where(row_top, rows, rows - half)
    col_in = jnp.where(col_top, cols, cols - half)
    row_member = jnp.where(row_top, 0, 2) + (row_in & 1)
    col_member = jnp.where(col_top, 0, 2) + (col_in & 1)
    same = (row_in >> 1) == (col_in >> 1)
    pair = row_member * 4 + col_member
    result = jnp.zeros((channels, channels), f32)
    for i in range(4):
        for j in range(4):
            result = jnp.where(pair == 4 * i + j, mix_ref[block, i, j], result)
    return jnp.where(same, result, 0.0)


def inverse_logdet(mix_ref, block):
    shape = (8, 128)
    left = [[jnp.full(shape, mix_ref[block, i, j], f32) for j in range(4)] for i in range(4)]
    right = [[jnp.full(shape, float(i == j), f32) for j in range(4)] for i in range(4)]
    log_total = jnp.zeros(shape, f32)
    for k in range(4):
        pivot = left[k][k]
        log_total = log_total + jnp.log(pivot)
        left[k] = [v / pivot for v in left[k]]
        right[k] = [v / pivot for v in right[k]]
        for i in range(4):
            if i != k:
                factor = left[i][k]
                left[i] = [v - factor * w for v, w in zip(left[i], left[k])]
                right[i] = [v - factor * w for v, w in zip(right[i], right[k])]
    return right, log_total


def fill_columns(rows_ref, cols_ref, block, vectors):
    rows_ref[...] = jnp.zeros_like(rows_ref)
    for j, vector in enumerate(vectors):
        rows_ref[j : j + 1, : vector.shape[1]] = vector
    cols_ref[...] = rows_ref[...].T


def frame_mask(length, frames):
    return (lax.broadcasted_iota(jnp.int32, (1, frames), 1) < length).astype(f32)


def fill_shifted(hidden, high_ref, low_ref, kernel, sign):
    channels, frames = hidden.shape
    for k in range(kernel):
        move = (sign * (k - kernel // 2)) % frames
        moved = pltpu.roll(hidden, move, 1) if move else hidden
        high, low = split(moved)
        high_ref[k * channels : (k + 1) * channels, :] = high
        low_ref[k * channels : (k + 1) * channels, :] = low


def forward_kernel(
    sizes,
    length_ref,
    mix_ref,
    x_ref,
    norm_bias_ref,
    norm_logs_ref,
    start_w_ref,
    start_b_ref,
    conv_w_ref,
    conv_b_ref,
    res_w_ref,
    res_b_ref,
    last_w_ref,
    last_b_ref,
    end_w_ref,
    end_b_ref,
    flowed_ref,
    logdet_ref,
    hid_out,
    tanh_out,
    sig_out,
    mixed_out,
    wn_out,
    scale_out,
    x_out,
    x_buf,
    hid_buf,
    tanh_buf,
    sig_buf,
    mixed_buf,
    wn_buf,
    scale_buf,
    conv_stage,
    res_stage,
    stack_high,
    stack_low,
    skip_buf,
    det_buf,
    rows_buf,
    cols_buf,
    in_sem,
    out_sem,
    misc_sem,
):
    blocks, layers, kernel, hidden_size, channels, frames = sizes
    half = channels // 2
    steps = blocks * layers
    length = length_ref[0]
    mask = frame_mask(length, frames)

    def conv_copy(block, layer):
        slot = layer % 2
        return pltpu.make_async_copy(conv_w_ref.at[block, layer], conv_stage.at[slot], in_sem.at[0, slot])

    def res_copy(block, layer):
        slot = layer % 2
        return pltpu.make_async_copy(res_w_ref.at[block, layer], res_stage.at[slot], in_sem.at[1, slot])

    def prefetch(block, layer):
        if layer < layers:
            conv_copy(block, layer).start()
            if layer < layers - 1:
                res_copy(block, layer).start()
        else:

            @pl.when(block + 1 < blocks)
            def _():
                prefetch(block + 1, 0)

    def saves(step):
        return [
            pltpu.make_async_copy(buf.at[step], out.at[step], out_sem.at[i, step])
            for i, (buf, out) in enumerate(
                ((hid_buf, hid_out), (tanh_buf, tanh_out), (sig_buf, sig_out))
            )
        ]

    def block_saves(block):
        return [
            pltpu.make_async_copy(buf.at[block], out.at[block], misc_sem.at[i, block])
            for i, (buf, out) in enumerate(
                ((mixed_buf, mixed_out), (wn_buf, wn_out), (scale_buf, scale_out), (x_buf, x_out))
            )
        ]

    prefetch(0, 0)
    x_buf[0] = x_ref[0]
    det_buf[...] = jnp.zeros_like(det_buf)

    def run_block(block, carry):
        fill_columns(
            rows_buf,
            cols_buf,
            block,
            [conv_b_ref[block, pl.ds(l, 1), :] for l in range(layers)]
            + [res_b_ref[l, pl.ds(block, 1), :] for l in range(layers - 1)]
            + [
                r[pl.ds(block, 1), :]
                for r in (start_b_ref, last_b_ref, end_b_ref, norm_bias_ref, norm_logs_ref)
            ],
        )
        base = 2 * layers - 1
        start_b = cols_buf[:hidden_size, base : base + 1]
        last_b = cols_buf[:hidden_size, base + 1 : base + 2]
        end_b = cols_buf[:channels, base + 2 : base + 3]
        norm_b = cols_buf[:channels, base + 3 : base + 4]
        norm_l = cols_buf[:channels, base + 4 : base + 5]
        normed = (norm_b + jnp.exp(norm_l) * x_buf[block]) * mask
        mixed = dot3(split(mix_matrix(mix_ref, block, channels)), split(normed))
        mixed_buf[block] = mixed
        hidden = (dot3(split(start_w_ref[block]), split(mixed[:half]), TN) + start_b) * mask
        hid_buf[block * layers] = hidden

        for layer in range(layers):
            step = block * layers + layer
            last = layer == layers - 1
            saves(step)[0].start()
            conv_copy(block, layer).wait()
            if not last:
                res_copy(block, layer).wait()
            conv_wt = split(conv_stage[layer % 2])
            fill_shifted(hid_buf[step], stack_high, stack_low, kernel, -1)
            res_wt = None if last else split(res_stage[layer % 2])
            prefetch(block, layer + 1)
            out = dot3(conv_wt, (stack_high[...], stack_low[...]), TN) + cols_buf[:, layer : layer + 1]
            tanh_part = jnp.tanh(out[:hidden_size])
            sig_part = 0.5 * jnp.tanh(0.5 * out[hidden_size:]) + 0.5
            tanh_buf[step] = tanh_part
            sig_buf[step] = sig_part
            gated = split(tanh_part * sig_part)
            if last:
                skip_buf[...] += dot3(split(last_w_ref[block]), gated)
            else:
                res = dot3(res_wt, gated, TN) + cols_buf[:, layers + layer : layers + layer + 1]
                if layer:
                    skip_buf[...] += res[hidden_size:]
                else:
                    skip_buf[...] = res[hidden_size:] + last_b
                hid_buf[step + 1] = (hid_buf[step] + res[:hidden_size]) * mask
            for save in saves(step)[1:]:
                save.start()
        wavenet = skip_buf[...] * mask
        wn_buf[block] = wavenet
        out = dot3(split(end_w_ref[block]), split(wavenet)) + end_b
        scale = jnp.exp(out[half:])
        scale_buf[block] = scale
        mixed = mixed_buf[block]
        moved = (out[:half] + scale * mixed[half:]) * mask
        _, log_det = inverse_logdet(mix_ref, block)
        det_buf[0:1, :] += jnp.sum(norm_l) + log_det[0:1, :] * (channels // 4)
        det_buf[1:2, :] += jnp.full((1, 128), jnp.sum(out[half:] * mask))
        x_buf[block + 1, :half] = mixed[:half]
        x_buf[block + 1, half:] = moved
        for save in block_saves(block):
            save.start()
        return carry

    lax.fori_loop(0, blocks, run_block, 0)
    flowed_ref[0] = x_buf[blocks]
    logdet_ref[...] = det_buf[0:1, :] + det_buf[1:2, :] / length.astype(f32)

    def finish(step, carry):
        for save in saves(step):
            save.wait()
        return carry

    lax.fori_loop(0, steps, finish, 0)

    def finish_block(block, carry):
        for save in block_saves(block):
            save.wait()
        return carry

    lax.fori_loop(0, blocks, finish_block, 0)


def forward_call(mel, lengths, params):
    (norm_bias, norm_logs, mix, start_w, start_b, conv_w, conv_b, res_w, res_b, last_w, last_b, end_w, end_b) = params
    _, channels, frames = mel.shape
    conv_w, res_w = conv_w.swapaxes(2, 3), res_w.swapaxes(2, 3)
    start_w, res_b = start_w.swapaxes(1, 2), res_b.swapaxes(0, 1)
    blocks, layers, deep, wide = conv_w.shape
    hidden_size = wide // 2
    kernel = deep // hidden_size
    half = channels // 2
    steps = blocks * layers
    sizes = (blocks, layers, kernel, hidden_size, channels, frames)
    vmem = pl.BlockSpec(memory_space=pltpu.VMEM)
    smem = pl.BlockSpec(memory_space=pltpu.SMEM)
    hbm = pl.BlockSpec(memory_space=pl.ANY)
    shape = jax.ShapeDtypeStruct
    act = (steps, hidden_size, frames)
    return pl.pallas_call(
        functools.partial(forward_kernel, sizes),
        name="flow_forward",
        out_shape=[
            shape((1, channels, frames), f32),
            shape((1, 128), f32),
            shape(act, f32),
            shape(act, f32),
            shape(act, f32),
            shape((blocks, channels, frames), f32),
            shape((blocks, hidden_size, frames), f32),
            shape((blocks, half, frames), f32),
            shape((blocks, channels, frames), f32),
        ],
        in_specs=[smem, smem, vmem, vmem, vmem, vmem, vmem, hbm, vmem, hbm, vmem, vmem, vmem, vmem, vmem],
        out_specs=[vmem, vmem] + [hbm] * 7,
        scratch_shapes=[
            pltpu.VMEM((blocks + 1, channels, frames), f32),
            pltpu.VMEM(act, f32),
            pltpu.VMEM(act, f32),
            pltpu.VMEM(act, f32),
            pltpu.VMEM((blocks, channels, frames), f32),
            pltpu.VMEM((blocks, hidden_size, frames), f32),
            pltpu.VMEM((blocks, half, frames), f32),
            pltpu.VMEM((2, deep, wide), f32),
            pltpu.VMEM((2, hidden_size, wide), f32),
            pltpu.VMEM((deep, frames), bf16),
            pltpu.VMEM((deep, frames), bf16),
            pltpu.VMEM((hidden_size, frames), f32),
            pltpu.VMEM((8, 128), f32),
            pltpu.VMEM((16, wide), f32),
            pltpu.VMEM((wide, 16), f32),
            pltpu.SemaphoreType.DMA((2, 2)),
            pltpu.SemaphoreType.DMA((3, steps)),
            pltpu.SemaphoreType.DMA((4, blocks)),
        ],
        compiler_params=pltpu.CompilerParams(vmem_limit_bytes=VMEM_LIMIT),
    )(lengths, mix, mel, norm_bias, norm_logs, start_w, start_b, conv_w, conv_b, res_w, res_b, last_w, last_b, end_w, end_b)
MESH = pl.DeviceIdType.MESH
MISC = 128
TICKS = 3


class Exchange:
    def __init__(self, bits, halvings):
        self.bits, self.halvings = bits, halvings
        self.hops = bits + halvings
        self.me = lax.axis_index("dp")
        self.value = [lax.rem(self.me // 2**b, 2) for b in range(bits)]

    def order(self, turn):
        pairs = [(self.value[b], 2**b) for b in range(self.bits)]

        def either(flag, yes, no):
            return tuple(flag * y + (1 - flag) * n for y, n in zip(yes, no))

        odd = self.value[0]
        first = either(odd, pairs[2], pairs[1])
        second = either(odd, pairs[1], pairs[2])
        return [
            pairs[0],
            either(turn, pairs[3], first),
            either(turn, first, second),
            either(turn, second, pairs[3]),
        ] + pairs[4:]

    def partner(self, hop):
        bit, stride = hop
        return (self.me + (1 - 2 * bit) * stride,)

    def spans(self, turn, rows):
        at, size, result = 0, rows, []
        for bit, _ in self.order(turn)[: self.halvings]:
            size //= 2
            result.append((at + bit * size, at + (1 - bit) * size, size))
            at = at + bit * size
        return result


class Reduction:
    def __init__(self, exchange, turn, source, target, slots, sems, rows, later=None):
        self.x, self.turn, self.source, self.target = exchange, turn, source, target
        self.slots, self.sems, self.rows, self.later = slots, sems, rows, later
        self.order = exchange.order(turn)
        self.spans = exchange.spans(turn, rows)

    def rows_of(self, at, size):
        return pl.ds(pl.multiple_of(at, 8), size)

    def copy(self, hop):
        halvings, bits = self.x.halvings, self.x.bits
        send, recv, _, _ = self.sems
        if hop < bits:
            if hop < halvings:
                _, at, size = self.spans[hop]
            else:
                at, _, size = self.spans[-1]
            src = self.source.at[self.rows_of(at, size)]
            dst = self.slots[hop]
            to = self.order[hop]
        else:
            level = halvings - 1 - (hop - bits)
            at, _, size = self.spans[level]
            base = self.source if hop == bits else self.target
            src = base.at[self.rows_of(at, size)]
            dst = self.target.at[self.rows_of(at, size)]
            to = self.order[level]
        return pltpu.make_async_remote_copy(
            src_ref=src,
            dst_ref=dst,
            send_sem=send.at[hop],
            recv_sem=recv.at[hop],
            device_id=self.x.partner(to),
            device_id_type=MESH,
        )

    def own(self):
        at, _, size = self.spans[-1]
        where = self.rows_of(at, size)
        return pltpu.make_async_copy(self.source.at[where], self.target.at[where], self.sems[2])

    def step(self, k):
        x = self.x
        if k > 0:
            done = k - 1
            self.copy(done).wait()
            if done < x.bits:
                at, _, size = self.spans[min(done, x.halvings - 1)]
                where = self.rows_of(at, size)
                self.source[where] += self.slots[done][...]
                self.free(done)
        if k == x.bits:
            self.own().start()
        if k == x.bits + 1:
            self.own().wait()
        if k < x.hops:
            if k < x.bits:
                self.wait_free(k)
            self.copy(k).start()

    def free(self, hop):
        if self.later is not None:
            turn, credit, exists = self.later

            @pl.when(exists)
            def _():
                pl.semaphore_signal(
                    credit.at[hop],
                    inc=1,
                    device_id=self.x.partner(self.x.order(turn)[hop]),
                    device_id_type=MESH,
                )

    def wait_free(self, hop):
        credit, needed = self.sems[3] if self.sems[3] is not None else (None, None)
        if credit is not None:

            @pl.when(needed)
            def _():
                pl.semaphore_wait(credit.at[hop], 1)


def backward_kernel(
    sizes,
    bits,
    halvings,
    depth,
    length_ref,
    grad_det_ref,
    mix_ref,
    grad_out_ref,
    norm_bias_ref,
    norm_logs_ref,
    start_w_ref,
    last_w_ref,
    end_w_ref,
    conv_w_ref,
    res_w_ref,
    hid_ref,
    tanh_ref,
    sig_ref,
    mixed_ref,
    wn_ref,
    scale_ref,
    x_ref,
    grad_in_ref,
    units_ref,
    misc_ref,
    *scratch,
):
    (
        unit_buf,
        misc_buf,
        act_buf,
        mixed_buf,
        wn_buf,
        scale_buf,
        x_buf,
        conv_stage,
        res_stage,
        stack_high,
        stack_low,
        back_high,
        back_low,
        turned_high,
        turned_low,
        gated_high,
        gated_low,
        pair_high,
        pair_low,
        grad_skip,
        grad_hid,
        grad_gated,
        grad_flow,
        grad_changed,
        columns_buf,
        act_sem,
        weight_sem,
        block_sem,
        send_sem,
        recv_sem,
        own_sem,
        credit_sem,
    ) = scratch[:32]
    slot_bufs = scratch[32 : 32 + bits]
    misc_slots = scratch[32 + bits :]
    blocks, layers, kernel, hidden_size, channels, frames = sizes
    half = channels // 2
    steps = blocks * layers
    deep = kernel * hidden_size
    wide = 2 * hidden_size
    middle = kernel // 2
    length = length_ref[0]
    mask = frame_mask(length, frames)
    grad_det = grad_det_ref[0]
    exchange = Exchange(bits, halvings)

    def turn_of(unit):
        return lax.rem(unit, 4) // 3

    def reduction(unit):
        slot = lax.rem(unit, depth)
        after = unit + depth
        capped = jnp.minimum(after, steps - 1)
        return Reduction(
            exchange,
            turn_of(unit),
            unit_buf.at[unit],
            units_ref.at[unit],
            [b.at[slot] for b in slot_bufs],
            (
                send_sem.at[unit],
                recv_sem.at[unit],
                own_sem.at[unit],
                (credit_sem.at[unit], unit >= depth),
            ),
            deep + hidden_size,
            (turn_of(after), credit_sem.at[capped], after < steps),
        )

    misc_sum = Reduction(
        exchange,
        0,
        misc_buf,
        misc_ref,
        misc_slots,
        (send_sem.at[steps], recv_sem.at[steps], own_sem.at[steps], None),
        blocks * MISC,
    )
    offsets = [0, 1, 3, 4, 5, 6, 7, 8, 9] + list(range(10, 10 + exchange.hops))
    offsets = offsets[: exchange.hops + 1]

    def tick(step, point):
        for k in range(exchange.hops + 1):
            late = offsets[k] + 1
            if late % TICKS == point:
                unit = step - late // TICKS
                if isinstance(unit, int):
                    if 0 <= unit < steps:
                        reduction(unit).step(k)
                else:

                    @pl.when((unit >= 0) & (unit < steps))
                    def _(unit=unit, k=k):
                        reduction(unit).step(k)

    def act_copies(step):
        slot = lax.rem(step, 2)
        at = steps - 1 - step
        return [
            pltpu.make_async_copy(ref.at[at], act_buf.at[slot, i], act_sem.at[slot, i])
            for i, ref in enumerate((hid_ref, tanh_ref, sig_ref))
        ]

    def weight_copies(step):
        slot = lax.rem(step, 2)
        block, layer = blocks - 1 - step // layers, layers - 1 - lax.rem(step, layers)
        conv = pltpu.make_async_copy(conv_w_ref.at[block, layer], conv_stage.at[slot], weight_sem.at[slot, 0])
        res = pltpu.make_async_copy(
            res_w_ref.at[block, jnp.minimum(layer, layers - 2)], res_stage.at[slot], weight_sem.at[slot, 1]
        )
        return [conv, res]

    def block_copies(block):
        return [
            pltpu.make_async_copy(ref.at[block], buf.at[block], block_sem.at[block, i])
            for i, (ref, buf) in enumerate(
                ((wn_ref, wn_buf), (scale_ref, scale_buf), (mixed_ref, mixed_buf), (x_ref, x_buf))
            )
        ]

    for block in reversed(range(blocks)):
        for copy in block_copies(block):
            copy.start()
    for copy in act_copies(0) + weight_copies(0):
        copy.start()

    barrier = pltpu.get_barrier_semaphore()
    for b in range(bits):
        pl.semaphore_signal(
            barrier, inc=1, device_id=exchange.partner((exchange.value[b], 2**b)), device_id_type=MESH
        )
    pl.semaphore_wait(barrier, bits)

    grad_flow[...] = grad_out_ref[0]
    misc_buf[...] = jnp.zeros_like(misc_buf)
    columns_buf[...] = jnp.zeros_like(columns_buf)
    for high, low, rows in ((stack_high, stack_low, deep), (gated_high, gated_low, hidden_size)):
        high[rows:, :] = jnp.ones((16, frames), bf16)
        low[rows:, :] = jnp.zeros((16, frames), bf16)

    def run_step(step, carry):
        block = blocks - 1 - step // layers
        layer = layers - 1 - lax.rem(step, layers)
        slot = lax.rem(step, 2)
        misc_at = block * MISC
        tick(step, 0)
        for copy in act_copies(step) + weight_copies(step):
            copy.wait()

        @pl.when(step + 1 < steps)
        def _():
            for copy in act_copies(step + 1) + weight_copies(step + 1):
                copy.start()

        tanh_part, sig_part = act_buf[slot, 1], act_buf[slot, 2]
        high, low = split(tanh_part * sig_part)
        gated_high[:hidden_size] = high
        gated_low[:hidden_size] = low

        @pl.when(layer == layers - 1)
        def _():
            for copy in block_copies(block):
                copy.wait()
            moved_grad = grad_flow[half:] * mask
            changed_grad = moved_grad * scale_buf[block]
            grad_changed[...] = changed_grad
            logs_grad = changed_grad * mixed_buf[block, half:] + (grad_det / length.astype(f32)) * mask
            out_grad = jnp.concatenate([moved_grad, logs_grad], axis=0)
            columns_buf[:channels, 0:1] = jnp.sum(out_grad, axis=1, keepdims=True)
            out_split = split(out_grad)
            end_grad = dot3(out_split, split(wn_buf[block]), NT)
            skip = dot3(split(end_w_ref[block]), out_split, TN) * mask
            columns_buf[:, 1:2] = jnp.sum(skip, axis=1, keepdims=True)
            skip_split = split(skip)
            pair_high[hidden_size:], pair_low[hidden_size:] = skip_split
            gated = (gated_high[:hidden_size], gated_low[:hidden_size])
            unit_buf[step, deep:, :hidden_size] = dot3(skip_split, gated, NT)
            unit_buf[step, deep : deep + channels, hidden_size:] = end_grad
            grad_gated[...] = dot3(split(last_w_ref[block]), skip_split, TN)
            grad_hid[...] = jnp.zeros_like(grad_hid)

        @pl.when(layer < layers - 1)
        def _():
            masked = grad_hid[...] * mask
            grad_hid[...] = masked
            pair_high[:hidden_size], pair_low[:hidden_size] = split(masked)
            pair = (pair_high[...], pair_low[...])
            grads = dot3((gated_high[...], gated_low[...]), pair, NT)
            unit_buf[step, deep:] = grads[:hidden_size]
            misc_buf[pl.ds(misc_at + half + 8 + layers + layer, 1), :] = grads[hidden_size : hidden_size + 1]
            grad_gated[...] = dot3(split(res_stage[slot]), pair)

        gated_grad = grad_gated[...]
        tanh_part, sig_part = act_buf[slot, 1], act_buf[slot, 2]
        inner = gated_grad * sig_part
        conv_grad = jnp.concatenate(
            [inner * (1.0 - tanh_part * tanh_part), inner * tanh_part * (1.0 - sig_part)], axis=0
        )
        fill_shifted(conv_grad, back_high, back_low, kernel, 1)
        fill_shifted(act_buf[slot, 0], stack_high, stack_low, kernel, -1)
        center = slice(middle * wide, (middle + 1) * wide)
        grads = dot3((stack_high[...], stack_low[...]), (back_high[center], back_low[center]), NT)
        unit_buf[step, :deep] = grads[:deep]
        misc_buf[pl.ds(misc_at + half + 8 + layer, 1), :] = grads[deep : deep + 1]
        tick(step, 1)
        for k in range(kernel):
            high, low = split(conv_stage[slot, k * hidden_size : (k + 1) * hidden_size])
            turned_high[:, k * wide : (k + 1) * wide] = high
            turned_low[:, k * wide : (k + 1) * wide] = low
        grad_hid[...] += dot3((turned_high[...], turned_low[...]), (back_high[...], back_low[...]))

        @pl.when(layer == 0)
        def _():
            hid_grad = grad_hid[...] * mask
            hid_split = split(hid_grad)
            mixed = mixed_buf[block]
            start_grad = dot3(split(mixed[:half]), hid_split, NT)
            misc_buf[pl.ds(misc_at, half), :hidden_size] = start_grad
            columns_buf[:, 2:3] = jnp.sum(hid_grad, axis=1, keepdims=True)
            passed_grad = grad_flow[:half] + dot3(split(start_w_ref[block]), hid_split)
            mixed_grad = split(jnp.concatenate([passed_grad, grad_changed[...]], axis=0))
            norm_b = jnp.transpose(jnp.broadcast_to(norm_bias_ref[pl.ds(block, 1), :], (8, channels)))[:, 0:1]
            norm_s = jnp.exp(jnp.transpose(jnp.broadcast_to(norm_logs_ref[pl.ds(block, 1), :], (8, channels)))[:, 0:1])
            scaled = norm_s * x_buf[block]
            normed = (norm_b + scaled) * mask
            mix_grad = dot3(mixed_grad, split(normed), NT)
            normed_grad = dot3(split(mix_matrix(mix_ref, block, channels)), mixed_grad, TN) * mask
            columns_buf[:channels, 3:4] = jnp.sum(normed_grad, axis=1, keepdims=True)
            columns_buf[:channels, 4:5] = jnp.sum(normed_grad * scaled, axis=1, keepdims=True) + grad_det
            grad_flow[...] = normed_grad * norm_s
            rows = columns_buf[...].T
            misc_buf[pl.ds(misc_at + half, 8), :hidden_size] = rows[:8]
            inverse, _ = inverse_logdet(mix_ref, block)
            misc_buf[pl.ds(misc_at + half + 7 + 2 * layers, 1), :] = mix_row(
                mix_grad, inverse, grad_det * (channels // 4), wide
            )

        tick(step, 2)
        return carry

    lax.fori_loop(0, steps, run_step, 0)
    grad_in_ref[0] = grad_flow[...]
    left = list(range(exchange.hops + 1))
    for step in range(steps, steps + (offsets[-1] + 1) // TICKS + 1):
        for point in range(TICKS):
            if left:
                misc_sum.step(left.pop(0))
            tick(step, point)
    for k in left:
        misc_sum.step(k)


def mix_row(products, inverse, factor, wide):
    channels = products.shape[0]
    half = channels // 2
    rows = lax.broadcasted_iota(jnp.int32, (channels, channels), 0)
    cols = lax.broadcasted_iota(jnp.int32, (channels, channels), 1)
    row_top, col_top = rows < half, cols < half
    row_in = jnp.where(row_top, rows, rows - half)
    col_in = jnp.where(col_top, cols, cols - half)
    row_member = jnp.where(row_top, 0, 2) + (row_in & 1)
    col_member = jnp.where(col_top, 0, 2) + (col_in & 1)
    same = (row_in >> 1) == (col_in >> 1)
    kept = jnp.where(same, products, 0.0)
    lane = lax.broadcasted_iota(jnp.int32, (1, wide), 1)
    result = jnp.zeros((1, wide), f32)
    for i in range(4):
        mine = jnp.where(row_member == i, kept, 0.0)
        for j in range(4):
            picked = jnp.where(col_member == j, mine, 0.0)
            total = jnp.sum(jnp.sum(picked, axis=0, keepdims=True), axis=1, keepdims=True)
            total = total + factor * inverse[j][i][0:1, 0:1]
            result = jnp.where(lane == 4 * i + j, total, result)
    return result


def backward_call(count, lengths, grad_det, grad_out, params, saved):
    (norm_bias, norm_logs, mix, start_w, _, conv_w, _, res_w, _, last_w, _, end_w, _) = params
    hid, tanh_all, sig_all, mixed, wn, scale, x_all = saved
    _, channels, frames = grad_out.shape
    conv_w, res_w, start_w = conv_w.swapaxes(2, 3), res_w.swapaxes(2, 3), start_w.swapaxes(1, 2)
    blocks, layers, deep, wide = conv_w.shape
    hidden_size = wide // 2
    kernel = deep // hidden_size
    half = channels // 2
    steps = blocks * layers
    sizes = (blocks, layers, kernel, hidden_size, channels, frames)
    bits = count.bit_length() - 1
    halvings = 4
    depth = 3
    rows = deep + hidden_size
    vmem = pl.BlockSpec(memory_space=pltpu.VMEM)
    smem = pl.BlockSpec(memory_space=pltpu.SMEM)
    hbm = pl.BlockSpec(memory_space=pl.ANY)
    shape = jax.ShapeDtypeStruct
    shares = [2 ** -min(hop + 1, halvings) for hop in range(bits)]
    hops = bits + halvings
    return pl.pallas_call(
        functools.partial(backward_kernel, sizes, bits, halvings, depth),
        name="flow_backward",
        out_shape=[
            shape((1, channels, frames), f32),
            shape((steps, rows, wide), f32),
            shape((blocks * MISC, wide), f32),
        ],
        in_specs=[smem, smem, smem] + [vmem] * 6 + [hbm] * 9,
        out_specs=[vmem, hbm, hbm],
        scratch_shapes=[
            pltpu.VMEM((steps, rows, wide), f32),
            pltpu.VMEM((blocks * MISC, wide), f32),
            pltpu.VMEM((2, 3, hidden_size, frames), f32),
            pltpu.VMEM((blocks, channels, frames), f32),
            pltpu.VMEM((blocks, hidden_size, frames), f32),
            pltpu.VMEM((blocks, half, frames), f32),
            pltpu.VMEM((blocks, channels, frames), f32),
            pltpu.VMEM((2, deep, wide), f32),
            pltpu.VMEM((2, hidden_size, wide), f32),
            pltpu.VMEM((deep + 16, frames), bf16),
            pltpu.VMEM((deep + 16, frames), bf16),
            pltpu.VMEM((kernel * wide, frames), bf16),
            pltpu.VMEM((kernel * wide, frames), bf16),
            pltpu.VMEM((hidden_size, kernel * wide), bf16),
            pltpu.VMEM((hidden_size, kernel * wide), bf16),
            pltpu.VMEM((hidden_size + 16, frames), bf16),
            pltpu.VMEM((hidden_size + 16, frames), bf16),
            pltpu.VMEM((wide, frames), bf16),
            pltpu.VMEM((wide, frames), bf16),
            pltpu.VMEM((hidden_size, frames), f32),
            pltpu.VMEM((hidden_size, frames), f32),
            pltpu.VMEM((hidden_size, frames), f32),
            pltpu.VMEM((channels, frames), f32),
            pltpu.VMEM((half, frames), f32),
            pltpu.VMEM((hidden_size, 128), f32),
            pltpu.SemaphoreType.DMA((2, 3)),
            pltpu.SemaphoreType.DMA((2, 2)),
            pltpu.SemaphoreType.DMA((blocks, 4)),
            pltpu.SemaphoreType.DMA((steps + 1, hops)),
            pltpu.SemaphoreType.DMA((steps + 1, hops)),
            pltpu.SemaphoreType.DMA((steps + 1,)),
            pltpu.SemaphoreType.REGULAR((steps, bits)),
        ]
        + [pltpu.VMEM((depth, int(rows * s), wide), f32) for s in shares]
        + [pltpu.VMEM((int(blocks * MISC * s), wide), f32) for s in shares],
        compiler_params=pltpu.CompilerParams(
            collective_id=0, has_side_effects=True, vmem_limit_bytes=VMEM_LIMIT
        ),
    )(lengths, grad_det, mix, grad_out, norm_bias, norm_logs, start_w, last_w, end_w, conv_w, res_w,
      hid, tanh_all, sig_all, mixed, wn, scale, x_all)


def shards(mesh_size, mel, lengths, *rest):
    params, grad_out, grad_det = rest[:13], rest[13], rest[14]
    flowed, logdet, *saved = forward_call(mel, lengths, params)
    grad_in, units, misc = backward_call(mesh_size, lengths, grad_det, grad_out, params, saved)
    blocks, layers, wide, deep = params[5].shape
    hidden_size = wide // 2
    channels = mel.shape[1]
    half = channels // 2
    units = units[::-1].reshape(blocks, layers, deep + hidden_size, wide)
    misc = misc.reshape(blocks, MISC, wide)
    ends = units[:, layers - 1, deep:]
    return (
        flowed,
        logdet[0, :1],
        grad_in,
        misc[:, half + 3, :channels],
        misc[:, half + 4, :channels],
        misc[:, half + 7 + 2 * layers, :16].reshape(blocks, 4, 4),
        misc[:, :half, :hidden_size].swapaxes(1, 2),
        misc[:, half + 2, :hidden_size],
        units[:, :, :deep].swapaxes(2, 3),
        misc[:, half + 8 : half + 8 + layers],
        units[:, : layers - 1, deep:].swapaxes(2, 3),
        misc[:, half + 8 + layers : half + 7 + 2 * layers],
        ends[:, :, :hidden_size],
        misc[:, half + 1, :hidden_size],
        ends[:, :channels, hidden_size:],
        misc[:, half, :channels],
    )


def solution(mesh):
    split_first, whole = P("dp", None, None), P()
    in_specs = (split_first, P("dp")) + (whole,) * 13 + (split_first, P("dp"))
    out_specs = (split_first, P("dp"), split_first) + (whole,) * 13
    return jax.shard_map(
        functools.partial(shards, mesh.shape["dp"]),
        mesh=mesh,
        in_specs=in_specs,
        out_specs=out_specs,
        check_vma=False,
    )
```

```python
import functools

import jax
import jax.numpy as jnp
from jax import lax
from jax.experimental import pallas as pl
from jax.experimental.pallas import tpu as pltpu
from jax.sharding import PartitionSpec as P

f32, bf16 = jnp.float32, jnp.bfloat16
NN = (((1,), (0,)), ((), ()))
NT = (((1,), (1,)), ((), ()))
TN = (((0,), (0,)), ((), ()))
VMEM_LIMIT = 60 * 2**20


def dot(left, right, form=NN):
    return lax.dot_general(left, right, form, preferred_element_type=f32)


def split(value):
    high = value.astype(bf16)
    return high, (value - high.astype(f32)).astype(bf16)


def dot3(left, right, form=NN):
    (left_high, left_low), (right_high, right_low) = left, right
    return (
        dot(left_high, right_high, form)
        + dot(left_high, right_low, form)
        + dot(left_low, right_high, form)
    )


def mix_matrix(mix_ref, block, channels):
    half = channels // 2
    rows = lax.broadcasted_iota(jnp.int32, (channels, channels), 0)
    cols = lax.broadcasted_iota(jnp.int32, (channels, channels), 1)
    row_top, col_top = rows < half, cols < half
    row_in = jnp.where(row_top, rows, rows - half)
    col_in = jnp.where(col_top, cols, cols - half)
    row_member = jnp.where(row_top, 0, 2) + (row_in & 1)
    col_member = jnp.where(col_top, 0, 2) + (col_in & 1)
    same = (row_in >> 1) == (col_in >> 1)
    pair = row_member * 4 + col_member
    result = jnp.zeros((channels, channels), f32)
    for i in range(4):
        for j in range(4):
            result = jnp.where(pair == 4 * i + j, mix_ref[block, i, j], result)
    return jnp.where(same, result, 0.0)


def inverse_logdet(mix_ref, block):
    shape = (8, 128)
    left = [[jnp.full(shape, mix_ref[block, i, j], f32) for j in range(4)] for i in range(4)]
    right = [[jnp.full(shape, float(i == j), f32) for j in range(4)] for i in range(4)]
    log_total = jnp.zeros(shape, f32)
    for k in range(4):
        pivot = left[k][k]
        log_total = log_total + jnp.log(pivot)
        left[k] = [v / pivot for v in left[k]]
        right[k] = [v / pivot for v in right[k]]
        for i in range(4):
            if i != k:
                factor = left[i][k]
                left[i] = [v - factor * w for v, w in zip(left[i], left[k])]
                right[i] = [v - factor * w for v, w in zip(right[i], right[k])]
    return right, log_total


def fill_columns(rows_ref, cols_ref, block, vectors):
    rows_ref[...] = jnp.zeros_like(rows_ref)
    for j, vector in enumerate(vectors):
        rows_ref[j : j + 1, : vector.shape[1]] = vector
    cols_ref[...] = rows_ref[...].T


def frame_mask(length, frames):
    return (lax.broadcasted_iota(jnp.int32, (1, frames), 1) < length).astype(f32)


def fill_shifted(hidden, high_ref, low_ref, kernel, sign):
    channels, frames = hidden.shape
    for k in range(kernel):
        move = (sign * (k - kernel // 2)) % frames
        moved = pltpu.roll(hidden, move, 1) if move else hidden
        high, low = split(moved)
        high_ref[k * channels : (k + 1) * channels, :] = high
        low_ref[k * channels : (k + 1) * channels, :] = low


def forward_kernel(
    sizes,
    length_ref,
    mix_ref,
    x_ref,
    norm_bias_ref,
    norm_logs_ref,
    start_w_ref,
    start_b_ref,
    conv_w_ref,
    conv_b_ref,
    res_w_ref,
    res_b_ref,
    last_w_ref,
    last_b_ref,
    end_w_ref,
    end_b_ref,
    flowed_ref,
    logdet_ref,
    hid_out,
    tanh_out,
    sig_out,
    mixed_out,
    wn_out,
    scale_out,
    x_out,
    x_buf,
    hid_buf,
    tanh_buf,
    sig_buf,
    mixed_buf,
    wn_buf,
    scale_buf,
    conv_stage,
    res_stage,
    stack_high,
    stack_low,
    skip_buf,
    det_buf,
    rows_buf,
    cols_buf,
    in_sem,
    out_sem,
    misc_sem,
):
    blocks, layers, kernel, hidden_size, channels, frames = sizes
    half = channels // 2
    steps = blocks * layers
    length = length_ref[0]
    mask = frame_mask(length, frames)

    def conv_copy(block, layer):
        slot = layer % 2
        return pltpu.make_async_copy(conv_w_ref.at[block, layer], conv_stage.at[slot], in_sem.at[0, slot])

    def res_copy(block, layer):
        slot = layer % 2
        return pltpu.make_async_copy(res_w_ref.at[block, layer], res_stage.at[slot], in_sem.at[1, slot])

    def prefetch(block, layer):
        if layer < layers:
            conv_copy(block, layer).start()
            if layer < layers - 1:
                res_copy(block, layer).start()
        else:

            @pl.when(block + 1 < blocks)
            def _():
                prefetch(block + 1, 0)

    def saves(step):
        return [
            pltpu.make_async_copy(buf.at[step], out.at[step], out_sem.at[i, step])
            for i, (buf, out) in enumerate(
                ((hid_buf, hid_out), (tanh_buf, tanh_out), (sig_buf, sig_out))
            )
        ]

    def block_saves(block):
        return [
            pltpu.make_async_copy(buf.at[block], out.at[block], misc_sem.at[i, block])
            for i, (buf, out) in enumerate(
                ((mixed_buf, mixed_out), (wn_buf, wn_out), (scale_buf, scale_out), (x_buf, x_out))
            )
        ]

    prefetch(0, 0)
    x_buf[0] = x_ref[0]
    det_buf[...] = jnp.zeros_like(det_buf)

    def run_block(block, carry):
        fill_columns(
            rows_buf,
            cols_buf,
            block,
            [conv_b_ref[block, pl.ds(l, 1), :] for l in range(layers)]
            + [res_b_ref[l, pl.ds(block, 1), :] for l in range(layers - 1)]
            + [
                r[pl.ds(block, 1), :]
                for r in (start_b_ref, last_b_ref, end_b_ref, norm_bias_ref, norm_logs_ref)
            ],
        )
        base = 2 * layers - 1
        start_b = cols_buf[:hidden_size, base : base + 1]
        last_b = cols_buf[:hidden_size, base + 1 : base + 2]
        end_b = cols_buf[:channels, base + 2 : base + 3]
        norm_b = cols_buf[:channels, base + 3 : base + 4]
        norm_l = cols_buf[:channels, base + 4 : base + 5]
        normed = (norm_b + jnp.exp(norm_l) * x_buf[block]) * mask
        mixed = dot3(split(mix_matrix(mix_ref, block, channels)), split(normed))
        mixed_buf[block] = mixed
        hidden = (dot3(split(start_w_ref[block]), split(mixed[:half]), TN) + start_b) * mask
        hid_buf[block * layers] = hidden

        for layer in range(layers):
            step = block * layers + layer
            last = layer == layers - 1
            saves(step)[0].start()
            conv_copy(block, layer).wait()
            if not last:
                res_copy(block, layer).wait()
            conv_wt = split(conv_stage[layer % 2])
            fill_shifted(hid_buf[step], stack_high, stack_low, kernel, -1)
            res_wt = None if last else split(res_stage[layer % 2])
            prefetch(block, layer + 1)
            out = dot3(conv_wt, (stack_high[...], stack_low[...]), TN) + cols_buf[:, layer : layer + 1]
            tanh_part = jnp.tanh(out[:hidden_size])
            sig_part = 0.5 * jnp.tanh(0.5 * out[hidden_size:]) + 0.5
            tanh_buf[step] = tanh_part
            sig_buf[step] = sig_part
            gated = split(tanh_part * sig_part)
            if last:
                skip_buf[...] += dot3(split(last_w_ref[block]), gated)
            else:
                res = dot3(res_wt, gated, TN) + cols_buf[:, layers + layer : layers + layer + 1]
                if layer:
                    skip_buf[...] += res[hidden_size:]
                else:
                    skip_buf[...] = res[hidden_size:] + last_b
                hid_buf[step + 1] = (hid_buf[step] + res[:hidden_size]) * mask
            for save in saves(step)[1:]:
                save.start()
        wavenet = skip_buf[...] * mask
        wn_buf[block] = wavenet
        out = dot3(split(end_w_ref[block]), split(wavenet)) + end_b
        scale = jnp.exp(out[half:])
        scale_buf[block] = scale
        mixed = mixed_buf[block]
        moved = (out[:half] + scale * mixed[half:]) * mask
        _, log_det = inverse_logdet(mix_ref, block)
        det_buf[0:1, :] += jnp.sum(norm_l) + log_det[0:1, :] * (channels // 4)
        det_buf[1:2, :] += jnp.full((1, 128), jnp.sum(out[half:] * mask))
        x_buf[block + 1, :half] = mixed[:half]
        x_buf[block + 1, half:] = moved
        for save in block_saves(block):
            save.start()
        return carry

    lax.fori_loop(0, blocks, run_block, 0)
    flowed_ref[0] = x_buf[blocks]
    logdet_ref[...] = det_buf[0:1, :] + det_buf[1:2, :] / length.astype(f32)

    def finish(step, carry):
        for save in saves(step):
            save.wait()
        return carry

    lax.fori_loop(0, steps, finish, 0)

    def finish_block(block, carry):
        for save in block_saves(block):
            save.wait()
        return carry

    lax.fori_loop(0, blocks, finish_block, 0)


def forward_call(mel, lengths, params):
    (norm_bias, norm_logs, mix, start_w, start_b, conv_w, conv_b, res_w, res_b, last_w, last_b, end_w, end_b) = params
    _, channels, frames = mel.shape
    conv_w, res_w = conv_w.swapaxes(2, 3), res_w.swapaxes(2, 3)
    start_w, res_b = start_w.swapaxes(1, 2), res_b.swapaxes(0, 1)
    blocks, layers, deep, wide = conv_w.shape
    hidden_size = wide // 2
    kernel = deep // hidden_size
    half = channels // 2
    steps = blocks * layers
    sizes = (blocks, layers, kernel, hidden_size, channels, frames)
    vmem = pl.BlockSpec(memory_space=pltpu.VMEM)
    smem = pl.BlockSpec(memory_space=pltpu.SMEM)
    hbm = pl.BlockSpec(memory_space=pl.ANY)
    shape = jax.ShapeDtypeStruct
    act = (steps, hidden_size, frames)
    return pl.pallas_call(
        functools.partial(forward_kernel, sizes),
        name="flow_forward",
        out_shape=[
            shape((1, channels, frames), f32),
            shape((1, 128), f32),
            shape(act, f32),
            shape(act, f32),
            shape(act, f32),
            shape((blocks, channels, frames), f32),
            shape((blocks, hidden_size, frames), f32),
            shape((blocks, half, frames), f32),
            shape((blocks, channels, frames), f32),
        ],
        in_specs=[smem, smem, vmem, vmem, vmem, vmem, vmem, hbm, vmem, hbm, vmem, vmem, vmem, vmem, vmem],
        out_specs=[vmem, vmem] + [hbm] * 7,
        scratch_shapes=[
            pltpu.VMEM((blocks + 1, channels, frames), f32),
            pltpu.VMEM(act, f32),
            pltpu.VMEM(act, f32),
            pltpu.VMEM(act, f32),
            pltpu.VMEM((blocks, channels, frames), f32),
            pltpu.VMEM((blocks, hidden_size, frames), f32),
            pltpu.VMEM((blocks, half, frames), f32),
            pltpu.VMEM((2, deep, wide), f32),
            pltpu.VMEM((2, hidden_size, wide), f32),
            pltpu.VMEM((deep, frames), bf16),
            pltpu.VMEM((deep, frames), bf16),
            pltpu.VMEM((hidden_size, frames), f32),
            pltpu.VMEM((8, 128), f32),
            pltpu.VMEM((16, wide), f32),
            pltpu.VMEM((wide, 16), f32),
            pltpu.SemaphoreType.DMA((2, 2)),
            pltpu.SemaphoreType.DMA((3, steps)),
            pltpu.SemaphoreType.DMA((4, blocks)),
        ],
        compiler_params=pltpu.CompilerParams(vmem_limit_bytes=VMEM_LIMIT),
    )(lengths, mix, mel, norm_bias, norm_logs, start_w, start_b, conv_w, conv_b, res_w, res_b, last_w, last_b, end_w, end_b)
MESH = pl.DeviceIdType.MESH
MISC = 128
PARTS = 3
POINTS = 6
READY = (2, 3, 4)
STARTS = ((2, 4, 6, 9, 11, 14, 17, 19, 32, 44), (3, 5, 8, 12, 16, 20, 25, 28, 32, 43), (4, 5, 9, 11, 13, 16, 18, 22, 40, 43))


POINT_US = (2.4, 1.1, 1.2, 1.2, 1.2, 3.0)
LINK_ROWS, CORE_ROWS = 55.0, 290.0


def drain_order(starts, bits, halvings, steps, part_rows, misc_rows):
    hops = bits + halvings
    free, arrival, taken = {}, {}, {}
    clock = 0.0

    def routes(part):
        late = part == PARTS - 1
        near, far = ("z", "a", "b") if late else ("a", "b", "z"), ["far"] * (bits - 4)
        names = ["core", *near, *far, *reversed(near), "core"]
        sizes = [2 ** -(h + 1) for h in range(halvings)]
        sizes += [sizes[-1]] * (bits - halvings) + sizes[::-1]
        return list(zip(names, sizes))

    def take(unit, part, k):
        nonlocal clock
        if k:
            clock = max(clock, arrival[unit, part]) + 0.2
        taken[unit, part] = k + 1
        if k == hops:
            return
        name, size = routes(part)[k]
        rows = size * (misc_rows if unit == steps else part_rows)
        ends = []
        for odd in range(2):
            if name == "core":
                pairs = [(("core", odd), 1.0, CORE_ROWS)]
            elif name == "far":
                pairs = [("z", 1.0, LINK_ROWS), ("middle", 2.0, LINK_ROWS)]
            else:
                pairs = [(name if name == "z" else "xy"[(name == "b") ^ odd], 1.0, LINK_ROWS)]
            for link, times, rate in pairs:
                free[link] = max(clock, free.get(link, 0.0)) + times * rows / rate
                ends.append(free[link])
        arrival[unit, part] = max(ends) + {"core": 1.4, "far": 3.4}.get(name, 2.9)

    for layer in range(steps):
        for point in range(POINTS):
            clock += POINT_US[point]
            for lag, part, k in due_steps(starts, point):
                if layer >= lag:
                    take(layer - lag, part, k)
    order = []
    waiting = [(unit, part) for unit in range(steps) for part in range(PARTS)] + [(steps, 0)]
    waiting = [w for w in waiting if taken.get(w, 0) <= hops]
    while waiting:
        ready = [w for w in waiting if taken.get(w, 0) == 0 or arrival[w] <= clock]
        if ready:
            best = min(ready, key=lambda w: (taken.get(w, 0) >= bits, w))
        else:
            best = min(waiting, key=lambda w: arrival[w])
        order.append((*best, taken.get(best, 0)))
        take(*order[-1])
        if taken[best] > hops:
            waiting.remove(best)
    return order


def due_steps(starts, point):
    due = [
        (start // POINTS, part, k)
        for part, row in enumerate(starts)
        for k, start in enumerate(row)
        if start % POINTS == point
    ]
    return sorted(due, key=lambda due: (-due[0], due[1], due[2]))


class Exchange:
    def __init__(self, bits, halvings):
        self.bits, self.halvings = bits, halvings
        self.hops = bits + halvings
        self.me = lax.axis_index("dp")
        self.value = [lax.rem(self.me // 2**b, 2) for b in range(bits)]

    def order(self, turn):
        pairs = [(self.value[b], 2**b) for b in range(self.bits)]

        def either(flag, yes, no):
            return tuple(flag * y + (1 - flag) * n for y, n in zip(yes, no))

        odd = self.value[0]
        first = either(odd, pairs[2], pairs[1])
        second = either(odd, pairs[1], pairs[2])
        return [
            pairs[0],
            either(turn, pairs[3], first),
            either(turn, first, second),
            either(turn, second, pairs[3]),
        ] + pairs[4:]

    def partner(self, hop):
        bit, stride = hop
        return (self.me + (1 - 2 * bit) * stride,)

    def spans(self, turn, rows):
        at, size, result = 0, rows, []
        for bit, _ in self.order(turn)[: self.halvings]:
            size //= 2
            result.append((at + bit * size, at + (1 - bit) * size, size))
            at = at + bit * size
        return result


class Reduction:
    def __init__(self, exchange, turn, source, target, slots, sems, base, rows, later=None):
        self.x, self.source, self.target = exchange, source, target
        self.slots, self.sems, self.base, self.rows, self.later = slots, sems, base, rows, later
        self.order = exchange.order(turn)
        self.spans = exchange.spans(turn, rows)

    def rows_of(self, at, size):
        return pl.ds(pl.multiple_of(self.base + at, 8), size)

    def copy(self, hop):
        halvings, bits = self.x.halvings, self.x.bits
        send, recv = self.sems[:2]
        if hop < bits:
            if hop < halvings:
                _, at, size = self.spans[hop]
            else:
                at, _, size = self.spans[-1]
            src = self.source.at[self.rows_of(at, size)]
            dst = self.slots[hop]
            to = self.order[hop]
        else:
            level = halvings - 1 - (hop - bits)
            at, _, size = self.spans[level]
            src = dst = self.source.at[self.rows_of(at, size)]
            to = self.order[level]
        return pltpu.make_async_remote_copy(
            src_ref=src,
            dst_ref=dst,
            send_sem=send.at[hop],
            recv_sem=recv.at[hop],
            device_id=self.x.partner(to),
            device_id_type=MESH,
        )

    def out(self):
        where = pl.ds(self.base, self.rows)
        return pltpu.make_async_copy(self.source.at[where], self.target.at[where], self.sems[2])

    def step(self, k):
        x = self.x
        if k > 0:
            done = k - 1
            self.copy(done).wait()
            if done < x.bits:
                at, _, size = self.spans[min(done, x.halvings - 1)]
                where = self.rows_of(at, size)
                self.source[where] += self.slots[done][...]
                self.free(done)
            if done < x.halvings:
                pl.semaphore_signal(
                    self.sems[4].at[done], inc=1, device_id=x.partner(self.order[done]), device_id_type=MESH
                )
        if k == x.hops:
            self.out().start()
        if k < x.hops:
            if k < x.bits:
                self.wait_free(k)
            else:
                pl.semaphore_wait(self.sems[4].at[x.hops - 1 - k], 1)
            self.copy(k).start()

    def free(self, hop):
        if self.later is not None:
            credit, exists = self.later

            @pl.when(exists)
            def _():
                pl.semaphore_signal(
                    credit.at[hop],
                    inc=1,
                    device_id=self.x.partner(self.order[hop]),
                    device_id_type=MESH,
                )

    def wait_free(self, hop):
        credit, needed = self.sems[3] if self.sems[3] is not None else (None, None)
        if credit is not None:

            @pl.when(needed)
            def _():
                pl.semaphore_wait(credit.at[hop], 1)


def backward_kernel(
    sizes,
    bits,
    halvings,
    depth,
    starts,
    order,
    length_ref,
    grad_det_ref,
    mix_ref,
    grad_out_ref,
    norm_bias_ref,
    norm_logs_ref,
    start_w_ref,
    last_w_ref,
    end_w_ref,
    conv_w_ref,
    res_w_ref,
    hid_ref,
    tanh_ref,
    sig_ref,
    mixed_ref,
    wn_ref,
    scale_ref,
    x_ref,
    grad_in_ref,
    units_ref,
    misc_ref,
    *scratch,
):
    (
        unit_buf,
        misc_buf,
        act_buf,
        mixed_buf,
        wn_buf,
        scale_buf,
        x_buf,
        conv_stage,
        res_stage,
        stack_high,
        stack_low,
        back_high,
        back_low,
        turned_high,
        turned_low,
        gated_high,
        gated_low,
        pair_high,
        pair_low,
        grad_skip,
        grad_hid,
        grad_gated,
        grad_flow,
        grad_changed,
        columns_buf,
        act_sem,
        weight_sem,
        block_sem,
        send_sem,
        recv_sem,
        own_sem,
        credit_sem,
        clear_sem,
    ) = scratch[:33]
    slot_bufs = scratch[33 : 33 + bits]
    misc_slots = scratch[33 + bits :]
    blocks, layers, kernel, hidden_size, channels, frames = sizes
    half = channels // 2
    steps = blocks * layers
    deep = kernel * hidden_size
    wide = 2 * hidden_size
    middle = kernel // 2
    length = length_ref[0]
    mask = frame_mask(length, frames)
    grad_det = grad_det_ref[0]
    exchange = Exchange(bits, halvings)

    part_rows = (deep + hidden_size) // PARTS

    def reduction(unit, part):
        slot = lax.rem(unit, depth)
        after = unit + depth
        return Reduction(
            exchange,
            int(part == PARTS - 1),
            unit_buf.at[unit],
            units_ref.at[steps - 1 - unit],
            [b.at[slot, part] for b in slot_bufs],
            (
                send_sem.at[unit, part],
                recv_sem.at[unit, part],
                own_sem.at[unit, part],
                (credit_sem.at[unit, part], unit >= depth),
                clear_sem.at[unit, part],
            ),
            part * part_rows,
            part_rows,
            (credit_sem.at[jnp.minimum(after, steps - 1), part], after < steps),
        )

    misc_sum = Reduction(
        exchange,
        0,
        misc_buf,
        misc_ref,
        misc_slots,
        (send_sem.at[steps, 0], recv_sem.at[steps, 0], own_sem.at[steps, 0], None, clear_sem.at[steps, 0]),
        0,
        blocks * MISC,
    )

    def tick(step, point):
        for lag, part, k in due_steps(starts, point):
            unit = step - lag

            @pl.when(unit >= 0)
            def _(unit=unit, part=part, k=k):
                reduction(unit, part).step(k)

    def act_copies(step):
        slot = lax.rem(step, 2)
        at = steps - 1 - step
        return [
            pltpu.make_async_copy(ref.at[at], act_buf.at[slot, i], act_sem.at[slot, i])
            for i, ref in enumerate((hid_ref, tanh_ref, sig_ref))
        ]

    def weight_copies(step):
        slot = lax.rem(step, 2)
        block, layer = blocks - 1 - step // layers, layers - 1 - lax.rem(step, layers)
        conv = pltpu.make_async_copy(conv_w_ref.at[block, layer], conv_stage.at[slot], weight_sem.at[slot, 0])
        res = pltpu.make_async_copy(
            res_w_ref.at[block, jnp.minimum(layer, layers - 2)], res_stage.at[slot], weight_sem.at[slot, 1]
        )
        return [conv, res]

    def block_copies(block):
        return [
            pltpu.make_async_copy(ref.at[block], buf.at[block], block_sem.at[block, i])
            for i, (ref, buf) in enumerate(
                ((wn_ref, wn_buf), (scale_ref, scale_buf), (mixed_ref, mixed_buf), (x_ref, x_buf))
            )
        ]

    for block in reversed(range(blocks)):
        for copy in block_copies(block):
            copy.start()
    for copy in act_copies(0) + weight_copies(0):
        copy.start()

    barrier = pltpu.get_barrier_semaphore()
    for b in range(bits):
        pl.semaphore_signal(
            barrier, inc=1, device_id=exchange.partner((exchange.value[b], 2**b)), device_id_type=MESH
        )
    pl.semaphore_wait(barrier, bits)

    grad_flow[...] = grad_out_ref[0]
    misc_buf[...] = jnp.zeros_like(misc_buf)
    columns_buf[...] = jnp.zeros_like(columns_buf)
    for high, low, rows in ((stack_high, stack_low, deep), (gated_high, gated_low, hidden_size)):
        high[rows:, :] = jnp.ones((16, frames), bf16)
        low[rows:, :] = jnp.zeros((16, frames), bf16)

    def run_step(step, carry):
        block = blocks - 1 - step // layers
        layer = layers - 1 - lax.rem(step, layers)
        slot = lax.rem(step, 2)
        misc_at = block * MISC
        for copy in act_copies(step) + weight_copies(step):
            copy.wait()

        @pl.when(step + 1 < steps)
        def _():
            for copy in act_copies(step + 1) + weight_copies(step + 1):
                copy.start()

        tanh_part, sig_part = act_buf[slot, 1], act_buf[slot, 2]
        high, low = split(tanh_part * sig_part)
        gated_high[:hidden_size] = high
        gated_low[:hidden_size] = low

        @pl.when(layer == layers - 1)
        def _():
            for copy in block_copies(block):
                copy.wait()
            moved_grad = grad_flow[half:] * mask
            changed_grad = moved_grad * scale_buf[block]
            grad_changed[...] = changed_grad
            logs_grad = changed_grad * mixed_buf[block, half:] + (grad_det / length.astype(f32)) * mask
            out_grad = jnp.concatenate([moved_grad, logs_grad], axis=0)
            columns_buf[:channels, 0:1] = jnp.sum(out_grad, axis=1, keepdims=True)
            out_split = split(out_grad)
            end_grad = dot3(out_split, split(wn_buf[block]), NT)
            skip = dot3(split(end_w_ref[block]), out_split, TN) * mask
            columns_buf[:, 1:2] = jnp.sum(skip, axis=1, keepdims=True)
            skip_split = split(skip)
            pair_high[hidden_size:], pair_low[hidden_size:] = skip_split
            gated = (gated_high[:hidden_size], gated_low[:hidden_size])
            unit_buf[step, deep:, :hidden_size] = dot3(skip_split, gated, NT)
            unit_buf[step, deep : deep + channels, hidden_size:] = end_grad
            grad_gated[...] = dot3(split(last_w_ref[block]), skip_split, TN)
            grad_hid[...] = jnp.zeros_like(grad_hid)

        @pl.when(layer < layers - 1)
        def _():
            masked = grad_hid[...] * mask
            grad_hid[...] = masked
            pair_high[:hidden_size], pair_low[:hidden_size] = split(masked)
            pair = (pair_high[...], pair_low[...])
            grads = dot3((gated_high[...], gated_low[...]), pair, NT)
            unit_buf[step, deep:] = grads[:hidden_size]
            misc_buf[pl.ds(misc_at + half + 8 + layers + layer, 1), :] = grads[hidden_size : hidden_size + 1]
            grad_gated[...] = dot3(split(res_stage[slot]), pair)

        tick(step, 0)
        gated_grad = grad_gated[...]
        tanh_part, sig_part = act_buf[slot, 1], act_buf[slot, 2]
        inner = gated_grad * sig_part
        conv_grad = jnp.concatenate(
            [inner * (1.0 - tanh_part * tanh_part), inner * tanh_part * (1.0 - sig_part)], axis=0
        )
        fill_shifted(conv_grad, back_high, back_low, kernel, 1)
        fill_shifted(act_buf[slot, 0], stack_high, stack_low, kernel, -1)
        tick(step, 1)
        center = slice(middle * wide, (middle + 1) * wide)
        for part in range(PARTS):
            at = part * part_rows
            end = at + part_rows if part < PARTS - 1 else deep + 16
            grads = dot3((stack_high[at:end], stack_low[at:end]), (back_high[center], back_low[center]), NT)
            if part < PARTS - 1:
                unit_buf[step, at:end] = grads
            else:
                unit_buf[step, at:deep] = grads[: deep - at]
                misc_buf[pl.ds(misc_at + half + 8 + layer, 1), :] = grads[deep - at : deep - at + 1]
            tick(step, 2 + part)
        for k in range(kernel):
            high, low = split(conv_stage[slot, k * hidden_size : (k + 1) * hidden_size])
            turned_high[:, k * wide : (k + 1) * wide] = high
            turned_low[:, k * wide : (k + 1) * wide] = low
        grad_hid[...] += dot3((turned_high[...], turned_low[...]), (back_high[...], back_low[...]))

        @pl.when(layer == 0)
        def _():
            hid_grad = grad_hid[...] * mask
            hid_split = split(hid_grad)
            mixed = mixed_buf[block]
            start_grad = dot3(split(mixed[:half]), hid_split, NT)
            misc_buf[pl.ds(misc_at, half), :hidden_size] = start_grad
            columns_buf[:, 2:3] = jnp.sum(hid_grad, axis=1, keepdims=True)
            passed_grad = grad_flow[:half] + dot3(split(start_w_ref[block]), hid_split)
            mixed_grad = split(jnp.concatenate([passed_grad, grad_changed[...]], axis=0))
            norm_b = jnp.transpose(jnp.broadcast_to(norm_bias_ref[pl.ds(block, 1), :], (8, channels)))[:, 0:1]
            norm_s = jnp.exp(jnp.transpose(jnp.broadcast_to(norm_logs_ref[pl.ds(block, 1), :], (8, channels)))[:, 0:1])
            scaled = norm_s * x_buf[block]
            normed = (norm_b + scaled) * mask
            mix_grad = dot3(mixed_grad, split(normed), NT)
            normed_grad = dot3(split(mix_matrix(mix_ref, block, channels)), mixed_grad, TN) * mask
            columns_buf[:channels, 3:4] = jnp.sum(normed_grad, axis=1, keepdims=True)
            columns_buf[:channels, 4:5] = jnp.sum(normed_grad * scaled, axis=1, keepdims=True) + grad_det
            grad_flow[...] = normed_grad * norm_s
            rows = columns_buf[...].T
            misc_buf[pl.ds(misc_at + half, 8), :hidden_size] = rows[:8]
            inverse, _ = inverse_logdet(mix_ref, block)
            misc_buf[pl.ds(misc_at + half + 16, 8), :] = mix_rows(
                mix_grad, inverse, grad_det * (channels // 4), wide
            )

        tick(step, POINTS - 1)
        return carry

    lax.fori_loop(0, steps, run_step, 0)
    grad_in_ref[0] = grad_flow[...]
    for unit, part, k in order:
        (misc_sum if unit == steps else reduction(unit, part)).step(k)
    misc_sum.out().wait()

    def end_outs(unit, carry):
        for part in range(PARTS):
            reduction(unit, part).out().wait()
        return carry

    lax.fori_loop(0, steps, end_outs, 0)


def mix_rows(products, inverse, factor, wide):
    channels = products.shape[0]
    half = channels // 2
    rows = lax.broadcasted_iota(jnp.int32, (channels, channels), 0)
    cols = lax.broadcasted_iota(jnp.int32, (channels, channels), 1)
    row_top, col_top = rows < half, cols < half
    row_in = jnp.where(row_top, rows, rows - half)
    col_in = jnp.where(col_top, cols, cols - half)
    row_member = jnp.where(row_top, 0, 2) + (row_in & 1)
    col_member = jnp.where(col_top, 0, 2) + (col_in & 1)
    same = (row_in >> 1) == (col_in >> 1)
    kept = jnp.where(same, products, 0.0)
    row = lax.broadcasted_iota(jnp.int32, (8, wide), 0)
    lane = lax.broadcasted_iota(jnp.int32, (8, wide), 1)
    result = jnp.zeros((8, wide), f32)
    for i in range(4):
        mine = jnp.where(row_member == i, kept, 0.0)
        for j in range(4):
            picked = jnp.where(col_member == j, mine, 0.0)
            total = jnp.sum(jnp.sum(picked, axis=0, keepdims=True), axis=1, keepdims=True)
            total = total + factor * inverse[j][i][0:1, 0:1]
            result = jnp.where((row == i) & (lane == j), total, result)
    return result


def finish_kernel(
    sizes,
    units_ref,
    misc_ref,
    grad_in_ref,
    grad_in_out,
    norm_b_out,
    norm_l_out,
    mix_out,
    start_w_out,
    start_b_out,
    conv_w_out,
    conv_b_out,
    res_w_out,
    res_b_out,
    last_w_out,
    last_b_out,
    end_w_out,
    end_b_out,
    units_buf,
    grad_in_buf,
    sems,
):
    blocks, layers, kernel, hidden_size, channels, frames = sizes
    half = channels // 2
    deep = kernel * hidden_size
    steps = blocks * layers
    loads = [pltpu.make_async_copy(units_ref.at[i], units_buf.at[i], sems.at[0, i]) for i in range(steps)]
    loads.append(pltpu.make_async_copy(grad_in_ref, grad_in_buf, sems.at[0, steps]))
    for load in loads:
        load.start()
    stores = []
    for i in range(steps):
        loads[i].wait()
        b, layer = i // layers, i % layers
        stores.append(pltpu.make_async_copy(units_buf.at[i, :deep], conv_w_out.at[b, layer], sems.at[1, i]))
        if layer < layers - 1:
            stores[-1].start()
            stores.append(pltpu.make_async_copy(units_buf.at[i, deep:], res_w_out.at[b, layer], sems.at[2, i]))
        stores[-1].start()
    loads[steps].wait()
    stores.append(pltpu.make_async_copy(grad_in_buf, grad_in_out, sems.at[1, steps]))
    stores[-1].start()
    for b in range(blocks):
        at = b * MISC
        start_w_out[b] = misc_ref[at : at + half, :hidden_size]
        at += half
        for row, (out, width) in enumerate(
            ((end_b_out, channels), (last_b_out, hidden_size), (start_b_out, hidden_size), (norm_b_out, channels), (norm_l_out, channels))
        ):
            out[b : b + 1, :] = misc_ref[at + row : at + row + 1, :width]
        conv_b_out[b] = misc_ref[at + 8 : at + 8 + layers]
        for layer in range(layers - 1):
            res_b_out[layer, b : b + 1, :] = misc_ref[at + 8 + layers + layer : at + 9 + layers + layer]
        mix_out[b] = misc_ref[at + 16 : at + 20, :4]
    for b in range(blocks):
        tail = units_buf[(b + 1) * layers - 1, deep:]
        last_w_out[b] = tail[:, :hidden_size]
        end_w_out[b] = tail[:channels, hidden_size:]
    for store in stores:
        store.wait()


def finish_call(sizes, grad_in, units, misc):
    blocks, layers, kernel, hidden_size, channels, frames = sizes
    half, deep, wide = channels // 2, kernel * hidden_size, 2 * hidden_size
    vmem = pl.BlockSpec(memory_space=pltpu.VMEM)
    hbm = pl.BlockSpec(memory_space=pl.ANY)
    dims = [
        (1, channels, frames),
        (blocks, channels),
        (blocks, channels),
        (blocks, 4, 4),
        (blocks, half, hidden_size),
        (blocks, hidden_size),
        (blocks, layers, deep, wide),
        (blocks, layers, wide),
        (blocks, layers - 1, hidden_size, wide),
        (layers - 1, blocks, wide),
        (blocks, hidden_size, hidden_size),
        (blocks, hidden_size),
        (blocks, channels, hidden_size),
        (blocks, channels),
    ]
    large = (0, 6, 8)
    return pl.pallas_call(
        functools.partial(finish_kernel, sizes),
        name="flow_finish",
        out_shape=[jax.ShapeDtypeStruct(d, f32) for d in dims],
        in_specs=[hbm, vmem, hbm],
        out_specs=[hbm if i in large else vmem for i in range(len(dims))],
        scratch_shapes=[
            pltpu.VMEM((blocks * layers, deep + hidden_size, wide), f32),
            pltpu.VMEM((1, channels, frames), f32),
            pltpu.SemaphoreType.DMA((3, blocks * layers + 1)),
        ],
        compiler_params=pltpu.CompilerParams(vmem_limit_bytes=VMEM_LIMIT),
    )(units, misc, grad_in)


def backward_call(count, lengths, grad_det, grad_out, params, saved):
    (norm_bias, norm_logs, mix, start_w, _, conv_w, _, res_w, _, last_w, _, end_w, _) = params
    hid, tanh_all, sig_all, mixed, wn, scale, x_all = saved
    _, channels, frames = grad_out.shape
    conv_w, res_w, start_w = conv_w.swapaxes(2, 3), res_w.swapaxes(2, 3), start_w.swapaxes(1, 2)
    blocks, layers, deep, wide = conv_w.shape
    hidden_size = wide // 2
    kernel = deep // hidden_size
    half = channels // 2
    steps = blocks * layers
    sizes = (blocks, layers, kernel, hidden_size, channels, frames)
    bits = count.bit_length() - 1
    halvings = 4
    depth = 3
    rows = deep + hidden_size
    part_rows = rows // PARTS
    vmem = pl.BlockSpec(memory_space=pltpu.VMEM)
    smem = pl.BlockSpec(memory_space=pltpu.SMEM)
    hbm = pl.BlockSpec(memory_space=pl.ANY)
    shape = jax.ShapeDtypeStruct
    shares = [2 ** -min(hop + 1, halvings) for hop in range(bits)]
    hops = bits + halvings
    starts = [
        row if len(row) == hops + 1 else [ready + 2 * k for k in range(hops + 1)]
        for row, ready in zip(STARTS, READY)
    ]
    order = drain_order(starts, bits, halvings, steps, part_rows, blocks * MISC)
    return pl.pallas_call(
        functools.partial(backward_kernel, sizes, bits, halvings, depth, starts, order),
        name="flow_backward",
        out_shape=[
            shape((1, channels, frames), f32),
            shape((steps, rows, wide), f32),
            shape((blocks * MISC, wide), f32),
        ],
        in_specs=[smem, smem, smem] + [vmem] * 6 + [hbm] * 9,
        out_specs=[vmem, hbm, hbm],
        scratch_shapes=[
            pltpu.VMEM((steps, rows, wide), f32),
            pltpu.VMEM((blocks * MISC, wide), f32),
            pltpu.VMEM((2, 3, hidden_size, frames), f32),
            pltpu.VMEM((blocks, channels, frames), f32),
            pltpu.VMEM((blocks, hidden_size, frames), f32),
            pltpu.VMEM((blocks, half, frames), f32),
            pltpu.VMEM((blocks, channels, frames), f32),
            pltpu.VMEM((2, deep, wide), f32),
            pltpu.VMEM((2, hidden_size, wide), f32),
            pltpu.VMEM((deep + 16, frames), bf16),
            pltpu.VMEM((deep + 16, frames), bf16),
            pltpu.VMEM((kernel * wide, frames), bf16),
            pltpu.VMEM((kernel * wide, frames), bf16),
            pltpu.VMEM((hidden_size, kernel * wide), bf16),
            pltpu.VMEM((hidden_size, kernel * wide), bf16),
            pltpu.VMEM((hidden_size + 16, frames), bf16),
            pltpu.VMEM((hidden_size + 16, frames), bf16),
            pltpu.VMEM((wide, frames), bf16),
            pltpu.VMEM((wide, frames), bf16),
            pltpu.VMEM((hidden_size, frames), f32),
            pltpu.VMEM((hidden_size, frames), f32),
            pltpu.VMEM((hidden_size, frames), f32),
            pltpu.VMEM((channels, frames), f32),
            pltpu.VMEM((half, frames), f32),
            pltpu.VMEM((hidden_size, 128), f32),
            pltpu.SemaphoreType.DMA((2, 3)),
            pltpu.SemaphoreType.DMA((2, 2)),
            pltpu.SemaphoreType.DMA((blocks, 4)),
            pltpu.SemaphoreType.DMA((steps + 1, PARTS, hops)),
            pltpu.SemaphoreType.DMA((steps + 1, PARTS, hops)),
            pltpu.SemaphoreType.DMA((steps + 1, PARTS)),
            pltpu.SemaphoreType.REGULAR((steps, PARTS, bits)),
            pltpu.SemaphoreType.REGULAR((steps + 1, PARTS, halvings)),
        ]
        + [pltpu.VMEM((depth, PARTS, int(part_rows * s), wide), f32) for s in shares]
        + [pltpu.VMEM((int(blocks * MISC * s), wide), f32) for s in shares],
        compiler_params=pltpu.CompilerParams(
            collective_id=0, has_side_effects=True, vmem_limit_bytes=VMEM_LIMIT
        ),
    )(lengths, grad_det, mix, grad_out, norm_bias, norm_logs, start_w, last_w, end_w, conv_w, res_w,
      hid, tanh_all, sig_all, mixed, wn, scale, x_all)


def shards(mesh_size, mel, lengths, *rest):
    params, grad_out, grad_det = rest[:13], rest[13], rest[14]
    flowed, logdet, *saved = forward_call(mel, lengths, params)
    blocks, layers, wide, deep = params[5].shape
    hidden_size = wide // 2
    sizes = (blocks, layers, deep // hidden_size, hidden_size, mel.shape[1], mel.shape[2])
    summed = backward_call(mesh_size, lengths, grad_det, grad_out, params, saved)
    grads = list(finish_call(sizes, *summed))
    for i in (6, 8):
        grads[i] = grads[i].swapaxes(2, 3)
    grads[4] = grads[4].swapaxes(1, 2)
    grads[9] = grads[9].swapaxes(0, 1)
    return (flowed, logdet[0, :1], *grads)


def solution(mesh):
    split_first, whole = P("dp", None, None), P()
    in_specs = (split_first, P("dp")) + (whole,) * 13 + (split_first, P("dp"))
    out_specs = (split_first, P("dp"), split_first) + (whole,) * 13
    return jax.shard_map(
        functools.partial(shards, mesh.shape["dp"]),
        mesh=mesh,
        in_specs=in_specs,
        out_specs=out_specs,
        check_vma=False,
    )
```

```python
import functools

import jax
import jax.numpy as jnp
from jax import lax
from jax.experimental import pallas as pl
from jax.experimental.pallas import tpu as pltpu
from jax.sharding import PartitionSpec as P

f32, bf16 = jnp.float32, jnp.bfloat16
NN = (((1,), (0,)), ((), ()))
NT = (((1,), (1,)), ((), ()))
TN = (((0,), (0,)), ((), ()))
VMEM_LIMIT = 60 * 2**20


def dot(left, right, form=NN):
    return lax.dot_general(left, right, form, preferred_element_type=f32)


def split(value):
    high = value.astype(bf16)
    return high, (value - high.astype(f32)).astype(bf16)


def dot3(left, right, form=NN):
    (left_high, left_low), (right_high, right_low) = left, right
    return (
        dot(left_high, right_high, form)
        + dot(left_high, right_low, form)
        + dot(left_low, right_high, form)
    )


def mix_matrix(mix_ref, block, channels):
    half = channels // 2
    rows = lax.broadcasted_iota(jnp.int32, (channels, channels), 0)
    cols = lax.broadcasted_iota(jnp.int32, (channels, channels), 1)
    row_top, col_top = rows < half, cols < half
    row_in = jnp.where(row_top, rows, rows - half)
    col_in = jnp.where(col_top, cols, cols - half)
    row_member = jnp.where(row_top, 0, 2) + (row_in & 1)
    col_member = jnp.where(col_top, 0, 2) + (col_in & 1)
    same = (row_in >> 1) == (col_in >> 1)
    pair = row_member * 4 + col_member
    result = jnp.zeros((channels, channels), f32)
    for i in range(4):
        for j in range(4):
            result = jnp.where(pair == 4 * i + j, mix_ref[block, i, j], result)
    return jnp.where(same, result, 0.0)


def inverse_logdet(mix_ref, block):
    shape = (8, 128)
    left = [[jnp.full(shape, mix_ref[block, i, j], f32) for j in range(4)] for i in range(4)]
    right = [[jnp.full(shape, float(i == j), f32) for j in range(4)] for i in range(4)]
    log_total = jnp.zeros(shape, f32)
    for k in range(4):
        pivot = left[k][k]
        log_total = log_total + jnp.log(pivot)
        left[k] = [v / pivot for v in left[k]]
        right[k] = [v / pivot for v in right[k]]
        for i in range(4):
            if i != k:
                factor = left[i][k]
                left[i] = [v - factor * w for v, w in zip(left[i], left[k])]
                right[i] = [v - factor * w for v, w in zip(right[i], right[k])]
    return right, log_total


def fill_columns(rows_ref, cols_ref, block, vectors):
    rows_ref[...] = jnp.zeros_like(rows_ref)
    for j, vector in enumerate(vectors):
        rows_ref[j : j + 1, : vector.shape[1]] = vector
    cols_ref[...] = rows_ref[...].T


def frame_mask(length, frames):
    return (lax.broadcasted_iota(jnp.int32, (1, frames), 1) < length).astype(f32)


ROWS = 16


def chunks(rows, size=ROWS):
    return [slice(at, min(at + size, rows)) for at in range(0, rows, size)]


def shift_by(at, by):
    return slice(at.start + by, at.stop + by)


def fill_shifted(source, high_ref, low_ref, kernel, sign):
    channels, frames = source.shape
    for at in chunks(channels):
        value = source[at]
        for k in range(kernel):
            move = (sign * (k - kernel // 2)) % frames
            to = shift_by(at, k * channels)
            high_ref[to], low_ref[to] = split(pltpu.roll(value, move, 1) if move else value)


def fill_split(source, high_ref, low_ref, size=64):
    for at in chunks(source.shape[0], size):
        high_ref[at], low_ref[at] = split(source[at])


def forward_kernel(
    sizes,
    length_ref,
    mix_ref,
    x_ref,
    norm_bias_ref,
    norm_logs_ref,
    start_w_ref,
    start_b_ref,
    conv_w_ref,
    conv_b_ref,
    res_w_ref,
    res_b_ref,
    last_w_ref,
    last_b_ref,
    end_w_ref,
    end_b_ref,
    flowed_ref,
    logdet_ref,
    hid_out,
    tanh_out,
    sig_out,
    mixed_out,
    wn_out,
    scale_out,
    x_out,
    x_buf,
    hid_buf,
    tanh_buf,
    sig_buf,
    mixed_buf,
    wn_buf,
    scale_buf,
    conv_stage,
    res_stage,
    stack_high,
    stack_low,
    conv_high,
    conv_low,
    res_high,
    res_low,
    gated_high,
    gated_low,
    out_buf,
    skip_buf,
    det_buf,
    rows_buf,
    cols_buf,
    in_sem,
    out_sem,
    misc_sem,
):
    blocks, layers, kernel, hidden_size, channels, frames = sizes
    half = channels // 2
    steps = blocks * layers
    length = length_ref[0]
    mask = frame_mask(length, frames)

    def conv_copy(block, layer):
        at = block * layers + layer
        return pltpu.make_async_copy(conv_w_ref.at[block, layer], conv_stage.at[at], in_sem.at[0, at])

    def res_copy(block, layer):
        at = block * layers + layer
        return pltpu.make_async_copy(res_w_ref.at[block, layer], res_stage.at[at], in_sem.at[1, at])

    def saves(step):
        return [
            pltpu.make_async_copy(buf.at[step], out.at[step], out_sem.at[i, step])
            for i, (buf, out) in enumerate(
                ((hid_buf, hid_out), (tanh_buf, tanh_out), (sig_buf, sig_out))
            )
        ]

    def block_saves(block):
        return [
            pltpu.make_async_copy(buf.at[block], out.at[block], misc_sem.at[i, block])
            for i, (buf, out) in enumerate(
                ((mixed_buf, mixed_out), (wn_buf, wn_out), (scale_buf, scale_out), (x_buf, x_out))
            )
        ]

    for block in range(blocks):
        for layer in range(layers):
            conv_copy(block, layer).start()
            if layer < layers - 1:
                res_copy(block, layer).start()
    x_buf[0] = x_ref[0]
    det_buf[...] = jnp.zeros_like(det_buf)

    def run_block(block, carry):
        fill_columns(
            rows_buf,
            cols_buf,
            block,
            [conv_b_ref[block, pl.ds(l, 1), :] for l in range(layers)]
            + [res_b_ref[l, pl.ds(block, 1), :] for l in range(layers - 1)]
            + [
                r[pl.ds(block, 1), :]
                for r in (start_b_ref, last_b_ref, end_b_ref, norm_bias_ref, norm_logs_ref)
            ],
        )
        base = 2 * layers - 1
        start_b = cols_buf[:hidden_size, base : base + 1]
        last_b = cols_buf[:hidden_size, base + 1 : base + 2]
        end_b = cols_buf[:channels, base + 2 : base + 3]
        norm_b = cols_buf[:channels, base + 3 : base + 4]
        norm_l = cols_buf[:channels, base + 4 : base + 5]
        normed = (norm_b + jnp.exp(norm_l) * x_buf[block]) * mask
        mixed = dot3(split(mix_matrix(mix_ref, block, channels)), split(normed))
        mixed_buf[block] = mixed
        hidden = (dot3(split(start_w_ref[block]), split(mixed[:half]), TN) + start_b) * mask
        hid_buf[block * layers] = hidden

        for layer in range(layers):
            step = block * layers + layer
            last = layer == layers - 1
            saves(step)[0].start()
            conv_copy(block, layer).wait()
            if not last:
                res_copy(block, layer).wait()
            fill_split(conv_stage.at[step], conv_high, conv_low)
            fill_shifted(hid_buf.at[step], stack_high, stack_low, kernel, -1)
            if not last:
                fill_split(res_stage.at[step], res_high, res_low)
            out_buf[...] = dot3((conv_high[...], conv_low[...]), (stack_high[...], stack_low[...]), TN)
            for at in chunks(hidden_size):
                below = shift_by(at, hidden_size)
                tanh_part = jnp.tanh(out_buf[at] + cols_buf[at, layer : layer + 1])
                sig_part = 0.5 * jnp.tanh(0.5 * (out_buf[below] + cols_buf[below, layer : layer + 1])) + 0.5
                tanh_buf[step, at] = tanh_part
                sig_buf[step, at] = sig_part
                gated_high[at], gated_low[at] = split(tanh_part * sig_part)
            gated = (gated_high[...], gated_low[...])
            if last:
                skip_buf[...] += dot3(split(last_w_ref[block]), gated)
            else:
                out_buf[...] = dot3((res_high[...], res_low[...]), gated, TN)
                bias = slice(layers + layer, layers + layer + 1)
                for at in chunks(hidden_size):
                    below = shift_by(at, hidden_size)
                    res = out_buf[below] + cols_buf[below, bias]
                    skip_buf[at] = res + (skip_buf[at] if layer else last_b[at])
                    hid_buf[step + 1, at] = (hid_buf[step, at] + (out_buf[at] + cols_buf[at, bias])) * mask
            for save in saves(step)[1:]:
                save.start()
        wavenet = skip_buf[...] * mask
        wn_buf[block] = wavenet
        out = dot3(split(end_w_ref[block]), split(wavenet)) + end_b
        scale = jnp.exp(out[half:])
        scale_buf[block] = scale
        mixed = mixed_buf[block]
        moved = (out[:half] + scale * mixed[half:]) * mask
        _, log_det = inverse_logdet(mix_ref, block)
        det_buf[0:1, :] += jnp.sum(norm_l) + log_det[0:1, :] * (channels // 4)
        det_buf[1:2, :] += jnp.full((1, 128), jnp.sum(out[half:] * mask))
        x_buf[block + 1, :half] = mixed[:half]
        x_buf[block + 1, half:] = moved
        for save in block_saves(block):
            save.start()
        return carry

    lax.fori_loop(0, blocks, run_block, 0)
    flowed_ref[0] = x_buf[blocks]
    logdet_ref[...] = det_buf[0:1, :] + det_buf[1:2, :] / length.astype(f32)

    def finish(step, carry):
        for save in saves(step):
            save.wait()
        return carry

    lax.fori_loop(0, steps, finish, 0)

    def finish_block(block, carry):
        for save in block_saves(block):
            save.wait()
        return carry

    lax.fori_loop(0, blocks, finish_block, 0)


def forward_call(mel, lengths, params):
    (norm_bias, norm_logs, mix, start_w, start_b, conv_w, conv_b, res_w, res_b, last_w, last_b, end_w, end_b) = params
    _, channels, frames = mel.shape
    conv_w, res_w = conv_w.swapaxes(2, 3), res_w.swapaxes(2, 3)
    start_w, res_b = start_w.swapaxes(1, 2), res_b.swapaxes(0, 1)
    blocks, layers, deep, wide = conv_w.shape
    hidden_size = wide // 2
    kernel = deep // hidden_size
    half = channels // 2
    steps = blocks * layers
    sizes = (blocks, layers, kernel, hidden_size, channels, frames)
    vmem = pl.BlockSpec(memory_space=pltpu.VMEM)
    smem = pl.BlockSpec(memory_space=pltpu.SMEM)
    hbm = pl.BlockSpec(memory_space=pl.ANY)
    shape = jax.ShapeDtypeStruct
    act = (steps, hidden_size, frames)
    return pl.pallas_call(
        functools.partial(forward_kernel, sizes),
        name="flow_forward",
        out_shape=[
            shape((1, channels, frames), f32),
            shape((1, 128), f32),
            shape(act, f32),
            shape(act, f32),
            shape(act, f32),
            shape((blocks, channels, frames), f32),
            shape((blocks, hidden_size, frames), f32),
            shape((blocks, half, frames), f32),
            shape((blocks, channels, frames), f32),
        ],
        in_specs=[smem, smem, vmem, vmem, vmem, vmem, vmem, hbm, vmem, hbm, vmem, vmem, vmem, vmem, vmem],
        out_specs=[vmem, vmem] + [hbm] * 7,
        scratch_shapes=[
            pltpu.VMEM((blocks + 1, channels, frames), f32),
            pltpu.VMEM(act, f32),
            pltpu.VMEM(act, f32),
            pltpu.VMEM(act, f32),
            pltpu.VMEM((blocks, channels, frames), f32),
            pltpu.VMEM((blocks, hidden_size, frames), f32),
            pltpu.VMEM((blocks, half, frames), f32),
            pltpu.VMEM((steps, deep, wide), f32),
            pltpu.VMEM((steps, hidden_size, wide), f32),
            pltpu.VMEM((deep, frames), bf16),
            pltpu.VMEM((deep, frames), bf16),
            pltpu.VMEM((deep, wide), bf16),
            pltpu.VMEM((deep, wide), bf16),
            pltpu.VMEM((hidden_size, wide), bf16),
            pltpu.VMEM((hidden_size, wide), bf16),
            pltpu.VMEM((hidden_size, frames), bf16),
            pltpu.VMEM((hidden_size, frames), bf16),
            pltpu.VMEM((wide, frames), f32),
            pltpu.VMEM((hidden_size, frames), f32),
            pltpu.VMEM((8, 128), f32),
            pltpu.VMEM((16, wide), f32),
            pltpu.VMEM((wide, 16), f32),
            pltpu.SemaphoreType.DMA((2, steps)),
            pltpu.SemaphoreType.DMA((3, steps)),
            pltpu.SemaphoreType.DMA((4, blocks)),
        ],
        compiler_params=pltpu.CompilerParams(vmem_limit_bytes=VMEM_LIMIT),
    )(lengths, mix, mel, norm_bias, norm_logs, start_w, start_b, conv_w, conv_b, res_w, res_b, last_w, last_b, end_w, end_b)
MESH = pl.DeviceIdType.MESH
MISC = 128
PARTS = 3
POINTS = 6
READY = (2, 3, 4)
STARTS = ((2, 3, 5, 8, 12, 17, 19, 23, 45, 46), (3, 4, 6, 9, 11, 14, 18, 20, 37, 47), (4, 5, 10, 12, 15, 17, 19, 22, 25, 31))


POINT_US = (2.2, 1.0, 1.1, 1.1, 1.1, 2.75)
LINK_ROWS, CORE_ROWS = 62.0, 420.0
LATENCY = {"core": 0.75, "far": 2.6}


class Link:
    def __init__(self, rate):
        self.queues, self.clock, self.rate = ([], []), 0.0, rate

    def run(self, until):
        while any(self.queues) and self.clock < until:
            heads = [queue[0] for queue in self.queues if queue]
            rate = self.rate / len(heads)
            spent = min(min(head[0] for head in heads) / rate, until - self.clock)
            self.clock += spent
            for queue in self.queues:
                if queue:
                    queue[0][0] -= spent * rate
                    if queue[0][0] < 1e-6:
                        queue.pop(0)[1] = self.clock
        if self.clock < until < float("inf"):
            self.clock = until

    def add(self, now, core, rows):
        self.run(now)
        job = [rows, None]
        self.queues[core].append(job)
        return self, job


class Plan:
    def __init__(self, bits, halvings, steps, part_rows, misc_rows):
        self.bits, self.hops, self.steps = bits, bits + halvings, steps
        self.rows = (part_rows, misc_rows)
        self.links = {name: Link(LINK_ROWS) for name in ("x", "y", "z", "middle")}
        self.links |= {("core", core): Link(CORE_ROWS) for core in range(2)}
        self.clock, self.jobs, self.taken = 0.0, {}, {}
        sizes = [2 ** -(h + 1) for h in range(halvings)]
        self.sizes = sizes + [sizes[-1]] * (bits - halvings) + sizes[::-1]

    def name(self, part, k):
        near = ("z", "a", "b") if part == PARTS - 1 else ("a", "b", "z")
        return ["core", *near, *["far"] * (self.bits - 4), *reversed(near), "core"][k]

    def start(self, unit, part, k):
        name, jobs = self.name(part, k), []
        rows = self.sizes[k] * self.rows[unit == self.steps]
        for core in range(2):
            if name == "core":
                jobs.append(self.links[name, core].add(self.clock, core, rows))
                continue
            link = "z" if name in ("z", "far") else "xy"[(name == "b") ^ core]
            jobs.append(self.links[link].add(self.clock, core, rows))
            if name == "far":
                jobs.append(self.links["middle"].add(self.clock, core, 2 * rows))
        self.jobs[unit, part] = jobs, LATENCY.get(name, 2.1)

    def arrival(self, unit, part, until=float("inf")):
        if not self.taken.get((unit, part)):
            return 0.0
        jobs, latency = self.jobs[unit, part]
        for link, job in jobs:
            if job[1] is None:
                link.run(until)
            if job[1] is None:
                return float("inf")
        return max(job[1] for _, job in jobs) + latency

    def take(self, unit, part, k):
        if k:
            self.clock = max(self.clock, self.arrival(unit, part)) + 0.1
        self.taken[unit, part] = k + 1
        if k < self.hops:
            self.start(unit, part, k)


def drain_order(starts, bits, halvings, depth, steps, part_rows, misc_rows):
    plan = Plan(bits, halvings, steps, part_rows, misc_rows)
    for layer in range(steps):
        for point in range(POINTS):
            plan.clock += POINT_US[point]
            for lag, part, k in due_steps(starts, point):
                if layer >= lag:
                    plan.take(layer - lag, part, k)
    order, taken = [], plan.taken
    waiting = [(unit, part) for unit in range(steps) for part in range(PARTS)] + [(steps, 0)]
    waiting = [w for w in waiting if taken.get(w, 0) <= plan.hops]
    while waiting:
        ready = []
        for unit, part in waiting:
            k = taken.get((unit, part), 0)
            slot_free = unit in range(depth) or unit == steps or k >= bits or taken[unit - depth, part] > k + 1
            if slot_free and plan.arrival(unit, part, plan.clock) <= plan.clock:
                ready.append((k >= bits, unit, part, k))
        if not ready:
            plan.clock += 0.1
            continue
        _, unit, part, k = min(ready)
        plan.take(unit, part, k)
        order.append((unit, part, k))
        if k == plan.hops:
            waiting.remove((unit, part))
    return order


def due_steps(starts, point):
    due = [
        (start // POINTS, part, k)
        for part, row in enumerate(starts)
        for k, start in enumerate(row)
        if start % POINTS == point
    ]
    return sorted(due, key=lambda due: (-due[0], due[1], due[2]))


class Exchange:
    def __init__(self, bits, halvings):
        self.bits, self.halvings = bits, halvings
        self.hops = bits + halvings
        self.me = lax.axis_index("dp")
        self.value = [lax.rem(self.me // 2**b, 2) for b in range(bits)]

    def order(self, turn):
        pairs = [(self.value[b], 2**b) for b in range(self.bits)]

        def either(flag, yes, no):
            return tuple(flag * y + (1 - flag) * n for y, n in zip(yes, no))

        odd = self.value[0]
        first = either(odd, pairs[2], pairs[1])
        second = either(odd, pairs[1], pairs[2])
        return [
            pairs[0],
            either(turn, pairs[3], first),
            either(turn, first, second),
            either(turn, second, pairs[3]),
        ] + pairs[4:]

    def partner(self, hop):
        bit, stride = hop
        return (self.me + (1 - 2 * bit) * stride,)

    def spans(self, turn, rows):
        at, size, result = 0, rows, []
        for bit, _ in self.order(turn)[: self.halvings]:
            size //= 2
            result.append((at + bit * size, at + (1 - bit) * size, size))
            at = at + bit * size
        return result


class Reduction:
    def __init__(self, exchange, turn, source, target, slots, sems, base, rows, later=None):
        self.x, self.source, self.target = exchange, source, target
        self.slots, self.sems, self.base, self.rows, self.later = slots, sems, base, rows, later
        self.order = exchange.order(turn)
        self.spans = exchange.spans(turn, rows)

    def rows_of(self, at, size):
        return pl.ds(pl.multiple_of(self.base + at, 8), size)

    def copy_sem(self, side, hop):
        out, back = self.sems[0], self.sems[1]
        return out.at[side, hop] if hop < self.x.bits else back.at[side, hop - self.x.bits]

    def copy(self, hop):
        halvings, bits = self.x.halvings, self.x.bits
        if hop < bits:
            if hop < halvings:
                _, at, size = self.spans[hop]
            else:
                at, _, size = self.spans[-1]
            src = self.source.at[self.rows_of(at, size)]
            dst = self.slots[hop]
            to = self.order[hop]
        else:
            level = halvings - 1 - (hop - bits)
            at, _, size = self.spans[level]
            src = dst = self.source.at[self.rows_of(at, size)]
            to = self.order[level]
        return pltpu.make_async_remote_copy(
            src_ref=src,
            dst_ref=dst,
            send_sem=self.copy_sem(0, hop),
            recv_sem=self.copy_sem(1, hop),
            device_id=self.x.partner(to),
            device_id_type=MESH,
        )

    def out(self):
        where = pl.ds(self.base, self.rows)
        return pltpu.make_async_copy(self.source.at[where], self.target.at[where], self.sems[2])

    def step(self, k):
        x = self.x
        if k > 0:
            done = k - 1
            self.copy(done).wait()
            if done < x.bits:
                at, _, size = self.spans[min(done, x.halvings - 1)]
                where = self.rows_of(at, size)
                self.source[where] += self.slots[done][...]
                self.free(done)
            if done < x.halvings:
                pl.semaphore_signal(
                    self.sems[4].at[done], inc=1, device_id=x.partner(self.order[done]), device_id_type=MESH
                )
        if k == x.hops:
            self.out().start()
        if k < x.hops:
            if k < x.bits:
                self.wait_free(k)
            else:
                pl.semaphore_wait(self.sems[4].at[x.hops - 1 - k], 1)
            self.copy(k).start()

    def free(self, hop):
        if self.later is not None:
            credit, exists = self.later

            @pl.when(exists)
            def _():
                pl.semaphore_signal(
                    credit.at[hop],
                    inc=1,
                    device_id=self.x.partner(self.order[hop]),
                    device_id_type=MESH,
                )

    def wait_free(self, hop):
        credit, needed = self.sems[3] if self.sems[3] is not None else (None, None)
        if credit is not None:

            @pl.when(needed)
            def _():
                pl.semaphore_wait(credit.at[hop], 1)


def backward_kernel(
    sizes,
    bits,
    halvings,
    depth,
    starts,
    order,
    length_ref,
    grad_det_ref,
    mix_ref,
    grad_out_ref,
    norm_bias_ref,
    norm_logs_ref,
    start_w_ref,
    last_w_ref,
    end_w_ref,
    conv_w_ref,
    res_w_ref,
    hid_ref,
    tanh_ref,
    sig_ref,
    mixed_ref,
    wn_ref,
    scale_ref,
    x_ref,
    grad_in_ref,
    units_ref,
    misc_ref,
    *scratch,
):
    (
        unit_buf,
        misc_buf,
        act_buf,
        mixed_buf,
        wn_buf,
        scale_buf,
        x_buf,
        conv_stage,
        res_stage,
        stack_high,
        stack_low,
        back_high,
        back_low,
        turned_high,
        turned_low,
        gated_high,
        gated_low,
        pair_high,
        pair_low,
        grad_skip,
        grad_hid,
        grad_gated,
        grad_flow,
        grad_changed,
        columns_buf,
        act_sem,
        weight_sem,
        block_sem,
        out_copy_sem,
        back_copy_sem,
        own_sem,
        credit_sem,
        clear_sem,
    ) = scratch[:33]
    slot_bufs = scratch[33 : 33 + bits]
    misc_slots = scratch[33 + bits :]
    blocks, layers, kernel, hidden_size, channels, frames = sizes
    half = channels // 2
    steps = blocks * layers
    deep = kernel * hidden_size
    wide = 2 * hidden_size
    middle = kernel // 2
    length = length_ref[0]
    mask = frame_mask(length, frames)
    grad_det = grad_det_ref[0]
    exchange = Exchange(bits, halvings)

    part_rows = (deep + hidden_size) // PARTS

    def reduction(unit, part):
        slot = lax.rem(unit, depth)
        after = unit + depth
        return Reduction(
            exchange,
            int(part == PARTS - 1),
            unit_buf.at[unit],
            units_ref.at[steps - 1 - unit],
            [b.at[slot, part] for b in slot_bufs],
            (
                out_copy_sem.at[slot * PARTS + part],
                back_copy_sem.at[unit * PARTS + part],
                own_sem.at[unit * PARTS + part],
                (credit_sem.at[slot * PARTS + part], unit >= depth),
                clear_sem.at[unit * PARTS + part],
            ),
            part * part_rows,
            part_rows,
            (credit_sem.at[slot * PARTS + part], after < steps),
        )

    misc_sum = Reduction(
        exchange,
        0,
        misc_buf,
        misc_ref,
        misc_slots,
        (
            out_copy_sem.at[depth * PARTS],
            back_copy_sem.at[steps * PARTS],
            own_sem.at[steps * PARTS],
            None,
            clear_sem.at[steps * PARTS],
        ),
        0,
        blocks * MISC,
    )

    def tick(step, point):
        for lag, part, k in due_steps(starts, point):
            unit = step - lag

            @pl.when(unit >= 0)
            def _(unit=unit, part=part, k=k):
                reduction(unit, part).step(k)

    def act_copies(step):
        slot = lax.rem(step, 2)
        at = steps - 1 - step
        return [
            pltpu.make_async_copy(ref.at[at], act_buf.at[slot, i], act_sem.at[slot, i])
            for i, ref in enumerate((hid_ref, tanh_ref, sig_ref))
        ]

    def weight_copies(step):
        slot = lax.rem(step, 2)
        block, layer = blocks - 1 - step // layers, layers - 1 - lax.rem(step, layers)
        conv = pltpu.make_async_copy(conv_w_ref.at[block, layer], conv_stage.at[slot], weight_sem.at[slot, 0])
        res = pltpu.make_async_copy(
            res_w_ref.at[block, jnp.minimum(layer, layers - 2)], res_stage.at[slot], weight_sem.at[slot, 1]
        )
        return [conv, res]

    def block_copies(block):
        return [
            pltpu.make_async_copy(ref.at[block], buf.at[block], block_sem.at[block, i])
            for i, (ref, buf) in enumerate(
                ((wn_ref, wn_buf), (scale_ref, scale_buf), (mixed_ref, mixed_buf), (x_ref, x_buf))
            )
        ]

    for block in reversed(range(blocks)):
        for copy in block_copies(block):
            copy.start()
    for copy in act_copies(0) + weight_copies(0):
        copy.start()

    barrier = pltpu.get_barrier_semaphore()
    for b in range(bits):
        pl.semaphore_signal(
            barrier, inc=1, device_id=exchange.partner((exchange.value[b], 2**b)), device_id_type=MESH
        )
    pl.semaphore_wait(barrier, bits)

    grad_flow[...] = grad_out_ref[0]
    misc_buf[...] = jnp.zeros_like(misc_buf)
    columns_buf[...] = jnp.zeros_like(columns_buf)
    for high, low, rows in ((stack_high, stack_low, deep), (gated_high, gated_low, hidden_size)):
        high[rows:, :] = jnp.ones((16, frames), bf16)
        low[rows:, :] = jnp.zeros((16, frames), bf16)

    def run_step(step, carry):
        block = blocks - 1 - step // layers
        layer = layers - 1 - lax.rem(step, layers)
        slot = lax.rem(step, 2)
        misc_at = block * MISC
        for copy in act_copies(step) + weight_copies(step):
            copy.wait()

        @pl.when(step + 1 < steps)
        def _():
            for copy in act_copies(step + 1) + weight_copies(step + 1):
                copy.start()

        tanh_part, sig_part = act_buf[slot, 1], act_buf[slot, 2]
        high, low = split(tanh_part * sig_part)
        gated_high[:hidden_size] = high
        gated_low[:hidden_size] = low

        @pl.when(layer == layers - 1)
        def _():
            for copy in block_copies(block):
                copy.wait()
            moved_grad = grad_flow[half:] * mask
            changed_grad = moved_grad * scale_buf[block]
            grad_changed[...] = changed_grad
            logs_grad = changed_grad * mixed_buf[block, half:] + (grad_det / length.astype(f32)) * mask
            out_grad = jnp.concatenate([moved_grad, logs_grad], axis=0)
            columns_buf[:channels, 0:1] = jnp.sum(out_grad, axis=1, keepdims=True)
            out_split = split(out_grad)
            end_grad = dot3(out_split, split(wn_buf[block]), NT)
            skip = dot3(split(end_w_ref[block]), out_split, TN) * mask
            columns_buf[:, 1:2] = jnp.sum(skip, axis=1, keepdims=True)
            skip_split = split(skip)
            pair_high[hidden_size:], pair_low[hidden_size:] = skip_split
            gated = (gated_high[:hidden_size], gated_low[:hidden_size])
            unit_buf[step, deep:, :hidden_size] = dot3(skip_split, gated, NT)
            unit_buf[step, deep : deep + channels, hidden_size:] = end_grad
            grad_gated[...] = dot3(split(last_w_ref[block]), skip_split, TN)
            grad_hid[...] = jnp.zeros_like(grad_hid)

        @pl.when(layer < layers - 1)
        def _():
            masked = grad_hid[...] * mask
            grad_hid[...] = masked
            pair_high[:hidden_size], pair_low[:hidden_size] = split(masked)
            pair = (pair_high[...], pair_low[...])
            grads = dot3((gated_high[...], gated_low[...]), pair, NT)
            unit_buf[step, deep:] = grads[:hidden_size]
            misc_buf[pl.ds(misc_at + half + 8 + layers + layer, 1), :] = grads[hidden_size : hidden_size + 1]
            grad_gated[...] = dot3(split(res_stage[slot]), pair)

        tick(step, 0)
        gated_grad = grad_gated[...]
        tanh_part, sig_part = act_buf[slot, 1], act_buf[slot, 2]
        inner = gated_grad * sig_part
        conv_grad = jnp.concatenate(
            [inner * (1.0 - tanh_part * tanh_part), inner * tanh_part * (1.0 - sig_part)], axis=0
        )
        fill_shifted(conv_grad, back_high, back_low, kernel, 1)
        fill_shifted(act_buf[slot, 0], stack_high, stack_low, kernel, -1)
        tick(step, 1)
        center = slice(middle * wide, (middle + 1) * wide)
        for part in range(PARTS):
            at = part * part_rows
            end = at + part_rows if part < PARTS - 1 else deep + 16
            grads = dot3((stack_high[at:end], stack_low[at:end]), (back_high[center], back_low[center]), NT)
            if part < PARTS - 1:
                unit_buf[step, at:end] = grads
            else:
                unit_buf[step, at:deep] = grads[: deep - at]
                misc_buf[pl.ds(misc_at + half + 8 + layer, 1), :] = grads[deep - at : deep - at + 1]
            tick(step, 2 + part)
        for k in range(kernel):
            high, low = split(conv_stage[slot, k * hidden_size : (k + 1) * hidden_size])
            turned_high[:, k * wide : (k + 1) * wide] = high
            turned_low[:, k * wide : (k + 1) * wide] = low
        grad_hid[...] += dot3((turned_high[...], turned_low[...]), (back_high[...], back_low[...]))

        @pl.when(layer == 0)
        def _():
            hid_grad = grad_hid[...] * mask
            hid_split = split(hid_grad)
            mixed = mixed_buf[block]
            start_grad = dot3(split(mixed[:half]), hid_split, NT)
            misc_buf[pl.ds(misc_at, half), :hidden_size] = start_grad
            columns_buf[:, 2:3] = jnp.sum(hid_grad, axis=1, keepdims=True)
            passed_grad = grad_flow[:half] + dot3(split(start_w_ref[block]), hid_split)
            mixed_grad = split(jnp.concatenate([passed_grad, grad_changed[...]], axis=0))
            norm_b = jnp.transpose(jnp.broadcast_to(norm_bias_ref[pl.ds(block, 1), :], (8, channels)))[:, 0:1]
            norm_s = jnp.exp(jnp.transpose(jnp.broadcast_to(norm_logs_ref[pl.ds(block, 1), :], (8, channels)))[:, 0:1])
            scaled = norm_s * x_buf[block]
            normed = (norm_b + scaled) * mask
            mix_grad = dot3(mixed_grad, split(normed), NT)
            normed_grad = dot3(split(mix_matrix(mix_ref, block, channels)), mixed_grad, TN) * mask
            columns_buf[:channels, 3:4] = jnp.sum(normed_grad, axis=1, keepdims=True)
            columns_buf[:channels, 4:5] = jnp.sum(normed_grad * scaled, axis=1, keepdims=True) + grad_det
            grad_flow[...] = normed_grad * norm_s
            rows = columns_buf[...].T
            misc_buf[pl.ds(misc_at + half, 8), :hidden_size] = rows[:8]
            inverse, _ = inverse_logdet(mix_ref, block)
            misc_buf[pl.ds(misc_at + half + 16, 8), :] = mix_rows(
                mix_grad, inverse, grad_det * (channels // 4), wide
            )

        tick(step, POINTS - 1)
        return carry

    lax.fori_loop(0, steps, run_step, 0)
    grad_in_ref[0] = grad_flow[...]
    for unit, part, k in order:
        (misc_sum if unit == steps else reduction(unit, part)).step(k)
    misc_sum.out().wait()

    def end_outs(unit, carry):
        for part in range(PARTS):
            reduction(unit, part).out().wait()
        return carry

    lax.fori_loop(0, steps, end_outs, 0)


def mix_rows(products, inverse, factor, wide):
    channels = products.shape[0]
    half = channels // 2
    rows = lax.broadcasted_iota(jnp.int32, (channels, channels), 0)
    cols = lax.broadcasted_iota(jnp.int32, (channels, channels), 1)
    row_top, col_top = rows < half, cols < half
    row_in = jnp.where(row_top, rows, rows - half)
    col_in = jnp.where(col_top, cols, cols - half)
    row_member = jnp.where(row_top, 0, 2) + (row_in & 1)
    col_member = jnp.where(col_top, 0, 2) + (col_in & 1)
    same = (row_in >> 1) == (col_in >> 1)
    kept = jnp.where(same, products, 0.0)
    row = lax.broadcasted_iota(jnp.int32, (8, wide), 0)
    lane = lax.broadcasted_iota(jnp.int32, (8, wide), 1)
    result = jnp.zeros((8, wide), f32)
    for i in range(4):
        mine = jnp.where(row_member == i, kept, 0.0)
        for j in range(4):
            picked = jnp.where(col_member == j, mine, 0.0)
            total = jnp.sum(jnp.sum(picked, axis=0, keepdims=True), axis=1, keepdims=True)
            total = total + factor * inverse[j][i][0:1, 0:1]
            result = jnp.where((row == i) & (lane == j), total, result)
    return result


def finish_kernel(
    sizes,
    units_ref,
    misc_ref,
    grad_in_ref,
    grad_in_out,
    norm_b_out,
    norm_l_out,
    mix_out,
    start_w_out,
    start_b_out,
    conv_w_out,
    conv_b_out,
    res_w_out,
    res_b_out,
    last_w_out,
    last_b_out,
    end_w_out,
    end_b_out,
    units_buf,
    grad_in_buf,
    sems,
):
    blocks, layers, kernel, hidden_size, channels, frames = sizes
    half = channels // 2
    deep = kernel * hidden_size
    steps = blocks * layers
    loads = [pltpu.make_async_copy(units_ref.at[i], units_buf.at[i], sems.at[0, i]) for i in range(steps)]
    loads.append(pltpu.make_async_copy(grad_in_ref, grad_in_buf, sems.at[0, steps]))
    for load in loads:
        load.start()
    stores = []
    for i in range(steps):
        loads[i].wait()
        b, layer = i // layers, i % layers
        stores.append(pltpu.make_async_copy(units_buf.at[i, :deep], conv_w_out.at[b, layer], sems.at[1, i]))
        if layer < layers - 1:
            stores[-1].start()
            stores.append(pltpu.make_async_copy(units_buf.at[i, deep:], res_w_out.at[b, layer], sems.at[2, i]))
        stores[-1].start()
    loads[steps].wait()
    stores.append(pltpu.make_async_copy(grad_in_buf, grad_in_out, sems.at[1, steps]))
    stores[-1].start()
    for b in range(blocks):
        at = b * MISC
        start_w_out[b] = misc_ref[at : at + half, :hidden_size]
        at += half
        for row, (out, width) in enumerate(
            ((end_b_out, channels), (last_b_out, hidden_size), (start_b_out, hidden_size), (norm_b_out, channels), (norm_l_out, channels))
        ):
            out[b : b + 1, :] = misc_ref[at + row : at + row + 1, :width]
        conv_b_out[b] = misc_ref[at + 8 : at + 8 + layers]
        for layer in range(layers - 1):
            res_b_out[layer, b : b + 1, :] = misc_ref[at + 8 + layers + layer : at + 9 + layers + layer]
        mix_out[b] = misc_ref[at + 16 : at + 20, :4]
    for b in range(blocks):
        tail = units_buf[(b + 1) * layers - 1, deep:]
        last_w_out[b] = tail[:, :hidden_size]
        end_w_out[b] = tail[:channels, hidden_size:]
    for store in stores:
        store.wait()


def finish_call(sizes, grad_in, units, misc):
    blocks, layers, kernel, hidden_size, channels, frames = sizes
    half, deep, wide = channels // 2, kernel * hidden_size, 2 * hidden_size
    vmem = pl.BlockSpec(memory_space=pltpu.VMEM)
    hbm = pl.BlockSpec(memory_space=pl.ANY)
    dims = [
        (1, channels, frames),
        (blocks, channels),
        (blocks, channels),
        (blocks, 4, 4),
        (blocks, half, hidden_size),
        (blocks, hidden_size),
        (blocks, layers, deep, wide),
        (blocks, layers, wide),
        (blocks, layers - 1, hidden_size, wide),
        (layers - 1, blocks, wide),
        (blocks, hidden_size, hidden_size),
        (blocks, hidden_size),
        (blocks, channels, hidden_size),
        (blocks, channels),
    ]
    large = (0, 6, 8)
    return pl.pallas_call(
        functools.partial(finish_kernel, sizes),
        name="flow_finish",
        out_shape=[jax.ShapeDtypeStruct(d, f32) for d in dims],
        in_specs=[hbm, vmem, hbm],
        out_specs=[hbm if i in large else vmem for i in range(len(dims))],
        scratch_shapes=[
            pltpu.VMEM((blocks * layers, deep + hidden_size, wide), f32),
            pltpu.VMEM((1, channels, frames), f32),
            pltpu.SemaphoreType.DMA((3, blocks * layers + 1)),
        ],
        compiler_params=pltpu.CompilerParams(vmem_limit_bytes=VMEM_LIMIT),
    )(units, misc, grad_in)


def backward_call(count, lengths, grad_det, grad_out, params, saved):
    (norm_bias, norm_logs, mix, start_w, _, conv_w, _, res_w, _, last_w, _, end_w, _) = params
    hid, tanh_all, sig_all, mixed, wn, scale, x_all = saved
    _, channels, frames = grad_out.shape
    conv_w, res_w, start_w = conv_w.swapaxes(2, 3), res_w.swapaxes(2, 3), start_w.swapaxes(1, 2)
    blocks, layers, deep, wide = conv_w.shape
    hidden_size = wide // 2
    kernel = deep // hidden_size
    half = channels // 2
    steps = blocks * layers
    sizes = (blocks, layers, kernel, hidden_size, channels, frames)
    bits = count.bit_length() - 1
    halvings = 4
    depth = 3
    rows = deep + hidden_size
    part_rows = rows // PARTS
    vmem = pl.BlockSpec(memory_space=pltpu.VMEM)
    smem = pl.BlockSpec(memory_space=pltpu.SMEM)
    hbm = pl.BlockSpec(memory_space=pl.ANY)
    shape = jax.ShapeDtypeStruct
    shares = [2 ** -min(hop + 1, halvings) for hop in range(bits)]
    hops = bits + halvings
    starts = [
        row if len(row) == hops + 1 else [ready + 2 * k for k in range(hops + 1)]
        for row, ready in zip(STARTS, READY)
    ]
    order = drain_order(starts, bits, halvings, depth, steps, part_rows, blocks * MISC)
    return pl.pallas_call(
        functools.partial(backward_kernel, sizes, bits, halvings, depth, starts, order),
        name="flow_backward",
        out_shape=[
            shape((1, channels, frames), f32),
            shape((steps, rows, wide), f32),
            shape((blocks * MISC, wide), f32),
        ],
        in_specs=[smem, smem, smem] + [vmem] * 6 + [hbm] * 9,
        out_specs=[vmem, hbm, hbm],
        scratch_shapes=[
            pltpu.VMEM((steps, rows, wide), f32),
            pltpu.VMEM((blocks * MISC, wide), f32),
            pltpu.VMEM((2, 3, hidden_size, frames), f32),
            pltpu.VMEM((blocks, channels, frames), f32),
            pltpu.VMEM((blocks, hidden_size, frames), f32),
            pltpu.VMEM((blocks, half, frames), f32),
            pltpu.VMEM((blocks, channels, frames), f32),
            pltpu.VMEM((2, deep, wide), f32),
            pltpu.VMEM((2, hidden_size, wide), f32),
            pltpu.VMEM((deep + 16, frames), bf16),
            pltpu.VMEM((deep + 16, frames), bf16),
            pltpu.VMEM((kernel * wide, frames), bf16),
            pltpu.VMEM((kernel * wide, frames), bf16),
            pltpu.VMEM((hidden_size, kernel * wide), bf16),
            pltpu.VMEM((hidden_size, kernel * wide), bf16),
            pltpu.VMEM((hidden_size + 16, frames), bf16),
            pltpu.VMEM((hidden_size + 16, frames), bf16),
            pltpu.VMEM((wide, frames), bf16),
            pltpu.VMEM((wide, frames), bf16),
            pltpu.VMEM((hidden_size, frames), f32),
            pltpu.VMEM((hidden_size, frames), f32),
            pltpu.VMEM((hidden_size, frames), f32),
            pltpu.VMEM((channels, frames), f32),
            pltpu.VMEM((half, frames), f32),
            pltpu.VMEM((hidden_size, 128), f32),
            pltpu.SemaphoreType.DMA((2, 3)),
            pltpu.SemaphoreType.DMA((2, 2)),
            pltpu.SemaphoreType.DMA((blocks, 4)),
            pltpu.SemaphoreType.DMA((depth * PARTS + 1, 2, bits)),
            pltpu.SemaphoreType.DMA((steps * PARTS + 1, 2, halvings)),
            pltpu.SemaphoreType.DMA((steps * PARTS + 1,)),
            pltpu.SemaphoreType.REGULAR((depth * PARTS, bits)),
            pltpu.SemaphoreType.REGULAR((steps * PARTS + 1, halvings)),
        ]
        + [pltpu.VMEM((depth, PARTS, int(part_rows * s), wide), f32) for s in shares]
        + [pltpu.VMEM((int(blocks * MISC * s), wide), f32) for s in shares],
        compiler_params=pltpu.CompilerParams(
            collective_id=0, has_side_effects=True, vmem_limit_bytes=VMEM_LIMIT
        ),
    )(lengths, grad_det, mix, grad_out, norm_bias, norm_logs, start_w, last_w, end_w, conv_w, res_w,
      hid, tanh_all, sig_all, mixed, wn, scale, x_all)


def shards(mesh_size, mel, lengths, *rest):
    params, grad_out, grad_det = rest[:13], rest[13], rest[14]
    flowed, logdet, *saved = forward_call(mel, lengths, params)
    blocks, layers, wide, deep = params[5].shape
    hidden_size = wide // 2
    sizes = (blocks, layers, deep // hidden_size, hidden_size, mel.shape[1], mel.shape[2])
    summed = backward_call(mesh_size, lengths, grad_det, grad_out, params, saved)
    grads = list(finish_call(sizes, *summed))
    for i in (6, 8):
        grads[i] = grads[i].swapaxes(2, 3)
    grads[4] = grads[4].swapaxes(1, 2)
    grads[9] = grads[9].swapaxes(0, 1)
    return (flowed, logdet[0, :1], *grads)


def solution(mesh):
    split_first, whole = P("dp", None, None), P()
    in_specs = (split_first, P("dp")) + (whole,) * 13 + (split_first, P("dp"))
    out_specs = (split_first, P("dp"), split_first) + (whole,) * 13
    return jax.shard_map(
        functools.partial(shards, mesh.shape["dp"]),
        mesh=mesh,
        in_specs=in_specs,
        out_specs=out_specs,
        check_vma=False,
    )
```

```python
import functools

import jax
import jax.numpy as jnp
from jax import lax
from jax.experimental import pallas as pl
from jax.experimental.pallas import tpu as pltpu
from jax.sharding import PartitionSpec as P

f32, bf16 = jnp.float32, jnp.bfloat16
NN = (((1,), (0,)), ((), ()))
NT = (((1,), (1,)), ((), ()))
TN = (((0,), (0,)), ((), ()))
VMEM_LIMIT = 60 * 2**20


def dot(left, right, form=NN):
    return lax.dot_general(left, right, form, preferred_element_type=f32)


def split(value):
    high = value.astype(bf16)
    return high, (value - high.astype(f32)).astype(bf16)


def dot3(left, right, form=NN):
    (left_high, left_low), (right_high, right_low) = left, right
    return (
        dot(left_high, right_high, form)
        + dot(left_high, right_low, form)
        + dot(left_low, right_high, form)
    )


def mix_matrix(mix_ref, block, channels):
    half = channels // 2
    rows = lax.broadcasted_iota(jnp.int32, (channels, channels), 0)
    cols = lax.broadcasted_iota(jnp.int32, (channels, channels), 1)
    row_top, col_top = rows < half, cols < half
    row_in = jnp.where(row_top, rows, rows - half)
    col_in = jnp.where(col_top, cols, cols - half)
    row_member = jnp.where(row_top, 0, 2) + (row_in & 1)
    col_member = jnp.where(col_top, 0, 2) + (col_in & 1)
    same = (row_in >> 1) == (col_in >> 1)
    pair = row_member * 4 + col_member
    result = jnp.zeros((channels, channels), f32)
    for i in range(4):
        for j in range(4):
            result = jnp.where(pair == 4 * i + j, mix_ref[block, i, j], result)
    return jnp.where(same, result, 0.0)


def inverse_logdet(mix_ref, block):
    shape = (8, 128)
    left = [[jnp.full(shape, mix_ref[block, i, j], f32) for j in range(4)] for i in range(4)]
    right = [[jnp.full(shape, float(i == j), f32) for j in range(4)] for i in range(4)]
    log_total = jnp.zeros(shape, f32)
    for k in range(4):
        pivot = left[k][k]
        log_total = log_total + jnp.log(pivot)
        left[k] = [v / pivot for v in left[k]]
        right[k] = [v / pivot for v in right[k]]
        for i in range(4):
            if i != k:
                factor = left[i][k]
                left[i] = [v - factor * w for v, w in zip(left[i], left[k])]
                right[i] = [v - factor * w for v, w in zip(right[i], right[k])]
    return right, log_total


def fill_columns(rows_ref, cols_ref, block, vectors):
    rows_ref[...] = jnp.zeros_like(rows_ref)
    for j, vector in enumerate(vectors):
        rows_ref[j : j + 1, : vector.shape[1]] = vector
    cols_ref[...] = rows_ref[...].T


def frame_mask(length, frames):
    return (lax.broadcasted_iota(jnp.int32, (1, frames), 1) < length).astype(f32)


ROWS = 16


def chunks(rows, size=ROWS):
    return [slice(at, min(at + size, rows)) for at in range(0, rows, size)]


def shift_by(at, by):
    return slice(at.start + by, at.stop + by)


def fill_rows(value, at, high_ref, low_ref, kernel, channels, sign):
    high, low = split(value)
    for k in range(kernel):
        move = (sign * (k - kernel // 2)) % value.shape[1]
        to = shift_by(at, k * channels)
        high_ref[to] = pltpu.roll(high, move, 1) if move else high
        low_ref[to] = pltpu.roll(low, move, 1) if move else low


def fill_split(source, high_ref, low_ref, size=64):
    for at in chunks(source.shape[0], size):
        high_ref[at], low_ref[at] = split(source[at])


def forward_kernel(
    sizes,
    length_ref,
    mix_ref,
    x_ref,
    norm_bias_ref,
    norm_logs_ref,
    start_w_ref,
    start_b_ref,
    conv_w_ref,
    conv_b_ref,
    res_w_ref,
    res_b_ref,
    last_w_ref,
    last_b_ref,
    end_w_ref,
    end_b_ref,
    flowed_ref,
    logdet_ref,
    hid_out,
    tanh_out,
    sig_out,
    mixed_out,
    wn_out,
    scale_out,
    x_out,
    x_buf,
    hid_buf,
    tanh_buf,
    sig_buf,
    mixed_buf,
    wn_buf,
    scale_buf,
    conv_stage,
    res_stage,
    stack_high,
    stack_low,
    conv_high,
    conv_low,
    res_high,
    res_low,
    gated_high,
    gated_low,
    out_buf,
    skip_buf,
    det_buf,
    rows_buf,
    cols_buf,
    in_sem,
    out_sem,
    misc_sem,
):
    blocks, layers, kernel, hidden_size, channels, frames = sizes
    half = channels // 2
    steps = blocks * layers
    length = length_ref[0]
    mask = frame_mask(length, frames)

    def conv_copy(block, layer):
        at = block * layers + layer
        return pltpu.make_async_copy(conv_w_ref.at[block, layer], conv_stage.at[at], in_sem.at[0, at])

    def res_copy(block, layer):
        at = block * layers + layer
        return pltpu.make_async_copy(res_w_ref.at[block, layer], res_stage.at[at], in_sem.at[1, at])

    def saves(step):
        return [
            pltpu.make_async_copy(buf.at[step], out.at[step], out_sem.at[i, step])
            for i, (buf, out) in enumerate(
                ((hid_buf, hid_out), (tanh_buf, tanh_out), (sig_buf, sig_out))
            )
        ]

    def block_saves(block):
        return [
            pltpu.make_async_copy(buf.at[block], out.at[block], misc_sem.at[i, block])
            for i, (buf, out) in enumerate(
                ((mixed_buf, mixed_out), (x_buf, x_out), (wn_buf, wn_out), (scale_buf, scale_out))
            )
        ]

    for block in range(blocks):
        for layer in range(layers):
            conv_copy(block, layer).start()
            if layer < layers - 1:
                res_copy(block, layer).start()
    x_buf[0] = x_ref[0]
    det_buf[...] = jnp.zeros_like(det_buf)

    def run_block(block, carry):
        fill_columns(
            rows_buf,
            cols_buf,
            block,
            [conv_b_ref[block, pl.ds(l, 1), :] for l in range(layers)]
            + [res_b_ref[l, pl.ds(block, 1), :] for l in range(layers - 1)]
            + [
                r[pl.ds(block, 1), :]
                for r in (start_b_ref, last_b_ref, end_b_ref, norm_bias_ref, norm_logs_ref)
            ],
        )
        base = 2 * layers - 1
        start_b = cols_buf[:hidden_size, base : base + 1]
        last_b = cols_buf[:hidden_size, base + 1 : base + 2]
        end_b = cols_buf[:channels, base + 2 : base + 3]
        norm_b = cols_buf[:channels, base + 3 : base + 4]
        norm_l = cols_buf[:channels, base + 4 : base + 5]
        normed = (norm_b + jnp.exp(norm_l) * x_buf[block]) * mask
        mixed = dot3(split(mix_matrix(mix_ref, block, channels)), split(normed))
        mixed_buf[block] = mixed
        for save in block_saves(block)[:2]:
            save.start()
        hidden = (dot3(split(start_w_ref[block]), split(mixed[:half]), TN) + start_b) * mask
        hid_buf[block * layers] = hidden

        for layer in range(layers):
            step = block * layers + layer
            last = layer == layers - 1
            saves(step)[0].start()
            conv_copy(block, layer).wait()
            if not last:
                res_copy(block, layer).wait()
            fill_split(conv_stage.at[step], conv_high, conv_low)
            for at in chunks(hidden_size):
                fill_rows(hid_buf[step, at], at, stack_high, stack_low, kernel, hidden_size, -1)
            if not last:
                fill_split(res_stage.at[step], res_high, res_low)
            out_buf[...] = dot3((conv_high[...], conv_low[...]), (stack_high[...], stack_low[...]), TN)
            for at in chunks(hidden_size):
                below = shift_by(at, hidden_size)
                tanh_part = jnp.tanh(out_buf[at] + cols_buf[at, layer : layer + 1])
                sig_part = 0.5 * jnp.tanh(0.5 * (out_buf[below] + cols_buf[below, layer : layer + 1])) + 0.5
                tanh_buf[step, at] = tanh_part
                sig_buf[step, at] = sig_part
                gated_high[at], gated_low[at] = split(tanh_part * sig_part)
            gated = (gated_high[...], gated_low[...])
            if last:
                skip_buf[...] += dot3(split(last_w_ref[block]), gated)
            else:
                out_buf[...] = dot3((res_high[...], res_low[...]), gated, TN)
                bias = slice(layers + layer, layers + layer + 1)
                for at in chunks(hidden_size):
                    below = shift_by(at, hidden_size)
                    res = out_buf[below] + cols_buf[below, bias]
                    skip_buf[at] = res + (skip_buf[at] if layer else last_b[at])
                    hid_buf[step + 1, at] = (hid_buf[step, at] + (out_buf[at] + cols_buf[at, bias])) * mask
            for save in saves(step)[1:]:
                save.start()
        wavenet = skip_buf[...] * mask
        wn_buf[block] = wavenet
        out = dot3(split(end_w_ref[block]), split(wavenet)) + end_b
        scale = jnp.exp(out[half:])
        scale_buf[block] = scale
        mixed = mixed_buf[block]
        moved = (out[:half] + scale * mixed[half:]) * mask
        _, log_det = inverse_logdet(mix_ref, block)
        det_buf[0:1, :] += jnp.sum(norm_l) + log_det[0:1, :] * (channels // 4)
        det_buf[1:2, :] += jnp.full((1, 128), jnp.sum(out[half:] * mask))
        x_buf[block + 1, :half] = mixed[:half]
        x_buf[block + 1, half:] = moved
        for save in block_saves(block)[2:]:
            save.start()
        return carry

    lax.fori_loop(0, blocks, run_block, 0)
    flowed_ref[0] = x_buf[blocks]
    logdet_ref[...] = det_buf[0:1, :] + det_buf[1:2, :] / length.astype(f32)

    def finish(step, carry):
        for save in saves(step):
            save.wait()
        return carry

    lax.fori_loop(0, steps, finish, 0)

    def finish_block(block, carry):
        for save in block_saves(block):
            save.wait()
        return carry

    lax.fori_loop(0, blocks, finish_block, 0)


def forward_call(mel, lengths, params):
    (norm_bias, norm_logs, mix, start_w, start_b, conv_w, conv_b, res_w, res_b, last_w, last_b, end_w, end_b) = params
    _, channels, frames = mel.shape
    conv_w, res_w = conv_w.swapaxes(2, 3), res_w.swapaxes(2, 3)
    start_w, res_b = start_w.swapaxes(1, 2), res_b.swapaxes(0, 1)
    blocks, layers, deep, wide = conv_w.shape
    hidden_size = wide // 2
    kernel = deep // hidden_size
    half = channels // 2
    steps = blocks * layers
    sizes = (blocks, layers, kernel, hidden_size, channels, frames)
    vmem = pl.BlockSpec(memory_space=pltpu.VMEM)
    smem = pl.BlockSpec(memory_space=pltpu.SMEM)
    hbm = pl.BlockSpec(memory_space=pl.ANY)
    shape = jax.ShapeDtypeStruct
    act = (steps, hidden_size, frames)
    return pl.pallas_call(
        functools.partial(forward_kernel, sizes),
        name="flow_forward",
        out_shape=[
            shape((1, channels, frames), f32),
            shape((1, 128), f32),
            shape(act, f32),
            shape(act, f32),
            shape(act, f32),
            shape((blocks, channels, frames), f32),
            shape((blocks, hidden_size, frames), f32),
            shape((blocks, half, frames), f32),
            shape((blocks, channels, frames), f32),
        ],
        in_specs=[smem, smem, vmem, vmem, vmem, vmem, vmem, hbm, vmem, hbm, vmem, vmem, vmem, vmem, vmem],
        out_specs=[vmem, vmem] + [hbm] * 7,
        scratch_shapes=[
            pltpu.VMEM((blocks + 1, channels, frames), f32),
            pltpu.VMEM(act, f32),
            pltpu.VMEM(act, f32),
            pltpu.VMEM(act, f32),
            pltpu.VMEM((blocks, channels, frames), f32),
            pltpu.VMEM((blocks, hidden_size, frames), f32),
            pltpu.VMEM((blocks, half, frames), f32),
            pltpu.VMEM((steps, deep, wide), f32),
            pltpu.VMEM((steps, hidden_size, wide), f32),
            pltpu.VMEM((deep, frames), bf16),
            pltpu.VMEM((deep, frames), bf16),
            pltpu.VMEM((deep, wide), bf16),
            pltpu.VMEM((deep, wide), bf16),
            pltpu.VMEM((hidden_size, wide), bf16),
            pltpu.VMEM((hidden_size, wide), bf16),
            pltpu.VMEM((hidden_size, frames), bf16),
            pltpu.VMEM((hidden_size, frames), bf16),
            pltpu.VMEM((wide, frames), f32),
            pltpu.VMEM((hidden_size, frames), f32),
            pltpu.VMEM((8, 128), f32),
            pltpu.VMEM((16, wide), f32),
            pltpu.VMEM((wide, 16), f32),
            pltpu.SemaphoreType.DMA((2, steps)),
            pltpu.SemaphoreType.DMA((3, steps)),
            pltpu.SemaphoreType.DMA((4, blocks)),
        ],
        compiler_params=pltpu.CompilerParams(vmem_limit_bytes=VMEM_LIMIT),
    )(lengths, mix, mel, norm_bias, norm_logs, start_w, start_b, conv_w, conv_b, res_w, res_b, last_w, last_b, end_w, end_b)
MESH = pl.DeviceIdType.MESH
MISC = 128
SUM_LIMIT = 47 * 2**20
PARTS = 3
POINTS = 6
READY = (2, 3, 4)
STARTS = ((2, 4, 6, 10, 15, 21, 24, 29, 34, 36), (3, 4, 7, 10, 13, 17, 23, 26, 29, 31), (4, 5, 9, 11, 14, 19, 21, 25, 31, 34))


POINT_US = (2.2, 1.0, 1.1, 1.1, 1.1, 2.6)
RATES = {"x": 58.6, "y": 58.6, "z": 61.8, "middle": 55.3}
CORE_ROWS = 420.0
LATENCY = {"core": 0.75, "far": 2.6}


class Link:
    def __init__(self, rate):
        self.queues, self.clock, self.rate = ([], []), 0.0, rate

    def run(self, until):
        while any(self.queues) and self.clock < until:
            heads = [queue[0] for queue in self.queues if queue]
            rate = self.rate / len(heads)
            spent = min(min(head[0] for head in heads) / rate, until - self.clock)
            self.clock += spent
            for queue in self.queues:
                if queue:
                    queue[0][0] -= spent * rate
                    if queue[0][0] < 1e-6:
                        queue.pop(0)[1] = self.clock
        if self.clock < until < float("inf"):
            self.clock = until

    def add(self, now, core, rows):
        self.run(now)
        job = [rows, None]
        self.queues[core].append(job)
        return self, job


class Plan:
    def __init__(self, bits, halvings, steps, part_rows, misc_rows):
        self.bits, self.hops, self.steps = bits, bits + halvings, steps
        self.rows = (part_rows, misc_rows)
        self.links = {name: Link(rate) for name, rate in RATES.items()}
        self.links |= {("core", core): Link(CORE_ROWS) for core in range(2)}
        self.clock, self.jobs, self.taken = 0.0, {}, {}
        sizes = [2 ** -(h + 1) for h in range(halvings)]
        self.sizes = sizes + [sizes[-1]] * (bits - halvings) + sizes[::-1]

    def name(self, part, k):
        near = ("z", "a", "b") if part == PARTS - 1 else ("a", "b", "z")
        return ["core", *near, *["far"] * (self.bits - 4), *reversed(near), "core"][k]

    def start(self, unit, part, k):
        name, jobs = self.name(part, k), []
        rows = self.sizes[k] * self.rows[unit == self.steps]
        for core in range(2):
            if name == "core":
                jobs.append(self.links[name, core].add(self.clock, core, rows))
                continue
            link = "z" if name in ("z", "far") else "xy"[(name == "b") ^ core]
            jobs.append(self.links[link].add(self.clock, core, rows))
            if name == "far":
                jobs.append(self.links["middle"].add(self.clock, core, 2 * rows))
        self.jobs[unit, part] = jobs, LATENCY.get(name, 2.1)

    def arrival(self, unit, part, until=float("inf")):
        if not self.taken.get((unit, part)):
            return 0.0
        jobs, latency = self.jobs[unit, part]
        for link, job in jobs:
            if job[1] is None:
                link.run(until)
            if job[1] is None:
                return float("inf")
        return max(job[1] for _, job in jobs) + latency

    def take(self, unit, part, k):
        if k:
            self.clock = max(self.clock, self.arrival(unit, part)) + 0.1
        self.taken[unit, part] = k + 1
        if k < self.hops:
            self.start(unit, part, k)


def drain_order(starts, bits, halvings, depth, steps, part_rows, misc_rows):
    plan = Plan(bits, halvings, steps, part_rows, misc_rows)
    for layer in range(steps):
        for point in range(POINTS):
            plan.clock += POINT_US[point]
            for lag, part, k in due_steps(starts, point):
                if layer >= lag:
                    plan.take(layer - lag, part, k)
    order, taken = [], plan.taken
    waiting = [(unit, part) for unit in range(steps) for part in range(PARTS)] + [(steps, 0)]
    waiting = [w for w in waiting if taken.get(w, 0) <= plan.hops]
    while waiting:
        ready = []
        for unit, part in waiting:
            k = taken.get((unit, part), 0)
            slot_free = unit in range(depth) or unit == steps or k >= bits or taken[unit - depth, part] > k + 1
            if slot_free and plan.arrival(unit, part, plan.clock) <= plan.clock:
                ready.append((k >= bits, unit, part, k))
        if not ready:
            plan.clock += 0.1
            continue
        _, unit, part, k = min(ready)
        plan.take(unit, part, k)
        order.append((unit, part, k))
        if k == plan.hops:
            waiting.remove((unit, part))
    return order


def due_steps(starts, point):
    due = [
        (start // POINTS, part, k)
        for part, row in enumerate(starts)
        for k, start in enumerate(row)
        if start % POINTS == point
    ]
    return sorted(due, key=lambda due: (-due[0], due[1], due[2]))


class Exchange:
    def __init__(self, bits, halvings):
        self.bits, self.halvings = bits, halvings
        self.hops = bits + halvings
        self.me = lax.axis_index("dp")
        self.value = [lax.rem(self.me // 2**b, 2) for b in range(bits)]

    def order(self, turn):
        pairs = [(self.value[b], 2**b) for b in range(self.bits)]

        def either(flag, yes, no):
            return tuple(flag * y + (1 - flag) * n for y, n in zip(yes, no))

        odd = self.value[0]
        first = either(odd, pairs[2], pairs[1])
        second = either(odd, pairs[1], pairs[2])
        return [
            pairs[0],
            either(turn, pairs[3], first),
            either(turn, first, second),
            either(turn, second, pairs[3]),
        ] + pairs[4:]

    def partner(self, hop):
        bit, stride = hop
        return (self.me + (1 - 2 * bit) * stride,)

    def spans(self, turn, rows):
        at, size, result = 0, rows, []
        for bit, _ in self.order(turn)[: self.halvings]:
            size //= 2
            result.append((at + bit * size, at + (1 - bit) * size, size))
            at = at + bit * size
        return result


class Reduction:
    def __init__(self, exchange, turn, source, slots, sems, base, rows, later=None):
        self.x, self.source = exchange, source
        self.slots, self.sems, self.base, self.rows, self.later = slots, sems, base, rows, later
        self.order = exchange.order(turn)
        self.spans = exchange.spans(turn, rows)

    def rows_of(self, at, size):
        return pl.ds(pl.multiple_of(self.base + at, 8), size)

    def copy_sem(self, side, hop):
        out, back = self.sems[0], self.sems[1]
        return out.at[side, hop] if hop < self.x.bits else back.at[side, hop - self.x.bits]

    def copy(self, hop):
        halvings, bits = self.x.halvings, self.x.bits
        if hop < bits:
            if hop < halvings:
                _, at, size = self.spans[hop]
            else:
                at, _, size = self.spans[-1]
            src = self.source.at[self.rows_of(at, size)]
            dst = self.slots[hop]
            to = self.order[hop]
        else:
            level = halvings - 1 - (hop - bits)
            at, _, size = self.spans[level]
            src = dst = self.source.at[self.rows_of(at, size)]
            to = self.order[level]
        return pltpu.make_async_remote_copy(
            src_ref=src,
            dst_ref=dst,
            send_sem=self.copy_sem(0, hop),
            recv_sem=self.copy_sem(1, hop),
            device_id=self.x.partner(to),
            device_id_type=MESH,
        )

    def step(self, k):
        x = self.x
        if k > 0:
            done = k - 1
            self.copy(done).wait()
            if done < x.bits:
                at, _, size = self.spans[min(done, x.halvings - 1)]
                where = self.rows_of(at, size)
                self.source[where] += self.slots[done][...]
                self.free(done)
            if done < x.halvings:
                pl.semaphore_signal(
                    self.sems[3].at[done], inc=1, device_id=x.partner(self.order[done]), device_id_type=MESH
                )
        if k < x.hops:
            if k < x.bits:
                self.wait_free(k)
            else:
                pl.semaphore_wait(self.sems[3].at[x.hops - 1 - k], 1)
            self.copy(k).start()

    def free(self, hop):
        if self.later is not None:
            credit, exists = self.later

            @pl.when(exists)
            def _():
                pl.semaphore_signal(
                    credit.at[hop],
                    inc=1,
                    device_id=self.x.partner(self.order[hop]),
                    device_id_type=MESH,
                )

    def wait_free(self, hop):
        credit, needed = self.sems[2] if self.sems[2] is not None else (None, None)
        if credit is not None:

            @pl.when(needed)
            def _():
                pl.semaphore_wait(credit.at[hop], 1)


def backward_kernel(
    sizes,
    bits,
    halvings,
    depth,
    starts,
    order,
    length_ref,
    grad_det_ref,
    mix_ref,
    grad_out_ref,
    norm_bias_ref,
    norm_logs_ref,
    start_w_ref,
    last_w_ref,
    end_w_ref,
    conv_w_ref,
    res_w_ref,
    hid_ref,
    tanh_ref,
    sig_ref,
    mixed_ref,
    wn_ref,
    scale_ref,
    x_ref,
    grad_in_ref,
    unit_buf,
    misc_buf,
    *scratch,
):
    (
        act_buf,
        mixed_buf,
        wn_buf,
        scale_buf,
        x_buf,
        conv_stage,
        res_stage,
        stack_high,
        stack_low,
        back_high,
        back_low,
        turned_high,
        turned_low,
        gated_high,
        gated_low,
        pair_high,
        pair_low,
        grad_skip,
        grad_hid,
        grad_gated,
        grad_flow,
        grad_changed,
        columns_buf,
        act_sem,
        weight_sem,
        block_sem,
        out_copy_sem,
        back_copy_sem,
        credit_sem,
        clear_sem,
    ) = scratch[:30]
    slot_bufs = scratch[30 : 30 + bits]
    misc_slots = scratch[30 + bits :]
    blocks, layers, kernel, hidden_size, channels, frames = sizes
    half = channels // 2
    steps = blocks * layers
    deep = kernel * hidden_size
    wide = 2 * hidden_size
    middle = kernel // 2
    length = length_ref[0]
    mask = frame_mask(length, frames)
    grad_det = grad_det_ref[0]
    exchange = Exchange(bits, halvings)

    part_rows = (deep + hidden_size) // PARTS

    def reduction(unit, part):
        slot = lax.rem(unit, depth)
        after = unit + depth
        return Reduction(
            exchange,
            int(part == PARTS - 1),
            unit_buf.at[unit],
            [b.at[slot, part] for b in slot_bufs],
            (
                out_copy_sem.at[slot * PARTS + part],
                back_copy_sem.at[unit * PARTS + part],
                (credit_sem.at[slot * PARTS + part], unit >= depth),
                clear_sem.at[unit * PARTS + part],
            ),
            part * part_rows,
            part_rows,
            (credit_sem.at[slot * PARTS + part], after < steps),
        )

    misc_sum = Reduction(
        exchange,
        0,
        misc_buf,
        misc_slots,
        (
            out_copy_sem.at[depth * PARTS],
            back_copy_sem.at[steps * PARTS],
            None,
            clear_sem.at[steps * PARTS],
        ),
        0,
        blocks * MISC,
    )

    def tick(step, point):
        for lag, part, k in due_steps(starts, point):
            unit = step - lag

            @pl.when(unit >= 0)
            def _(unit=unit, part=part, k=k):
                reduction(unit, part).step(k)

    def act_copies(step):
        slot = lax.rem(step, 2)
        at = steps - 1 - step
        return [
            pltpu.make_async_copy(ref.at[at], act_buf.at[slot, i], act_sem.at[slot, i])
            for i, ref in enumerate((hid_ref, tanh_ref, sig_ref))
        ]

    def weight_copies(step):
        slot = lax.rem(step, 2)
        block, layer = blocks - 1 - step // layers, layers - 1 - lax.rem(step, layers)
        conv = pltpu.make_async_copy(conv_w_ref.at[block, layer], conv_stage.at[slot], weight_sem.at[slot, 0])
        res = pltpu.make_async_copy(
            res_w_ref.at[block, jnp.minimum(layer, layers - 2)], res_stage.at[slot], weight_sem.at[slot, 1]
        )
        return [conv, res]

    def block_copies(block):
        return [
            pltpu.make_async_copy(ref.at[block], buf.at[block], block_sem.at[block, i])
            for i, (ref, buf) in enumerate(
                ((wn_ref, wn_buf), (scale_ref, scale_buf), (mixed_ref, mixed_buf), (x_ref, x_buf))
            )
        ]

    for block in reversed(range(blocks)):
        for copy in block_copies(block):
            copy.start()
    for copy in act_copies(0) + weight_copies(0):
        copy.start()

    barrier = pltpu.get_barrier_semaphore()
    for b in range(bits):
        pl.semaphore_signal(
            barrier, inc=1, device_id=exchange.partner((exchange.value[b], 2**b)), device_id_type=MESH
        )
    pl.semaphore_wait(barrier, bits)

    grad_flow[...] = grad_out_ref[0]
    misc_buf[...] = jnp.zeros_like(misc_buf)
    columns_buf[...] = jnp.zeros_like(columns_buf)
    for high, low, rows in ((stack_high, stack_low, deep), (gated_high, gated_low, hidden_size)):
        high[rows:, :] = jnp.ones((16, frames), bf16)
        low[rows:, :] = jnp.zeros((16, frames), bf16)

    def run_step(step, carry):
        block = blocks - 1 - step // layers
        layer = layers - 1 - lax.rem(step, layers)
        slot = lax.rem(step, 2)
        misc_at = block * MISC
        for copy in act_copies(step) + weight_copies(step):
            copy.wait()

        @pl.when(step + 1 < steps)
        def _():
            for copy in act_copies(step + 1) + weight_copies(step + 1):
                copy.start()

        for at in chunks(hidden_size):
            gated_high[at], gated_low[at] = split(act_buf[slot, 1, at] * act_buf[slot, 2, at])

        @pl.when(layer == layers - 1)
        def _():
            for copy in block_copies(block):
                copy.wait()
            moved_grad = grad_flow[half:] * mask
            changed_grad = moved_grad * scale_buf[block]
            grad_changed[...] = changed_grad
            logs_grad = changed_grad * mixed_buf[block, half:] + (grad_det / length.astype(f32)) * mask
            out_grad = jnp.concatenate([moved_grad, logs_grad], axis=0)
            columns_buf[:channels, 0:1] = jnp.sum(out_grad, axis=1, keepdims=True)
            out_split = split(out_grad)
            end_grad = dot3(out_split, split(wn_buf[block]), NT)
            skip = dot3(split(end_w_ref[block]), out_split, TN) * mask
            columns_buf[:, 1:2] = jnp.sum(skip, axis=1, keepdims=True)
            skip_split = split(skip)
            pair_high[hidden_size:], pair_low[hidden_size:] = skip_split
            gated = (gated_high[:hidden_size], gated_low[:hidden_size])
            unit_buf[step, deep:, :hidden_size] = dot3(skip_split, gated, NT)
            unit_buf[step, deep : deep + channels, hidden_size:] = end_grad
            grad_gated[...] = dot3(split(last_w_ref[block]), skip_split, TN)
            grad_hid[...] = jnp.zeros_like(grad_hid)

        @pl.when(layer < layers - 1)
        def _():
            masked = grad_hid[...] * mask
            grad_hid[...] = masked
            pair_high[:hidden_size], pair_low[:hidden_size] = split(masked)
            pair = (pair_high[...], pair_low[...])
            grads = dot3((gated_high[...], gated_low[...]), pair, NT)
            unit_buf[step, deep:] = grads[:hidden_size]
            misc_buf[pl.ds(misc_at + half + 8 + layers + layer, 1), :] = grads[hidden_size : hidden_size + 1]
            grad_gated[...] = dot3(split(res_stage[slot]), pair)

        tick(step, 0)
        for at in chunks(hidden_size):
            tanh_part, sig_part = act_buf[slot, 1, at], act_buf[slot, 2, at]
            inner = grad_gated[at] * sig_part
            fill_rows(inner * (1.0 - tanh_part * tanh_part), at, back_high, back_low, kernel, wide, 1)
            below = shift_by(at, hidden_size)
            fill_rows(inner * tanh_part * (1.0 - sig_part), below, back_high, back_low, kernel, wide, 1)
            fill_rows(act_buf[slot, 0, at], at, stack_high, stack_low, kernel, hidden_size, -1)
        tick(step, 1)
        center = slice(middle * wide, (middle + 1) * wide)
        for part in range(PARTS):
            at = part * part_rows
            end = at + part_rows if part < PARTS - 1 else deep + 16
            grads = dot3((stack_high[at:end], stack_low[at:end]), (back_high[center], back_low[center]), NT)
            if part < PARTS - 1:
                unit_buf[step, at:end] = grads
            else:
                unit_buf[step, at:deep] = grads[: deep - at]
                misc_buf[pl.ds(misc_at + half + 8 + layer, 1), :] = grads[deep - at : deep - at + 1]
            tick(step, 2 + part)
        for k in range(kernel):
            high, low = split(conv_stage[slot, k * hidden_size : (k + 1) * hidden_size])
            turned_high[:, k * wide : (k + 1) * wide] = high
            turned_low[:, k * wide : (k + 1) * wide] = low
        grad_hid[...] += dot3((turned_high[...], turned_low[...]), (back_high[...], back_low[...]))

        @pl.when(layer == 0)
        def _():
            hid_grad = grad_hid[...] * mask
            hid_split = split(hid_grad)
            mixed = mixed_buf[block]
            start_grad = dot3(split(mixed[:half]), hid_split, NT)
            misc_buf[pl.ds(misc_at, half), :hidden_size] = start_grad
            columns_buf[:, 2:3] = jnp.sum(hid_grad, axis=1, keepdims=True)
            passed_grad = grad_flow[:half] + dot3(split(start_w_ref[block]), hid_split)
            mixed_grad = split(jnp.concatenate([passed_grad, grad_changed[...]], axis=0))
            norm_b = jnp.transpose(jnp.broadcast_to(norm_bias_ref[pl.ds(block, 1), :], (8, channels)))[:, 0:1]
            norm_s = jnp.exp(jnp.transpose(jnp.broadcast_to(norm_logs_ref[pl.ds(block, 1), :], (8, channels)))[:, 0:1])
            scaled = norm_s * x_buf[block]
            normed = (norm_b + scaled) * mask
            mix_grad = dot3(mixed_grad, split(normed), NT)
            normed_grad = dot3(split(mix_matrix(mix_ref, block, channels)), mixed_grad, TN) * mask
            columns_buf[:channels, 3:4] = jnp.sum(normed_grad, axis=1, keepdims=True)
            columns_buf[:channels, 4:5] = jnp.sum(normed_grad * scaled, axis=1, keepdims=True) + grad_det
            grad_flow[...] = normed_grad * norm_s
            rows = columns_buf[...].T
            misc_buf[pl.ds(misc_at + half, 8), :hidden_size] = rows[:8]
            inverse, _ = inverse_logdet(mix_ref, block)
            misc_buf[pl.ds(misc_at + half + 16, 8), :] = mix_rows(
                mix_grad, inverse, grad_det * (channels // 4), wide
            )

        tick(step, POINTS - 1)
        return carry

    lax.fori_loop(0, steps, run_step, 0)
    grad_in_ref[0] = grad_flow[...]
    for unit, part, k in order:
        (misc_sum if unit == steps else reduction(unit, part)).step(k)


def mix_rows(products, inverse, factor, wide):
    channels = products.shape[0]
    half = channels // 2
    rows = lax.broadcasted_iota(jnp.int32, (channels, channels), 0)
    cols = lax.broadcasted_iota(jnp.int32, (channels, channels), 1)
    row_top, col_top = rows < half, cols < half
    row_in = jnp.where(row_top, rows, rows - half)
    col_in = jnp.where(col_top, cols, cols - half)
    row_member = jnp.where(row_top, 0, 2) + (row_in & 1)
    col_member = jnp.where(col_top, 0, 2) + (col_in & 1)
    same = (row_in >> 1) == (col_in >> 1)
    kept = jnp.where(same, products, 0.0)
    row = lax.broadcasted_iota(jnp.int32, (8, wide), 0)
    lane = lax.broadcasted_iota(jnp.int32, (8, wide), 1)
    result = jnp.zeros((8, wide), f32)
    for i in range(4):
        mine = jnp.where(row_member == i, kept, 0.0)
        for j in range(4):
            picked = jnp.where(col_member == j, mine, 0.0)
            total = jnp.sum(jnp.sum(picked, axis=0, keepdims=True), axis=1, keepdims=True)
            total = total + factor * inverse[j][i][0:1, 0:1]
            result = jnp.where((row == i) & (lane == j), total, result)
    return result


def finish_kernel(
    sizes,
    units_ref,
    misc_ref,
    grad_in_ref,
    grad_in_out,
    norm_b_out,
    norm_l_out,
    mix_out,
    start_w_out,
    start_b_out,
    conv_w_out,
    conv_b_out,
    res_w_out,
    res_b_out,
    last_w_out,
    last_b_out,
    end_w_out,
    end_b_out,
    sems,
):
    blocks, layers, kernel, hidden_size, channels, frames = sizes
    half = channels // 2
    deep = kernel * hidden_size
    steps = blocks * layers
    stores = []

    def store(source, target):
        stores.append(pltpu.make_async_copy(source, target, sems.at[len(stores)]))
        stores[-1].start()

    for step in range(steps):
        b, layer = blocks - 1 - step // layers, layers - 1 - step % layers
        store(units_ref.at[step, :deep], conv_w_out.at[b, layer])
        if layer < layers - 1:
            store(units_ref.at[step, deep:], res_w_out.at[b, layer])
    for b in range(blocks):
        at = b * MISC
        start_w_out[b] = misc_ref[at : at + half, :hidden_size]
        at += half
        for row, (out, width) in enumerate(
            ((end_b_out, channels), (last_b_out, hidden_size), (start_b_out, hidden_size), (norm_b_out, channels), (norm_l_out, channels))
        ):
            out[b : b + 1, :] = misc_ref[at + row : at + row + 1, :width]
        conv_b_out[b] = misc_ref[at + 8 : at + 8 + layers]
        for layer in range(layers - 1):
            res_b_out[layer, b : b + 1, :] = misc_ref[at + 8 + layers + layer : at + 9 + layers + layer]
        mix_out[b] = misc_ref[at + 16 : at + 20, :4]
    for b in range(blocks):
        tail = units_ref[(blocks - 1 - b) * layers, deep:]
        last_w_out[b] = tail[:, :hidden_size]
        end_w_out[b] = tail[:channels, hidden_size:]
    grad_in_out[...] = grad_in_ref[...]
    for made in stores:
        made.wait()


def finish_call(sizes, grad_in, units, misc):
    blocks, layers, kernel, hidden_size, channels, frames = sizes
    half, deep, wide = channels // 2, kernel * hidden_size, 2 * hidden_size
    vmem = pl.BlockSpec(memory_space=pltpu.VMEM)
    hbm = pl.BlockSpec(memory_space=pl.ANY)
    dims = [
        (1, channels, frames),
        (blocks, channels),
        (blocks, channels),
        (blocks, 4, 4),
        (blocks, half, hidden_size),
        (blocks, hidden_size),
        (blocks, layers, deep, wide),
        (blocks, layers, wide),
        (blocks, layers - 1, hidden_size, wide),
        (layers - 1, blocks, wide),
        (blocks, hidden_size, hidden_size),
        (blocks, hidden_size),
        (blocks, channels, hidden_size),
        (blocks, channels),
    ]
    large = (6, 8)
    return pl.pallas_call(
        functools.partial(finish_kernel, sizes),
        name="flow_finish",
        out_shape=[jax.ShapeDtypeStruct(d, f32) for d in dims],
        in_specs=[vmem, vmem, vmem],
        out_specs=[hbm if i in large else vmem for i in range(len(dims))],
        scratch_shapes=[
            pltpu.SemaphoreType.DMA((2 * blocks * layers,)),
        ],
        compiler_params=pltpu.CompilerParams(vmem_limit_bytes=32 * 2**20),
    )(units, misc, grad_in)


def backward_call(count, lengths, grad_det, grad_out, params, saved):
    (norm_bias, norm_logs, mix, start_w, _, conv_w, _, res_w, _, last_w, _, end_w, _) = params
    hid, tanh_all, sig_all, mixed, wn, scale, x_all = saved
    _, channels, frames = grad_out.shape
    conv_w, res_w, start_w = conv_w.swapaxes(2, 3), res_w.swapaxes(2, 3), start_w.swapaxes(1, 2)
    blocks, layers, deep, wide = conv_w.shape
    hidden_size = wide // 2
    kernel = deep // hidden_size
    half = channels // 2
    steps = blocks * layers
    sizes = (blocks, layers, kernel, hidden_size, channels, frames)
    bits = count.bit_length() - 1
    halvings = 4
    depth = 3
    rows = deep + hidden_size
    part_rows = rows // PARTS
    vmem = pl.BlockSpec(memory_space=pltpu.VMEM)
    smem = pl.BlockSpec(memory_space=pltpu.SMEM)
    hbm = pl.BlockSpec(memory_space=pl.ANY)
    shape = jax.ShapeDtypeStruct
    shares = [2 ** -min(hop + 1, halvings) for hop in range(bits)]
    hops = bits + halvings
    starts = [
        row if len(row) == hops + 1 else [ready + 2 * k for k in range(hops + 1)]
        for row, ready in zip(STARTS, READY)
    ]
    order = drain_order(starts, bits, halvings, depth, steps, part_rows, blocks * MISC)
    return pl.pallas_call(
        functools.partial(backward_kernel, sizes, bits, halvings, depth, starts, order),
        name="flow_backward",
        out_shape=[
            pltpu.VMEM((1, channels, frames), f32),
            pltpu.VMEM((steps, rows, wide), f32),
            pltpu.VMEM((blocks * MISC, wide), f32),
        ],
        in_specs=[smem, smem, smem] + [vmem] * 6 + [hbm] * 9,
        out_specs=[vmem, vmem, vmem],
        scratch_shapes=[
            pltpu.VMEM((2, 3, hidden_size, frames), f32),
            pltpu.VMEM((blocks, channels, frames), f32),
            pltpu.VMEM((blocks, hidden_size, frames), f32),
            pltpu.VMEM((blocks, half, frames), f32),
            pltpu.VMEM((blocks, channels, frames), f32),
            pltpu.VMEM((2, deep, wide), f32),
            pltpu.VMEM((2, hidden_size, wide), f32),
            pltpu.VMEM((deep + 16, frames), bf16),
            pltpu.VMEM((deep + 16, frames), bf16),
            pltpu.VMEM((kernel * wide, frames), bf16),
            pltpu.VMEM((kernel * wide, frames), bf16),
            pltpu.VMEM((hidden_size, kernel * wide), bf16),
            pltpu.VMEM((hidden_size, kernel * wide), bf16),
            pltpu.VMEM((hidden_size + 16, frames), bf16),
            pltpu.VMEM((hidden_size + 16, frames), bf16),
            pltpu.VMEM((wide, frames), bf16),
            pltpu.VMEM((wide, frames), bf16),
            pltpu.VMEM((hidden_size, frames), f32),
            pltpu.VMEM((hidden_size, frames), f32),
            pltpu.VMEM((hidden_size, frames), f32),
            pltpu.VMEM((channels, frames), f32),
            pltpu.VMEM((half, frames), f32),
            pltpu.VMEM((hidden_size, 128), f32),
            pltpu.SemaphoreType.DMA((2, 3)),
            pltpu.SemaphoreType.DMA((2, 2)),
            pltpu.SemaphoreType.DMA((blocks, 4)),
            pltpu.SemaphoreType.DMA((depth * PARTS + 1, 2, bits)),
            pltpu.SemaphoreType.DMA((steps * PARTS + 1, 2, halvings)),
            pltpu.SemaphoreType.REGULAR((depth * PARTS, bits)),
            pltpu.SemaphoreType.REGULAR((steps * PARTS + 1, halvings)),
        ]
        + [pltpu.VMEM((depth, PARTS, int(part_rows * s), wide), f32) for s in shares]
        + [pltpu.VMEM((int(blocks * MISC * s), wide), f32) for s in shares],
        compiler_params=pltpu.CompilerParams(
            collective_id=0, has_side_effects=True, vmem_limit_bytes=SUM_LIMIT
        ),
    )(lengths, grad_det, mix, grad_out, norm_bias, norm_logs, start_w, last_w, end_w, conv_w, res_w,
      hid, tanh_all, sig_all, mixed, wn, scale, x_all)


def shards(mesh_size, mel, lengths, *rest):
    params, grad_out, grad_det = rest[:13], rest[13], rest[14]
    flowed, logdet, *saved = forward_call(mel, lengths, params)
    blocks, layers, wide, deep = params[5].shape
    hidden_size = wide // 2
    sizes = (blocks, layers, deep // hidden_size, hidden_size, mel.shape[1], mel.shape[2])
    summed = backward_call(mesh_size, lengths, grad_det, grad_out, params, saved)
    grads = list(finish_call(sizes, *summed))
    for i in (6, 8):
        grads[i] = grads[i].swapaxes(2, 3)
    grads[4] = grads[4].swapaxes(1, 2)
    grads[9] = grads[9].swapaxes(0, 1)
    return (flowed, logdet[0, :1], *grads)


def solution(mesh):
    split_first, whole = P("dp", None, None), P()
    in_specs = (split_first, P("dp")) + (whole,) * 13 + (split_first, P("dp"))
    out_specs = (split_first, P("dp"), split_first) + (whole,) * 13
    return jax.shard_map(
        functools.partial(shards, mesh.shape["dp"]),
        mesh=mesh,
        in_specs=in_specs,
        out_specs=out_specs,
        check_vma=False,
    )
```

```python
import functools

import jax
import jax.numpy as jnp
from jax import lax
from jax.experimental import pallas as pl
from jax.experimental.pallas import tpu as pltpu
from jax.sharding import PartitionSpec as P

f32, bf16 = jnp.float32, jnp.bfloat16
NN = (((1,), (0,)), ((), ()))
NT = (((1,), (1,)), ((), ()))
TN = (((0,), (0,)), ((), ()))
VMEM_LIMIT = 60 * 2**20


def dot(left, right, form=NN):
    return lax.dot_general(left, right, form, preferred_element_type=f32)


def split(value):
    high = value.astype(bf16)
    return high, (value - high.astype(f32)).astype(bf16)


def dot3(left, right, form=NN):
    (left_high, left_low), (right_high, right_low) = left, right
    return (
        dot(left_high, right_high, form)
        + dot(left_high, right_low, form)
        + dot(left_low, right_high, form)
    )


def mix_matrix(mix_ref, block, channels):
    half = channels // 2
    rows = lax.broadcasted_iota(jnp.int32, (channels, channels), 0)
    cols = lax.broadcasted_iota(jnp.int32, (channels, channels), 1)
    row_top, col_top = rows < half, cols < half
    row_in = jnp.where(row_top, rows, rows - half)
    col_in = jnp.where(col_top, cols, cols - half)
    row_member = jnp.where(row_top, 0, 2) + (row_in & 1)
    col_member = jnp.where(col_top, 0, 2) + (col_in & 1)
    same = (row_in >> 1) == (col_in >> 1)
    pair = row_member * 4 + col_member
    result = jnp.zeros((channels, channels), f32)
    for i in range(4):
        for j in range(4):
            result = jnp.where(pair == 4 * i + j, mix_ref[block, i, j], result)
    return jnp.where(same, result, 0.0)


def inverse_logdet(mix_ref, block):
    shape = (8, 128)
    left = [[jnp.full(shape, mix_ref[block, i, j], f32) for j in range(4)] for i in range(4)]
    right = [[jnp.full(shape, float(i == j), f32) for j in range(4)] for i in range(4)]
    log_total = jnp.zeros(shape, f32)
    for k in range(4):
        pivot = left[k][k]
        log_total = log_total + jnp.log(pivot)
        left[k] = [v / pivot for v in left[k]]
        right[k] = [v / pivot for v in right[k]]
        for i in range(4):
            if i != k:
                factor = left[i][k]
                left[i] = [v - factor * w for v, w in zip(left[i], left[k])]
                right[i] = [v - factor * w for v, w in zip(right[i], right[k])]
    return right, log_total


def fill_columns(rows_ref, cols_ref, block, vectors):
    rows_ref[...] = jnp.zeros_like(rows_ref)
    for j, vector in enumerate(vectors):
        rows_ref[j : j + 1, : vector.shape[1]] = vector
    cols_ref[...] = rows_ref[...].T


def frame_mask(length, frames):
    return (lax.broadcasted_iota(jnp.int32, (1, frames), 1) < length).astype(f32)


ROWS = 16


def chunks(rows, size=ROWS):
    return [slice(at, min(at + size, rows)) for at in range(0, rows, size)]


def shift_by(at, by):
    return slice(at.start + by, at.stop + by)


def fill_rows(value, at, high_ref, low_ref, kernel, channels, sign):
    high, low = split(value)
    for k in range(kernel):
        move = (sign * (k - kernel // 2)) % value.shape[1]
        to = shift_by(at, k * channels)
        high_ref[to] = pltpu.roll(high, move, 1) if move else high
        low_ref[to] = pltpu.roll(low, move, 1) if move else low


def fill_split(source, high_ref, low_ref, size=64):
    for at in chunks(source.shape[0], size):
        high_ref[at], low_ref[at] = split(source[at])


def forward_kernel(
    sizes,
    length_ref,
    mix_ref,
    x_ref,
    norm_bias_ref,
    norm_logs_ref,
    start_w_ref,
    start_b_ref,
    conv_w_ref,
    conv_b_ref,
    res_w_ref,
    res_b_ref,
    last_w_ref,
    last_b_ref,
    end_w_ref,
    end_b_ref,
    flowed_ref,
    logdet_ref,
    hid_out,
    tanh_out,
    sig_out,
    mixed_out,
    wn_out,
    scale_out,
    x_out,
    x_buf,
    hid_buf,
    tanh_buf,
    sig_buf,
    mixed_buf,
    wn_buf,
    scale_buf,
    conv_stage,
    res_stage,
    stack_high,
    stack_low,
    conv_high,
    conv_low,
    res_high,
    res_low,
    gated_high,
    gated_low,
    out_buf,
    skip_buf,
    det_buf,
    rows_buf,
    cols_buf,
    in_sem,
    out_sem,
    misc_sem,
):
    blocks, layers, kernel, hidden_size, channels, frames = sizes
    half = channels // 2
    steps = blocks * layers
    length = length_ref[0]
    mask = frame_mask(length, frames)

    def conv_copy(block, layer):
        at = block * layers + layer
        return pltpu.make_async_copy(conv_w_ref.at[block, layer], conv_stage.at[at], in_sem.at[0, at])

    def res_copy(block, layer):
        at = block * layers + layer
        return pltpu.make_async_copy(res_w_ref.at[block, layer], res_stage.at[at], in_sem.at[1, at])

    def saves(step):
        return [
            pltpu.make_async_copy(buf.at[step], out.at[step], out_sem.at[i, step])
            for i, (buf, out) in enumerate(
                ((hid_buf, hid_out), (tanh_buf, tanh_out), (sig_buf, sig_out))
            )
        ]

    def block_saves(block):
        return [
            pltpu.make_async_copy(buf.at[block], out.at[block], misc_sem.at[i, block])
            for i, (buf, out) in enumerate(
                ((mixed_buf, mixed_out), (x_buf, x_out), (wn_buf, wn_out), (scale_buf, scale_out))
            )
        ]

    for block in range(blocks):
        for layer in range(layers):
            conv_copy(block, layer).start()
            if layer < layers - 1:
                res_copy(block, layer).start()
    x_buf[0] = x_ref[0]
    det_buf[...] = jnp.zeros_like(det_buf)

    def run_block(block, carry):
        fill_columns(
            rows_buf,
            cols_buf,
            block,
            [conv_b_ref[block, pl.ds(l, 1), :] for l in range(layers)]
            + [res_b_ref[l, pl.ds(block, 1), :] for l in range(layers - 1)]
            + [
                r[pl.ds(block, 1), :]
                for r in (start_b_ref, last_b_ref, end_b_ref, norm_bias_ref, norm_logs_ref)
            ],
        )
        base = 2 * layers - 1
        start_b = cols_buf[:hidden_size, base : base + 1]
        last_b = cols_buf[:hidden_size, base + 1 : base + 2]
        end_b = cols_buf[:channels, base + 2 : base + 3]
        norm_b = cols_buf[:channels, base + 3 : base + 4]
        norm_l = cols_buf[:channels, base + 4 : base + 5]
        normed = (norm_b + jnp.exp(norm_l) * x_buf[block]) * mask
        mixed = dot3(split(mix_matrix(mix_ref, block, channels)), split(normed))
        mixed_buf[block] = mixed
        for save in block_saves(block)[:2]:
            save.start()
        hidden = (dot3(split(start_w_ref[block]), split(mixed[:half]), TN) + start_b) * mask
        hid_buf[block * layers] = hidden

        for layer in range(layers):
            step = block * layers + layer
            last = layer == layers - 1
            saves(step)[0].start()
            conv_copy(block, layer).wait()
            if not last:
                res_copy(block, layer).wait()
            fill_split(conv_stage.at[step], conv_high, conv_low)
            for at in chunks(hidden_size):
                fill_rows(hid_buf[step, at], at, stack_high, stack_low, kernel, hidden_size, -1)
            if not last:
                fill_split(res_stage.at[step], res_high, res_low)
            out_buf[...] = dot3((conv_high[...], conv_low[...]), (stack_high[...], stack_low[...]), TN)
            for at in chunks(hidden_size):
                below = shift_by(at, hidden_size)
                tanh_part = jnp.tanh(out_buf[at] + cols_buf[at, layer : layer + 1])
                sig_part = 0.5 * jnp.tanh(0.5 * (out_buf[below] + cols_buf[below, layer : layer + 1])) + 0.5
                tanh_buf[step, at] = tanh_part
                sig_buf[step, at] = sig_part
                gated_high[at], gated_low[at] = split(tanh_part * sig_part)
            gated = (gated_high[...], gated_low[...])
            if last:
                skip_buf[...] += dot3(split(last_w_ref[block]), gated)
            else:
                out_buf[...] = dot3((res_high[...], res_low[...]), gated, TN)
                bias = slice(layers + layer, layers + layer + 1)
                for at in chunks(hidden_size):
                    below = shift_by(at, hidden_size)
                    res = out_buf[below] + cols_buf[below, bias]
                    skip_buf[at] = res + (skip_buf[at] if layer else last_b[at])
                    hid_buf[step + 1, at] = (hid_buf[step, at] + (out_buf[at] + cols_buf[at, bias])) * mask
            for save in saves(step)[1:]:
                save.start()
        wavenet = skip_buf[...] * mask
        wn_buf[block] = wavenet
        out = dot3(split(end_w_ref[block]), split(wavenet)) + end_b
        scale = jnp.exp(out[half:])
        scale_buf[block] = scale
        mixed = mixed_buf[block]
        moved = (out[:half] + scale * mixed[half:]) * mask
        _, log_det = inverse_logdet(mix_ref, block)
        det_buf[0:1, :] += jnp.sum(norm_l) + log_det[0:1, :] * (channels // 4)
        det_buf[1:2, :] += jnp.full((1, 128), jnp.sum(out[half:] * mask))
        x_buf[block + 1, :half] = mixed[:half]
        x_buf[block + 1, half:] = moved
        for save in block_saves(block)[2:]:
            save.start()
        return carry

    lax.fori_loop(0, blocks, run_block, 0)
    flowed_ref[0] = x_buf[blocks]
    logdet_ref[...] = det_buf[0:1, :] + det_buf[1:2, :] / length.astype(f32)

    def finish(step, carry):
        for save in saves(step):
            save.wait()
        return carry

    lax.fori_loop(0, steps, finish, 0)

    def finish_block(block, carry):
        for save in block_saves(block):
            save.wait()
        return carry

    lax.fori_loop(0, blocks, finish_block, 0)


def forward_call(mel, lengths, params):
    (norm_bias, norm_logs, mix, start_w, start_b, conv_w, conv_b, res_w, res_b, last_w, last_b, end_w, end_b) = params
    _, channels, frames = mel.shape
    conv_w, res_w = conv_w.swapaxes(2, 3), res_w.swapaxes(2, 3)
    start_w, res_b = start_w.swapaxes(1, 2), res_b.swapaxes(0, 1)
    blocks, layers, deep, wide = conv_w.shape
    hidden_size = wide // 2
    kernel = deep // hidden_size
    half = channels // 2
    steps = blocks * layers
    sizes = (blocks, layers, kernel, hidden_size, channels, frames)
    vmem = pl.BlockSpec(memory_space=pltpu.VMEM)
    smem = pl.BlockSpec(memory_space=pltpu.SMEM)
    hbm = pl.BlockSpec(memory_space=pl.ANY)
    shape = jax.ShapeDtypeStruct
    act = (steps, hidden_size, frames)
    return pl.pallas_call(
        functools.partial(forward_kernel, sizes),
        name="flow_forward",
        out_shape=[
            shape((1, channels, frames), f32),
            shape((1, 128), f32),
            shape(act, f32),
            shape(act, f32),
            shape(act, f32),
            shape((blocks, channels, frames), f32),
            shape((blocks, hidden_size, frames), f32),
            shape((blocks, half, frames), f32),
            shape((blocks, channels, frames), f32),
        ],
        in_specs=[smem, smem, vmem, vmem, vmem, vmem, vmem, hbm, vmem, hbm, vmem, vmem, vmem, vmem, vmem],
        out_specs=[vmem, vmem] + [hbm] * 7,
        scratch_shapes=[
            pltpu.VMEM((blocks + 1, channels, frames), f32),
            pltpu.VMEM(act, f32),
            pltpu.VMEM(act, f32),
            pltpu.VMEM(act, f32),
            pltpu.VMEM((blocks, channels, frames), f32),
            pltpu.VMEM((blocks, hidden_size, frames), f32),
            pltpu.VMEM((blocks, half, frames), f32),
            pltpu.VMEM((steps, deep, wide), f32),
            pltpu.VMEM((steps, hidden_size, wide), f32),
            pltpu.VMEM((deep, frames), bf16),
            pltpu.VMEM((deep, frames), bf16),
            pltpu.VMEM((deep, wide), bf16),
            pltpu.VMEM((deep, wide), bf16),
            pltpu.VMEM((hidden_size, wide), bf16),
            pltpu.VMEM((hidden_size, wide), bf16),
            pltpu.VMEM((hidden_size, frames), bf16),
            pltpu.VMEM((hidden_size, frames), bf16),
            pltpu.VMEM((wide, frames), f32),
            pltpu.VMEM((hidden_size, frames), f32),
            pltpu.VMEM((8, 128), f32),
            pltpu.VMEM((16, wide), f32),
            pltpu.VMEM((wide, 16), f32),
            pltpu.SemaphoreType.DMA((2, steps)),
            pltpu.SemaphoreType.DMA((3, steps)),
            pltpu.SemaphoreType.DMA((4, blocks)),
        ],
        compiler_params=pltpu.CompilerParams(vmem_limit_bytes=VMEM_LIMIT),
    )(lengths, mix, mel, norm_bias, norm_logs, start_w, start_b, conv_w, conv_b, res_w, res_b, last_w, last_b, end_w, end_b)
MESH = pl.DeviceIdType.MESH
MISC = 128
SLOTS = 3
SUM_LIMIT = 47 * 2**20
PARTS = 3
POINTS = 6
READY = (2, 3, 4)
STARTS = ((2, 4, 6, 10, 15, 21, 24, 29, 34, 36), (3, 4, 7, 10, 13, 17, 23, 26, 29, 31), (4, 5, 9, 11, 14, 19, 21, 25, 31, 34))


POINT_US = (2.2, 1.0, 1.1, 1.1, 1.1, 2.6)
RATES = {"x": 58.6, "y": 58.6, "z": 61.8, "middle": 55.3}
CORE_ROWS = 420.0
LATENCY = {"core": 0.75, "far": 2.6}


class Link:
    def __init__(self, rate):
        self.queues, self.clock, self.rate = ([], []), 0.0, rate

    def run(self, until):
        while any(self.queues) and self.clock < until:
            heads = [queue[0] for queue in self.queues if queue]
            rate = self.rate / len(heads)
            spent = min(min(head[0] for head in heads) / rate, until - self.clock)
            self.clock += spent
            for queue in self.queues:
                if queue:
                    queue[0][0] -= spent * rate
                    if queue[0][0] < 1e-6:
                        queue.pop(0)[1] = self.clock
        if self.clock < until < float("inf"):
            self.clock = until

    def add(self, now, core, rows):
        self.run(now)
        job = [rows, None]
        self.queues[core].append(job)
        return self, job


class Plan:
    def __init__(self, bits, halvings, steps, part_rows, misc_rows):
        self.bits, self.hops, self.steps = bits, bits + halvings, steps
        self.rows = (part_rows, misc_rows)
        self.links = {name: Link(rate) for name, rate in RATES.items()}
        self.links |= {("core", core): Link(CORE_ROWS) for core in range(2)}
        self.clock, self.jobs, self.taken = 0.0, {}, {}
        sizes = [2 ** -(h + 1) for h in range(halvings)]
        self.sizes = sizes + [sizes[-1]] * (bits - halvings) + sizes[::-1]

    def name(self, part, k):
        near = ("z", "a", "b") if part == PARTS - 1 else ("a", "b", "z")
        return ["core", *near, *["far"] * (self.bits - 4), *reversed(near), "core"][k]

    def start(self, unit, part, k):
        name, jobs = self.name(part, k), []
        rows = self.sizes[k] * self.rows[unit == self.steps]
        for core in range(2):
            if name == "core":
                jobs.append(self.links[name, core].add(self.clock, core, rows))
                continue
            link = "z" if name in ("z", "far") else "xy"[(name == "b") ^ core]
            jobs.append(self.links[link].add(self.clock, core, rows))
            if name == "far":
                jobs.append(self.links["middle"].add(self.clock, core, 2 * rows))
        self.jobs[unit, part] = jobs, LATENCY.get(name, 2.1)

    def arrival(self, unit, part, until=float("inf")):
        if not self.taken.get((unit, part)):
            return 0.0
        jobs, latency = self.jobs[unit, part]
        for link, job in jobs:
            if job[1] is None:
                link.run(until)
            if job[1] is None:
                return float("inf")
        return max(job[1] for _, job in jobs) + latency

    def take(self, unit, part, k):
        if k:
            self.clock = max(self.clock, self.arrival(unit, part)) + 0.1
        self.taken[unit, part] = k + 1
        if k < self.hops:
            self.start(unit, part, k)


def drain_order(starts, bits, halvings, depth, steps, part_rows, misc_rows):
    plan = Plan(bits, halvings, steps, part_rows, misc_rows)
    for layer in range(steps):
        for point in range(POINTS):
            plan.clock += POINT_US[point]
            for lag, part, k in due_steps(starts, point):
                if layer >= lag:
                    plan.take(layer - lag, part, k)
    order, taken = [], plan.taken
    waiting = [(unit, part) for unit in range(steps) for part in range(PARTS)] + [(steps, 0)]
    waiting = [w for w in waiting if taken.get(w, 0) <= plan.hops]
    while waiting:
        ready = []
        for unit, part in waiting:
            k = taken.get((unit, part), 0)
            slot_free = unit in range(depth) or unit == steps or k >= bits or taken[unit - depth, part] > k + 1
            if slot_free and plan.arrival(unit, part, plan.clock) <= plan.clock:
                ready.append((k >= bits, unit, part, k))
        if not ready:
            plan.clock += 0.1
            continue
        _, unit, part, k = min(ready)
        plan.take(unit, part, k)
        order.append((unit, part, k))
        if k == plan.hops:
            waiting.remove((unit, part))
    return order


def due_steps(starts, point):
    due = [
        (start // POINTS, part, k)
        for part, row in enumerate(starts)
        for k, start in enumerate(row)
        if start % POINTS == point
    ]
    return sorted(due, key=lambda due: (-due[0], due[1], due[2]))


class Exchange:
    def __init__(self, bits, halvings):
        self.bits, self.halvings = bits, halvings
        self.hops = bits + halvings
        self.me = lax.axis_index("dp")
        self.value = [lax.rem(self.me // 2**b, 2) for b in range(bits)]
        self.orders = [self.order(turn) for turn in range(2)]
        self.partners = [[self.partner(hop) for hop in order] for order in self.orders]

    def order(self, turn):
        pairs = [(self.value[b], 2**b) for b in range(self.bits)]

        def either(flag, yes, no):
            return tuple(flag * y + (1 - flag) * n for y, n in zip(yes, no))

        odd = self.value[0]
        first = either(odd, pairs[2], pairs[1])
        second = either(odd, pairs[1], pairs[2])
        return [
            pairs[0],
            either(turn, pairs[3], first),
            either(turn, first, second),
            either(turn, second, pairs[3]),
        ] + pairs[4:]

    def partner(self, hop):
        bit, stride = hop
        return (self.me + (1 - 2 * bit) * stride,)

    def spans(self, turn, rows):
        at, size, result = 0, rows, []
        for bit, _ in self.orders[turn][: self.halvings]:
            size //= 2
            result.append((at + bit * size, at + (1 - bit) * size, size))
            at = at + bit * size
        return result


class Reduction:
    def __init__(self, exchange, turn, spans, source, slots, sems, base, later=None):
        self.x, self.source = exchange, source
        self.slots, self.sems, self.base, self.later = slots, sems, base, later
        self.partners, self.spans = exchange.partners[turn], spans

    def rows_of(self, at, size):
        return pl.ds(pl.multiple_of(self.base + at, 8), size)

    def copy_sem(self, side, hop):
        out, back = self.sems[0], self.sems[1]
        return out.at[side, hop] if hop < self.x.bits else back.at[side, hop - self.x.bits]

    def copy(self, hop):
        halvings, bits = self.x.halvings, self.x.bits
        if hop < bits:
            if hop < halvings:
                _, at, size = self.spans[hop]
            else:
                at, _, size = self.spans[-1]
            src = self.source.at[self.rows_of(at, size)]
            dst = self.slots[hop]
            to = self.partners[hop]
        else:
            level = halvings - 1 - (hop - bits)
            at, _, size = self.spans[level]
            src = dst = self.source.at[self.rows_of(at, size)]
            to = self.partners[level]
        return pltpu.make_async_remote_copy(
            src_ref=src,
            dst_ref=dst,
            send_sem=self.copy_sem(0, hop),
            recv_sem=self.copy_sem(1, hop),
            device_id=to,
            device_id_type=MESH,
        )

    def step(self, k):
        x = self.x
        if k > 0:
            done = k - 1
            self.copy(done).wait()
            if done < x.bits:
                at, _, size = self.spans[min(done, x.halvings - 1)]
                where = self.rows_of(at, size)
                self.source[where] += self.slots[done][...]
                self.free(done)
            if done < x.halvings:
                pl.semaphore_signal(
                    self.sems[3].at[done], inc=1, device_id=self.partners[done], device_id_type=MESH
                )
        if k < x.hops:
            if k < x.bits:
                self.wait_free(k)
            else:
                pl.semaphore_wait(self.sems[3].at[x.hops - 1 - k], 1)
            self.copy(k).start()

    def free(self, hop):
        if self.later is not None:
            credit, exists = self.later

            @pl.when(exists)
            def _():
                pl.semaphore_signal(
                    credit.at[hop],
                    inc=1,
                    device_id=self.partners[hop],
                    device_id_type=MESH,
                )

    def wait_free(self, hop):
        credit, needed = self.sems[2] if self.sems[2] is not None else (None, None)
        if credit is not None:

            @pl.when(needed)
            def _():
                pl.semaphore_wait(credit.at[hop], 1)


def backward_kernel(
    sizes,
    bits,
    halvings,
    depth,
    starts,
    order,
    length_ref,
    grad_det_ref,
    mix_ref,
    grad_out_ref,
    norm_bias_ref,
    norm_logs_ref,
    start_w_ref,
    last_w_ref,
    end_w_ref,
    conv_w_ref,
    res_w_ref,
    hid_ref,
    tanh_ref,
    sig_ref,
    mixed_ref,
    wn_ref,
    scale_ref,
    x_ref,
    grad_in_ref,
    unit_buf,
    misc_buf,
    *scratch,
):
    (
        act_buf,
        mixed_buf,
        wn_buf,
        scale_buf,
        x_buf,
        conv_stage,
        res_stage,
        stack_high,
        stack_low,
        back_high,
        back_low,
        turned_high,
        turned_low,
        gated_high,
        gated_low,
        pair_high,
        pair_low,
        grad_skip,
        grad_hid,
        grad_gated,
        grad_flow,
        grad_changed,
        columns_buf,
        act_sem,
        weight_sem,
        block_sem,
        out_copy_sem,
        back_copy_sem,
        credit_sem,
        clear_sem,
    ) = scratch[:30]
    slot_bufs = scratch[30 : 30 + bits]
    misc_slots = scratch[30 + bits :]
    blocks, layers, kernel, hidden_size, channels, frames = sizes
    half = channels // 2
    steps = blocks * layers
    deep = kernel * hidden_size
    wide = 2 * hidden_size
    middle = kernel // 2
    length = length_ref[0]
    mask = frame_mask(length, frames)
    grad_det = grad_det_ref[0]
    exchange = Exchange(bits, halvings)

    part_rows = (deep + hidden_size) // PARTS
    spans = [exchange.spans(turn, part_rows) for turn in range(2)]

    def reduction(unit, part):
        slot = lax.rem(unit, depth)
        after = unit + depth
        return Reduction(
            exchange,
            int(part == PARTS - 1),
            spans[int(part == PARTS - 1)],
            unit_buf.at[unit],
            [b.at[slot, part] for b in slot_bufs],
            (
                out_copy_sem.at[slot * PARTS + part],
                back_copy_sem.at[unit * PARTS + part],
                (credit_sem.at[slot * PARTS + part], unit >= depth),
                clear_sem.at[unit * PARTS + part],
            ),
            part * part_rows,
            (credit_sem.at[slot * PARTS + part], after < steps),
        )

    misc_sum = Reduction(
        exchange,
        0,
        exchange.spans(0, blocks * MISC),
        misc_buf,
        misc_slots,
        (
            out_copy_sem.at[depth * PARTS],
            back_copy_sem.at[steps * PARTS],
            None,
            clear_sem.at[steps * PARTS],
        ),
        0,
    )

    def tick(step, point):
        for lag, part, k in due_steps(starts, point):
            unit = step - lag

            @pl.when(unit >= 0)
            def _(unit=unit, part=part, k=k):
                reduction(unit, part).step(k)

    def act_copies(step):
        slot = lax.rem(step, SLOTS)
        at = steps - 1 - step
        return [
            pltpu.make_async_copy(ref.at[at], act_buf.at[slot, i], act_sem.at[slot, i])
            for i, ref in enumerate((hid_ref, tanh_ref, sig_ref))
        ]

    def weight_copies(step):
        slot = lax.rem(step, SLOTS)
        block, layer = blocks - 1 - step // layers, layers - 1 - lax.rem(step, layers)
        conv = pltpu.make_async_copy(conv_w_ref.at[block, layer], conv_stage.at[slot], weight_sem.at[slot, 0])
        res = pltpu.make_async_copy(
            res_w_ref.at[block, jnp.minimum(layer, layers - 2)], res_stage.at[slot], weight_sem.at[slot, 1]
        )
        return [conv, res]

    def block_copies(block):
        return [
            pltpu.make_async_copy(ref.at[block], buf.at[block], block_sem.at[block, i])
            for i, (ref, buf) in enumerate(
                ((wn_ref, wn_buf), (scale_ref, scale_buf), (mixed_ref, mixed_buf), (x_ref, x_buf))
            )
        ]

    for copy in act_copies(0) + block_copies(blocks - 1) + weight_copies(0):
        copy.start()

    barrier = pltpu.get_barrier_semaphore()
    for b in range(bits):
        pl.semaphore_signal(
            barrier, inc=1, device_id=exchange.partner((exchange.value[b], 2**b)), device_id_type=MESH
        )
    grad_flow[...] = grad_out_ref[0]
    misc_buf[...] = jnp.zeros_like(misc_buf)
    columns_buf[...] = jnp.zeros_like(columns_buf)
    for high, low, rows in ((stack_high, stack_low, deep), (gated_high, gated_low, hidden_size)):
        high[rows:, :] = jnp.ones((16, frames), bf16)
        low[rows:, :] = jnp.zeros((16, frames), bf16)
    pl.semaphore_wait(barrier, bits)
    for step in range(1, SLOTS - 1):
        for copy in act_copies(step) + weight_copies(step):
            copy.start()
    for block in reversed(range(blocks - 1)):
        for copy in block_copies(block):
            copy.start()

    def run_step(step, carry):
        block = blocks - 1 - step // layers
        layer = layers - 1 - lax.rem(step, layers)
        slot = lax.rem(step, SLOTS)
        misc_at = block * MISC
        for copy in act_copies(step) + weight_copies(step):
            copy.wait()

        @pl.when(step + SLOTS - 1 < steps)
        def _():
            for copy in act_copies(step + SLOTS - 1) + weight_copies(step + SLOTS - 1):
                copy.start()

        for at in chunks(hidden_size):
            gated_high[at], gated_low[at] = split(act_buf[slot, 1, at] * act_buf[slot, 2, at])

        @pl.when(layer == layers - 1)
        def _():
            for copy in block_copies(block):
                copy.wait()
            moved_grad = grad_flow[half:] * mask
            changed_grad = moved_grad * scale_buf[block]
            grad_changed[...] = changed_grad
            logs_grad = changed_grad * mixed_buf[block, half:] + (grad_det / length.astype(f32)) * mask
            out_grad = jnp.concatenate([moved_grad, logs_grad], axis=0)
            columns_buf[:channels, 0:1] = jnp.sum(out_grad, axis=1, keepdims=True)
            out_split = split(out_grad)
            end_grad = dot3(out_split, split(wn_buf[block]), NT)
            skip = dot3(split(end_w_ref[block]), out_split, TN) * mask
            columns_buf[:, 1:2] = jnp.sum(skip, axis=1, keepdims=True)
            skip_split = split(skip)
            pair_high[hidden_size:], pair_low[hidden_size:] = skip_split
            gated = (gated_high[:hidden_size], gated_low[:hidden_size])
            unit_buf[step, deep:, :hidden_size] = dot3(skip_split, gated, NT)
            unit_buf[step, deep : deep + channels, hidden_size:] = end_grad
            grad_gated[...] = dot3(split(last_w_ref[block]), skip_split, TN)
            grad_hid[...] = jnp.zeros_like(grad_hid)

        @pl.when(layer < layers - 1)
        def _():
            masked = grad_hid[...] * mask
            grad_hid[...] = masked
            pair_high[:hidden_size], pair_low[:hidden_size] = split(masked)
            pair = (pair_high[...], pair_low[...])
            grads = dot3((gated_high[...], gated_low[...]), pair, NT)
            unit_buf[step, deep:] = grads[:hidden_size]
            misc_buf[pl.ds(misc_at + half + 8 + layers + layer, 1), :] = grads[hidden_size : hidden_size + 1]
            grad_gated[...] = dot3(split(res_stage[slot]), pair)

        tick(step, 0)
        for at in chunks(hidden_size):
            tanh_part, sig_part = act_buf[slot, 1, at], act_buf[slot, 2, at]
            inner = grad_gated[at] * sig_part
            fill_rows(inner * (1.0 - tanh_part * tanh_part), at, back_high, back_low, kernel, wide, 1)
            below = shift_by(at, hidden_size)
            fill_rows(inner * tanh_part * (1.0 - sig_part), below, back_high, back_low, kernel, wide, 1)
            fill_rows(act_buf[slot, 0, at], at, stack_high, stack_low, kernel, hidden_size, -1)
        tick(step, 1)
        center = slice(middle * wide, (middle + 1) * wide)
        for part in range(PARTS):
            at = part * part_rows
            end = at + part_rows if part < PARTS - 1 else deep + 16
            grads = dot3((stack_high[at:end], stack_low[at:end]), (back_high[center], back_low[center]), NT)
            if part < PARTS - 1:
                unit_buf[step, at:end] = grads
            else:
                unit_buf[step, at:deep] = grads[: deep - at]
                misc_buf[pl.ds(misc_at + half + 8 + layer, 1), :] = grads[deep - at : deep - at + 1]
            tick(step, 2 + part)
        for k in range(kernel):
            high, low = split(conv_stage[slot, k * hidden_size : (k + 1) * hidden_size])
            turned_high[:, k * wide : (k + 1) * wide] = high
            turned_low[:, k * wide : (k + 1) * wide] = low
        grad_hid[...] += dot3((turned_high[...], turned_low[...]), (back_high[...], back_low[...]))

        @pl.when(layer == 0)
        def _():
            hid_grad = grad_hid[...] * mask
            hid_split = split(hid_grad)
            mixed = mixed_buf[block]
            start_grad = dot3(split(mixed[:half]), hid_split, NT)
            misc_buf[pl.ds(misc_at, half), :hidden_size] = start_grad
            columns_buf[:, 2:3] = jnp.sum(hid_grad, axis=1, keepdims=True)
            passed_grad = grad_flow[:half] + dot3(split(start_w_ref[block]), hid_split)
            mixed_grad = split(jnp.concatenate([passed_grad, grad_changed[...]], axis=0))
            norm_b = jnp.transpose(jnp.broadcast_to(norm_bias_ref[pl.ds(block, 1), :], (8, channels)))[:, 0:1]
            norm_s = jnp.exp(jnp.transpose(jnp.broadcast_to(norm_logs_ref[pl.ds(block, 1), :], (8, channels)))[:, 0:1])
            scaled = norm_s * x_buf[block]
            normed = (norm_b + scaled) * mask
            mix_grad = dot3(mixed_grad, split(normed), NT)
            normed_grad = dot3(split(mix_matrix(mix_ref, block, channels)), mixed_grad, TN) * mask
            columns_buf[:channels, 3:4] = jnp.sum(normed_grad, axis=1, keepdims=True)
            columns_buf[:channels, 4:5] = jnp.sum(normed_grad * scaled, axis=1, keepdims=True) + grad_det
            grad_flow[...] = normed_grad * norm_s
            rows = columns_buf[...].T
            misc_buf[pl.ds(misc_at + half, 8), :hidden_size] = rows[:8]
            inverse, _ = inverse_logdet(mix_ref, block)
            misc_buf[pl.ds(misc_at + half + 16, 8), :] = mix_rows(
                mix_grad, inverse, grad_det * (channels // 4), wide
            )

        tick(step, POINTS - 1)
        return carry

    lax.fori_loop(0, steps, run_step, 0)
    grad_in_ref[0] = grad_flow[...]
    for unit, part, k in order:
        (misc_sum if unit == steps else reduction(unit, part)).step(k)


def mix_rows(products, inverse, factor, wide):
    channels = products.shape[0]
    half = channels // 2
    rows = lax.broadcasted_iota(jnp.int32, (channels, channels), 0)
    cols = lax.broadcasted_iota(jnp.int32, (channels, channels), 1)
    row_top, col_top = rows < half, cols < half
    row_in = jnp.where(row_top, rows, rows - half)
    col_in = jnp.where(col_top, cols, cols - half)
    row_member = jnp.where(row_top, 0, 2) + (row_in & 1)
    col_member = jnp.where(col_top, 0, 2) + (col_in & 1)
    same = (row_in >> 1) == (col_in >> 1)
    kept = jnp.where(same, products, 0.0)
    row = lax.broadcasted_iota(jnp.int32, (8, wide), 0)
    lane = lax.broadcasted_iota(jnp.int32, (8, wide), 1)
    result = jnp.zeros((8, wide), f32)
    for i in range(4):
        mine = jnp.where(row_member == i, kept, 0.0)
        for j in range(4):
            picked = jnp.where(col_member == j, mine, 0.0)
            total = jnp.sum(jnp.sum(picked, axis=0, keepdims=True), axis=1, keepdims=True)
            total = total + factor * inverse[j][i][0:1, 0:1]
            result = jnp.where((row == i) & (lane == j), total, result)
    return result


def finish_kernel(
    sizes,
    units_ref,
    misc_ref,
    grad_in_ref,
    grad_in_out,
    norm_b_out,
    norm_l_out,
    mix_out,
    start_w_out,
    start_b_out,
    conv_w_out,
    conv_b_out,
    res_w_out,
    res_b_out,
    last_w_out,
    last_b_out,
    end_w_out,
    end_b_out,
    sems,
):
    blocks, layers, kernel, hidden_size, channels, frames = sizes
    half = channels // 2
    deep = kernel * hidden_size
    steps = blocks * layers
    stores = []

    def store(source, target):
        stores.append(pltpu.make_async_copy(source, target, sems.at[len(stores)]))
        stores[-1].start()

    for step in range(steps):
        b, layer = blocks - 1 - step // layers, layers - 1 - step % layers
        store(units_ref.at[step, :deep], conv_w_out.at[b, layer])
        if layer < layers - 1:
            store(units_ref.at[step, deep:], res_w_out.at[b, layer])
    for b in range(blocks):
        at = b * MISC
        start_w_out[b] = misc_ref[at : at + half, :hidden_size]
        at += half
        for row, (out, width) in enumerate(
            ((end_b_out, channels), (last_b_out, hidden_size), (start_b_out, hidden_size), (norm_b_out, channels), (norm_l_out, channels))
        ):
            out[b : b + 1, :] = misc_ref[at + row : at + row + 1, :width]
        conv_b_out[b] = misc_ref[at + 8 : at + 8 + layers]
        for layer in range(layers - 1):
            res_b_out[layer, b : b + 1, :] = misc_ref[at + 8 + layers + layer : at + 9 + layers + layer]
        mix_out[b] = misc_ref[at + 16 : at + 20, :4]
    for b in range(blocks):
        tail = units_ref[(blocks - 1 - b) * layers, deep:]
        last_w_out[b] = tail[:, :hidden_size]
        end_w_out[b] = tail[:channels, hidden_size:]
    grad_in_out[...] = grad_in_ref[...]
    for made in stores:
        made.wait()


def finish_call(sizes, grad_in, units, misc):
    blocks, layers, kernel, hidden_size, channels, frames = sizes
    half, deep, wide = channels // 2, kernel * hidden_size, 2 * hidden_size
    vmem = pl.BlockSpec(memory_space=pltpu.VMEM)
    hbm = pl.BlockSpec(memory_space=pl.ANY)
    dims = [
        (1, channels, frames),
        (blocks, channels),
        (blocks, channels),
        (blocks, 4, 4),
        (blocks, half, hidden_size),
        (blocks, hidden_size),
        (blocks, layers, deep, wide),
        (blocks, layers, wide),
        (blocks, layers - 1, hidden_size, wide),
        (layers - 1, blocks, wide),
        (blocks, hidden_size, hidden_size),
        (blocks, hidden_size),
        (blocks, channels, hidden_size),
        (blocks, channels),
    ]
    large = (6, 8)
    return pl.pallas_call(
        functools.partial(finish_kernel, sizes),
        name="flow_finish",
        out_shape=[jax.ShapeDtypeStruct(d, f32) for d in dims],
        in_specs=[vmem, vmem, vmem],
        out_specs=[hbm if i in large else vmem for i in range(len(dims))],
        scratch_shapes=[
            pltpu.SemaphoreType.DMA((2 * blocks * layers,)),
        ],
        compiler_params=pltpu.CompilerParams(vmem_limit_bytes=32 * 2**20),
    )(units, misc, grad_in)


def backward_call(count, lengths, grad_det, grad_out, params, saved):
    (norm_bias, norm_logs, mix, start_w, _, conv_w, _, res_w, _, last_w, _, end_w, _) = params
    hid, tanh_all, sig_all, mixed, wn, scale, x_all = saved
    _, channels, frames = grad_out.shape
    conv_w, res_w, start_w = conv_w.swapaxes(2, 3), res_w.swapaxes(2, 3), start_w.swapaxes(1, 2)
    blocks, layers, deep, wide = conv_w.shape
    hidden_size = wide // 2
    kernel = deep // hidden_size
    half = channels // 2
    steps = blocks * layers
    sizes = (blocks, layers, kernel, hidden_size, channels, frames)
    bits = count.bit_length() - 1
    halvings = 4
    depth = 2
    rows = deep + hidden_size
    part_rows = rows // PARTS
    vmem = pl.BlockSpec(memory_space=pltpu.VMEM)
    smem = pl.BlockSpec(memory_space=pltpu.SMEM)
    hbm = pl.BlockSpec(memory_space=pl.ANY)
    shape = jax.ShapeDtypeStruct
    shares = [2 ** -min(hop + 1, halvings) for hop in range(bits)]
    hops = bits + halvings
    starts = [
        row if len(row) == hops + 1 else [ready + 2 * k for k in range(hops + 1)]
        for row, ready in zip(STARTS, READY)
    ]
    order = drain_order(starts, bits, halvings, depth, steps, part_rows, blocks * MISC)
    return pl.pallas_call(
        functools.partial(backward_kernel, sizes, bits, halvings, depth, starts, order),
        name="flow_backward",
        out_shape=[
            pltpu.VMEM((1, channels, frames), f32),
            pltpu.VMEM((steps, rows, wide), f32),
            pltpu.VMEM((blocks * MISC, wide), f32),
        ],
        in_specs=[smem, smem, smem] + [vmem] * 6 + [hbm] * 9,
        out_specs=[vmem, vmem, vmem],
        scratch_shapes=[
            pltpu.VMEM((SLOTS, 3, hidden_size, frames), f32),
            pltpu.VMEM((blocks, channels, frames), f32),
            pltpu.VMEM((blocks, hidden_size, frames), f32),
            pltpu.VMEM((blocks, half, frames), f32),
            pltpu.VMEM((blocks, channels, frames), f32),
            pltpu.VMEM((SLOTS, deep, wide), f32),
            pltpu.VMEM((SLOTS, hidden_size, wide), f32),
            pltpu.VMEM((deep + 16, frames), bf16),
            pltpu.VMEM((deep + 16, frames), bf16),
            pltpu.VMEM((kernel * wide, frames), bf16),
            pltpu.VMEM((kernel * wide, frames), bf16),
            pltpu.VMEM((hidden_size, kernel * wide), bf16),
            pltpu.VMEM((hidden_size, kernel * wide), bf16),
            pltpu.VMEM((hidden_size + 16, frames), bf16),
            pltpu.VMEM((hidden_size + 16, frames), bf16),
            pltpu.VMEM((wide, frames), bf16),
            pltpu.VMEM((wide, frames), bf16),
            pltpu.VMEM((hidden_size, frames), f32),
            pltpu.VMEM((hidden_size, frames), f32),
            pltpu.VMEM((hidden_size, frames), f32),
            pltpu.VMEM((channels, frames), f32),
            pltpu.VMEM((half, frames), f32),
            pltpu.VMEM((hidden_size, 128), f32),
            pltpu.SemaphoreType.DMA((SLOTS, 3)),
            pltpu.SemaphoreType.DMA((SLOTS, 2)),
            pltpu.SemaphoreType.DMA((blocks, 4)),
            pltpu.SemaphoreType.DMA((depth * PARTS + 1, 2, bits)),
            pltpu.SemaphoreType.DMA((steps * PARTS + 1, 2, halvings)),
            pltpu.SemaphoreType.REGULAR((depth * PARTS, bits)),
            pltpu.SemaphoreType.REGULAR((steps * PARTS + 1, halvings)),
        ]
        + [pltpu.VMEM((depth, PARTS, int(part_rows * s), wide), f32) for s in shares]
        + [pltpu.VMEM((int(blocks * MISC * s), wide), f32) for s in shares],
        compiler_params=pltpu.CompilerParams(
            collective_id=0, has_side_effects=True, vmem_limit_bytes=SUM_LIMIT
        ),
    )(lengths, grad_det, mix, grad_out, norm_bias, norm_logs, start_w, last_w, end_w, conv_w, res_w,
      hid, tanh_all, sig_all, mixed, wn, scale, x_all)


def shards(mesh_size, mel, lengths, *rest):
    params, grad_out, grad_det = rest[:13], rest[13], rest[14]
    flowed, logdet, *saved = forward_call(mel, lengths, params)
    blocks, layers, wide, deep = params[5].shape
    hidden_size = wide // 2
    sizes = (blocks, layers, deep // hidden_size, hidden_size, mel.shape[1], mel.shape[2])
    summed = backward_call(mesh_size, lengths, grad_det, grad_out, params, saved)
    grads = list(finish_call(sizes, *summed))
    for i in (6, 8):
        grads[i] = grads[i].swapaxes(2, 3)
    grads[4] = grads[4].swapaxes(1, 2)
    grads[9] = grads[9].swapaxes(0, 1)
    return (flowed, logdet[0, :1], *grads)


def solution(mesh):
    split_first, whole = P("dp", None, None), P()
    in_specs = (split_first, P("dp")) + (whole,) * 13 + (split_first, P("dp"))
    out_specs = (split_first, P("dp"), split_first) + (whole,) * 13
    return jax.shard_map(
        functools.partial(shards, mesh.shape["dp"]),
        mesh=mesh,
        in_specs=in_specs,
        out_specs=out_specs,
        check_vma=False,
    )
```

```python
import functools

import jax
import jax.numpy as jnp
from jax import lax
from jax.experimental import pallas as pl
from jax.experimental.pallas import tpu as pltpu
from jax.sharding import PartitionSpec as P

f32, bf16 = jnp.float32, jnp.bfloat16
NN = (((1,), (0,)), ((), ()))
NT = (((1,), (1,)), ((), ()))
TN = (((0,), (0,)), ((), ()))
VMEM_LIMIT = 60 * 2**20


def dot(left, right, form=NN):
    return lax.dot_general(left, right, form, preferred_element_type=f32)


def split(value):
    high = value.astype(bf16)
    return high, (value - high.astype(f32)).astype(bf16)


def dot3(left, right, form=NN):
    (left_high, left_low), (right_high, right_low) = left, right
    return (
        dot(left_high, right_high, form)
        + dot(left_high, right_low, form)
        + dot(left_low, right_high, form)
    )


def mix_matrix(mix_ref, block, channels):
    half = channels // 2
    rows = lax.broadcasted_iota(jnp.int32, (channels, channels), 0)
    cols = lax.broadcasted_iota(jnp.int32, (channels, channels), 1)
    row_top, col_top = rows < half, cols < half
    row_in = jnp.where(row_top, rows, rows - half)
    col_in = jnp.where(col_top, cols, cols - half)
    row_member = jnp.where(row_top, 0, 2) + (row_in & 1)
    col_member = jnp.where(col_top, 0, 2) + (col_in & 1)
    same = (row_in >> 1) == (col_in >> 1)
    pair = row_member * 4 + col_member
    result = jnp.zeros((channels, channels), f32)
    for i in range(4):
        for j in range(4):
            result = jnp.where(pair == 4 * i + j, mix_ref[block, i, j], result)
    return jnp.where(same, result, 0.0)


def inverse_logdet(mix_ref, block):
    shape = (8, 128)
    left = [[jnp.full(shape, mix_ref[block, i, j], f32) for j in range(4)] for i in range(4)]
    right = [[jnp.full(shape, float(i == j), f32) for j in range(4)] for i in range(4)]
    log_total = jnp.zeros(shape, f32)
    for k in range(4):
        pivot = left[k][k]
        log_total = log_total + jnp.log(pivot)
        left[k] = [v / pivot for v in left[k]]
        right[k] = [v / pivot for v in right[k]]
        for i in range(4):
            if i != k:
                factor = left[i][k]
                left[i] = [v - factor * w for v, w in zip(left[i], left[k])]
                right[i] = [v - factor * w for v, w in zip(right[i], right[k])]
    return right, log_total


def fill_columns(rows_ref, cols_ref, block, vectors):
    rows_ref[...] = jnp.zeros_like(rows_ref)
    for j, vector in enumerate(vectors):
        rows_ref[j : j + 1, : vector.shape[1]] = vector
    cols_ref[...] = rows_ref[...].T


def frame_mask(length, frames):
    return (lax.broadcasted_iota(jnp.int32, (1, frames), 1) < length).astype(f32)


ROWS = 16


def chunks(rows, size=ROWS):
    return [slice(at, min(at + size, rows)) for at in range(0, rows, size)]


def shift_by(at, by):
    return slice(at.start + by, at.stop + by)


def fill_rows(value, at, high_ref, low_ref, kernel, channels, sign):
    high, low = split(value)
    for k in range(kernel):
        move = (sign * (k - kernel // 2)) % value.shape[1]
        to = shift_by(at, k * channels)
        high_ref[to] = pltpu.roll(high, move, 1) if move else high
        low_ref[to] = pltpu.roll(low, move, 1) if move else low


def fill_split(source, high_ref, low_ref, size=64):
    for at in chunks(source.shape[0], size):
        high_ref[at], low_ref[at] = split(source[at])


def forward_kernel(
    sizes,
    length_ref,
    mix_ref,
    x_ref,
    norm_bias_ref,
    norm_logs_ref,
    start_w_ref,
    start_b_ref,
    conv_w_ref,
    conv_b_ref,
    res_w_ref,
    res_b_ref,
    last_w_ref,
    last_b_ref,
    end_w_ref,
    end_b_ref,
    flowed_ref,
    logdet_ref,
    hid_out,
    tanh_out,
    sig_out,
    mixed_out,
    wn_out,
    scale_out,
    x_out,
    x_buf,
    hid_buf,
    tanh_buf,
    sig_buf,
    mixed_buf,
    wn_buf,
    scale_buf,
    conv_stage,
    res_stage,
    stack_high,
    stack_low,
    conv_high,
    conv_low,
    res_high,
    res_low,
    gated_high,
    gated_low,
    out_buf,
    skip_buf,
    det_buf,
    rows_buf,
    cols_buf,
    in_sem,
    out_sem,
    misc_sem,
):
    blocks, layers, kernel, hidden_size, channels, frames = sizes
    half = channels // 2
    steps = blocks * layers
    length = length_ref[0]
    mask = frame_mask(length, frames)

    def conv_copy(block, layer):
        at = block * layers + layer
        return pltpu.make_async_copy(conv_w_ref.at[block, layer], conv_stage.at[at], in_sem.at[0, at])

    def res_copy(block, layer):
        at = block * layers + layer
        return pltpu.make_async_copy(res_w_ref.at[block, layer], res_stage.at[at], in_sem.at[1, at])

    def saves(step):
        return [
            pltpu.make_async_copy(buf.at[step], out.at[step], out_sem.at[i, step])
            for i, (buf, out) in enumerate(
                ((hid_buf, hid_out), (tanh_buf, tanh_out), (sig_buf, sig_out))
            )
        ]

    def block_saves(block):
        return [
            pltpu.make_async_copy(buf.at[block], out.at[block], misc_sem.at[i, block])
            for i, (buf, out) in enumerate(
                ((mixed_buf, mixed_out), (x_buf, x_out), (wn_buf, wn_out), (scale_buf, scale_out))
            )
        ]

    for block in range(blocks):
        for layer in range(layers):
            conv_copy(block, layer).start()
            if layer < layers - 1:
                res_copy(block, layer).start()
    x_buf[0] = x_ref[0]
    det_buf[...] = jnp.zeros_like(det_buf)

    def run_block(block, carry):
        fill_columns(
            rows_buf,
            cols_buf,
            block,
            [conv_b_ref[block, pl.ds(l, 1), :] for l in range(layers)]
            + [res_b_ref[l, pl.ds(block, 1), :] for l in range(layers - 1)]
            + [
                r[pl.ds(block, 1), :]
                for r in (start_b_ref, last_b_ref, end_b_ref, norm_bias_ref, norm_logs_ref)
            ],
        )
        base = 2 * layers - 1
        start_b = cols_buf[:hidden_size, base : base + 1]
        last_b = cols_buf[:hidden_size, base + 1 : base + 2]
        end_b = cols_buf[:channels, base + 2 : base + 3]
        norm_b = cols_buf[:channels, base + 3 : base + 4]
        norm_l = cols_buf[:channels, base + 4 : base + 5]
        normed = (norm_b + jnp.exp(norm_l) * x_buf[block]) * mask
        mixed = dot3(split(mix_matrix(mix_ref, block, channels)), split(normed))
        mixed_buf[block] = mixed
        for save in block_saves(block)[:2]:
            save.start()
        hidden = (dot3(split(start_w_ref[block]), split(mixed[:half]), TN) + start_b) * mask
        hid_buf[block * layers] = hidden

        for layer in range(layers):
            step = block * layers + layer
            last = layer == layers - 1
            saves(step)[0].start()
            conv_copy(block, layer).wait()
            if not last:
                res_copy(block, layer).wait()
            fill_split(conv_stage.at[step], conv_high, conv_low)
            for at in chunks(hidden_size):
                fill_rows(hid_buf[step, at], at, stack_high, stack_low, kernel, hidden_size, -1)
            if not last:
                fill_split(res_stage.at[step], res_high, res_low)
            out_buf[...] = dot3((conv_high[...], conv_low[...]), (stack_high[...], stack_low[...]), TN)
            for at in chunks(hidden_size):
                below = shift_by(at, hidden_size)
                tanh_part = jnp.tanh(out_buf[at] + cols_buf[at, layer : layer + 1])
                sig_part = 0.5 * jnp.tanh(0.5 * (out_buf[below] + cols_buf[below, layer : layer + 1])) + 0.5
                tanh_buf[step, at] = tanh_part
                sig_buf[step, at] = sig_part
                gated_high[at], gated_low[at] = split(tanh_part * sig_part)
            gated = (gated_high[...], gated_low[...])
            if last:
                skip_buf[...] += dot3(split(last_w_ref[block]), gated)
            else:
                out_buf[...] = dot3((res_high[...], res_low[...]), gated, TN)
                bias = slice(layers + layer, layers + layer + 1)
                for at in chunks(hidden_size):
                    below = shift_by(at, hidden_size)
                    res = out_buf[below] + cols_buf[below, bias]
                    skip_buf[at] = res + (skip_buf[at] if layer else last_b[at])
                    hid_buf[step + 1, at] = (hid_buf[step, at] + (out_buf[at] + cols_buf[at, bias])) * mask
            for save in saves(step)[1:]:
                save.start()
        wavenet = skip_buf[...] * mask
        wn_buf[block] = wavenet
        out = dot3(split(end_w_ref[block]), split(wavenet)) + end_b
        scale = jnp.exp(out[half:])
        scale_buf[block] = scale
        mixed = mixed_buf[block]
        moved = (out[:half] + scale * mixed[half:]) * mask
        _, log_det = inverse_logdet(mix_ref, block)
        det_buf[0:1, :] += jnp.sum(norm_l) + log_det[0:1, :] * (channels // 4)
        det_buf[1:2, :] += jnp.full((1, 128), jnp.sum(out[half:] * mask))
        x_buf[block + 1, :half] = mixed[:half]
        x_buf[block + 1, half:] = moved
        for save in block_saves(block)[2:]:
            save.start()
        return carry

    lax.fori_loop(0, blocks, run_block, 0)
    flowed_ref[0] = x_buf[blocks]
    logdet_ref[...] = det_buf[0:1, :] + det_buf[1:2, :] / length.astype(f32)

    def finish(step, carry):
        for save in saves(step):
            save.wait()
        return carry

    lax.fori_loop(0, steps, finish, 0)

    def finish_block(block, carry):
        for save in block_saves(block):
            save.wait()
        return carry

    lax.fori_loop(0, blocks, finish_block, 0)


def forward_call(mel, lengths, params):
    (norm_bias, norm_logs, mix, start_w, start_b, conv_w, conv_b, res_w, res_b, last_w, last_b, end_w, end_b) = params
    _, channels, frames = mel.shape
    conv_w, res_w = conv_w.swapaxes(2, 3), res_w.swapaxes(2, 3)
    start_w, res_b = start_w.swapaxes(1, 2), res_b.swapaxes(0, 1)
    blocks, layers, deep, wide = conv_w.shape
    hidden_size = wide // 2
    kernel = deep // hidden_size
    half = channels // 2
    steps = blocks * layers
    sizes = (blocks, layers, kernel, hidden_size, channels, frames)
    vmem = pl.BlockSpec(memory_space=pltpu.VMEM)
    smem = pl.BlockSpec(memory_space=pltpu.SMEM)
    hbm = pl.BlockSpec(memory_space=pl.ANY)
    shape = jax.ShapeDtypeStruct
    act = (steps, hidden_size, frames)
    return pl.pallas_call(
        functools.partial(forward_kernel, sizes),
        name="flow_forward",
        out_shape=[
            shape((1, channels, frames), f32),
            shape((1, 128), f32),
            shape(act, f32),
            shape(act, f32),
            shape(act, f32),
            shape((blocks, channels, frames), f32),
            shape((blocks, hidden_size, frames), f32),
            shape((blocks, half, frames), f32),
            shape((blocks, channels, frames), f32),
        ],
        in_specs=[smem, smem, vmem, vmem, vmem, vmem, vmem, hbm, vmem, hbm, vmem, vmem, vmem, vmem, vmem],
        out_specs=[vmem, vmem] + [hbm] * 7,
        scratch_shapes=[
            pltpu.VMEM((blocks + 1, channels, frames), f32),
            pltpu.VMEM(act, f32),
            pltpu.VMEM(act, f32),
            pltpu.VMEM(act, f32),
            pltpu.VMEM((blocks, channels, frames), f32),
            pltpu.VMEM((blocks, hidden_size, frames), f32),
            pltpu.VMEM((blocks, half, frames), f32),
            pltpu.VMEM((steps, deep, wide), f32),
            pltpu.VMEM((steps, hidden_size, wide), f32),
            pltpu.VMEM((deep, frames), bf16),
            pltpu.VMEM((deep, frames), bf16),
            pltpu.VMEM((deep, wide), bf16),
            pltpu.VMEM((deep, wide), bf16),
            pltpu.VMEM((hidden_size, wide), bf16),
            pltpu.VMEM((hidden_size, wide), bf16),
            pltpu.VMEM((hidden_size, frames), bf16),
            pltpu.VMEM((hidden_size, frames), bf16),
            pltpu.VMEM((wide, frames), f32),
            pltpu.VMEM((hidden_size, frames), f32),
            pltpu.VMEM((8, 128), f32),
            pltpu.VMEM((16, wide), f32),
            pltpu.VMEM((wide, 16), f32),
            pltpu.SemaphoreType.DMA((2, steps)),
            pltpu.SemaphoreType.DMA((3, steps)),
            pltpu.SemaphoreType.DMA((4, blocks)),
        ],
        compiler_params=pltpu.CompilerParams(vmem_limit_bytes=VMEM_LIMIT),
    )(lengths, mix, mel, norm_bias, norm_logs, start_w, start_b, conv_w, conv_b, res_w, res_b, last_w, last_b, end_w, end_b)
MESH = pl.DeviceIdType.MESH
MISC = 128
SLOTS = 3
SUM_LIMIT = 47 * 2**20
PARTS = 3
POINTS = 6
READY = (2, 3, 4)
STARTS = ((2, 4, 6, 10, 15, 21, 24, 29, 34, 36), (3, 4, 7, 10, 13, 17, 23, 26, 29, 31), (4, 5, 9, 11, 14, 19, 21, 25, 31, 34))


POINT_US = (2.2, 1.0, 1.1, 1.1, 1.1, 2.6)
RATES = {"x": 58.6, "y": 58.6, "z": 61.8, "middle": 55.3}
CORE_ROWS = 420.0
LATENCY = {"core": 0.75, "far": 2.6}


class Link:
    def __init__(self, rate):
        self.queues, self.clock, self.rate = ([], []), 0.0, rate

    def run(self, until):
        while any(self.queues) and self.clock < until:
            heads = [queue[0] for queue in self.queues if queue]
            rate = self.rate / len(heads)
            spent = min(min(head[0] for head in heads) / rate, until - self.clock)
            self.clock += spent
            for queue in self.queues:
                if queue:
                    queue[0][0] -= spent * rate
                    if queue[0][0] < 1e-6:
                        queue.pop(0)[1] = self.clock
        if self.clock < until < float("inf"):
            self.clock = until

    def add(self, now, core, rows):
        self.run(now)
        job = [rows, None]
        self.queues[core].append(job)
        return self, job


class Plan:
    def __init__(self, bits, halvings, steps, part_rows, misc_rows):
        self.bits, self.hops, self.steps = bits, bits + halvings, steps
        self.rows = (part_rows, misc_rows)
        self.links = {name: Link(rate) for name, rate in RATES.items()}
        self.links |= {("core", core): Link(CORE_ROWS) for core in range(2)}
        self.clock, self.jobs, self.taken = 0.0, {}, {}
        sizes = [2 ** -(h + 1) for h in range(halvings)]
        self.sizes = sizes + [sizes[-1]] * (bits - halvings) + sizes[::-1]

    def name(self, part, k):
        near = ("z", "a", "b") if part == PARTS - 1 else ("a", "b", "z")
        return ["core", *near, *["far"] * (self.bits - 4), *reversed(near), "core"][k]

    def start(self, unit, part, k):
        name, jobs = self.name(part, k), []
        rows = self.sizes[k] * self.rows[unit == self.steps]
        for core in range(2):
            if name == "core":
                jobs.append(self.links[name, core].add(self.clock, core, rows))
                continue
            link = "z" if name in ("z", "far") else "xy"[(name == "b") ^ core]
            jobs.append(self.links[link].add(self.clock, core, rows))
            if name == "far":
                jobs.append(self.links["middle"].add(self.clock, core, 2 * rows))
        self.jobs[unit, part] = jobs, LATENCY.get(name, 2.1)

    def arrival(self, unit, part, until=float("inf")):
        if not self.taken.get((unit, part)):
            return 0.0
        jobs, latency = self.jobs[unit, part]
        for link, job in jobs:
            if job[1] is None:
                link.run(until)
            if job[1] is None:
                return float("inf")
        return max(job[1] for _, job in jobs) + latency

    def take(self, unit, part, k):
        if k:
            self.clock = max(self.clock, self.arrival(unit, part)) + 0.1
        self.taken[unit, part] = k + 1
        if k < self.hops:
            self.start(unit, part, k)


def drain_order(starts, bits, halvings, depth, steps, part_rows, misc_rows):
    plan = Plan(bits, halvings, steps, part_rows, misc_rows)
    for layer in range(steps):
        for point in range(POINTS):
            plan.clock += POINT_US[point]
            for lag, part, k in due_steps(starts, point):
                if layer >= lag:
                    plan.take(layer - lag, part, k)
    order, taken = [], plan.taken
    waiting = [(unit, part) for unit in range(steps) for part in range(PARTS)] + [(steps, 0)]
    waiting = [w for w in waiting if taken.get(w, 0) <= plan.hops]
    while waiting:
        ready = []
        for unit, part in waiting:
            k = taken.get((unit, part), 0)
            slot_free = unit in range(depth) or unit == steps or k >= bits or taken[unit - depth, part] > k + 1
            if slot_free and plan.arrival(unit, part, plan.clock) <= plan.clock:
                ready.append((k >= bits, unit, part, k))
        if not ready:
            plan.clock += 0.1
            continue
        _, unit, part, k = min(ready)
        plan.take(unit, part, k)
        order.append((unit, part, k))
        if k == plan.hops:
            waiting.remove((unit, part))
    return order


def due_steps(starts, point):
    due = [
        (start // POINTS, part, k)
        for part, row in enumerate(starts)
        for k, start in enumerate(row)
        if start % POINTS == point
    ]
    return sorted(due, key=lambda due: (-due[2], due[0], due[1]))


class Exchange:
    def __init__(self, bits, halvings):
        self.bits, self.halvings = bits, halvings
        self.hops = bits + halvings
        self.me = lax.axis_index("dp")
        self.value = [lax.rem(self.me // 2**b, 2) for b in range(bits)]
        self.orders = [self.order(turn) for turn in range(2)]
        self.partners = [[self.partner(hop) for hop in order] for order in self.orders]

    def order(self, turn):
        pairs = [(self.value[b], 2**b) for b in range(self.bits)]

        def either(flag, yes, no):
            return tuple(flag * y + (1 - flag) * n for y, n in zip(yes, no))

        odd = self.value[0]
        first = either(odd, pairs[2], pairs[1])
        second = either(odd, pairs[1], pairs[2])
        return [
            pairs[0],
            either(turn, pairs[3], first),
            either(turn, first, second),
            either(turn, second, pairs[3]),
        ] + pairs[4:]

    def partner(self, hop):
        bit, stride = hop
        return (self.me + (1 - 2 * bit) * stride,)

    def spans(self, turn, rows):
        at, size, result = 0, rows, []
        for bit, _ in self.orders[turn][: self.halvings]:
            size //= 2
            result.append((at + bit * size, at + (1 - bit) * size, size))
            at = at + bit * size
        return result


class Reduction:
    def __init__(self, exchange, turn, spans, source, slots, sems, base, later=None):
        self.x, self.source = exchange, source
        self.slots, self.sems, self.base, self.later = slots, sems, base, later
        self.partners, self.spans = exchange.partners[turn], spans

    def rows_of(self, at, size):
        return pl.ds(pl.multiple_of(self.base + at, 8), size)

    def copy_sem(self, side, hop):
        out, back = self.sems[0], self.sems[1]
        return out.at[side, hop] if hop < self.x.bits else back.at[side, hop - self.x.bits]

    def copy(self, hop):
        halvings, bits = self.x.halvings, self.x.bits
        if hop < bits:
            if hop < halvings:
                _, at, size = self.spans[hop]
            else:
                at, _, size = self.spans[-1]
            src = self.source.at[self.rows_of(at, size)]
            dst = self.slots[hop]
            to = self.partners[hop]
        else:
            level = halvings - 1 - (hop - bits)
            at, _, size = self.spans[level]
            src = dst = self.source.at[self.rows_of(at, size)]
            to = self.partners[level]
        return pltpu.make_async_remote_copy(
            src_ref=src,
            dst_ref=dst,
            send_sem=self.copy_sem(0, hop),
            recv_sem=self.copy_sem(1, hop),
            device_id=to,
            device_id_type=MESH,
        )

    def step(self, k):
        x = self.x
        if k > 0:
            done = k - 1
            self.copy(done).wait()
            if done < x.bits:
                at, _, size = self.spans[min(done, x.halvings - 1)]
                where = self.rows_of(at, size)
                self.source[where] += self.slots[done][...]
                self.free(done)
            if done < x.halvings:
                pl.semaphore_signal(
                    self.sems[3].at[done], inc=1, device_id=self.partners[done], device_id_type=MESH
                )
        if k < x.hops:
            if k < x.bits:
                self.wait_free(k)
            else:
                pl.semaphore_wait(self.sems[3].at[x.hops - 1 - k], 1)
            self.copy(k).start()

    def free(self, hop):
        if self.later is not None:
            credit, exists = self.later

            @pl.when(exists)
            def _():
                pl.semaphore_signal(
                    credit.at[hop],
                    inc=1,
                    device_id=self.partners[hop],
                    device_id_type=MESH,
                )

    def wait_free(self, hop):
        credit, needed = self.sems[2] if self.sems[2] is not None else (None, None)
        if credit is not None:

            @pl.when(needed)
            def _():
                pl.semaphore_wait(credit.at[hop], 1)


def backward_kernel(
    sizes,
    bits,
    halvings,
    depth,
    starts,
    order,
    length_ref,
    grad_det_ref,
    mix_ref,
    grad_out_ref,
    norm_bias_ref,
    norm_logs_ref,
    start_w_ref,
    last_w_ref,
    end_w_ref,
    conv_w_ref,
    res_w_ref,
    hid_ref,
    tanh_ref,
    sig_ref,
    mixed_ref,
    wn_ref,
    scale_ref,
    x_ref,
    grad_in_ref,
    unit_buf,
    misc_buf,
    *scratch,
):
    (
        act_buf,
        mixed_buf,
        wn_buf,
        scale_buf,
        x_buf,
        conv_stage,
        res_stage,
        stack_high,
        stack_low,
        back_high,
        back_low,
        turned_high,
        turned_low,
        gated_high,
        gated_low,
        pair_high,
        pair_low,
        grad_skip,
        grad_hid,
        grad_gated,
        grad_flow,
        grad_changed,
        columns_buf,
        act_sem,
        weight_sem,
        block_sem,
        out_copy_sem,
        back_copy_sem,
        credit_sem,
        clear_sem,
    ) = scratch[:30]
    slot_bufs = scratch[30 : 30 + bits]
    misc_slots = scratch[30 + bits :]
    blocks, layers, kernel, hidden_size, channels, frames = sizes
    half = channels // 2
    steps = blocks * layers
    deep = kernel * hidden_size
    wide = 2 * hidden_size
    middle = kernel // 2
    length = length_ref[0]
    mask = frame_mask(length, frames)
    grad_det = grad_det_ref[0]
    exchange = Exchange(bits, halvings)

    part_rows = (deep + hidden_size) // PARTS
    spans = [exchange.spans(turn, part_rows) for turn in range(2)]

    def reduction(unit, part):
        slot = lax.rem(unit, depth)
        after = unit + depth
        return Reduction(
            exchange,
            int(part == PARTS - 1),
            spans[int(part == PARTS - 1)],
            unit_buf.at[unit],
            [b.at[slot, part] for b in slot_bufs],
            (
                out_copy_sem.at[slot * PARTS + part],
                back_copy_sem.at[unit * PARTS + part],
                (credit_sem.at[slot * PARTS + part], unit >= depth),
                clear_sem.at[unit * PARTS + part],
            ),
            part * part_rows,
            (credit_sem.at[slot * PARTS + part], after < steps),
        )

    misc_sum = Reduction(
        exchange,
        0,
        exchange.spans(0, blocks * MISC),
        misc_buf,
        misc_slots,
        (
            out_copy_sem.at[depth * PARTS],
            back_copy_sem.at[steps * PARTS],
            None,
            clear_sem.at[steps * PARTS],
        ),
        0,
    )

    def tick(step, point):
        for lag, part, k in due_steps(starts, point):
            unit = step - lag

            @pl.when(unit >= 0)
            def _(unit=unit, part=part, k=k):
                reduction(unit, part).step(k)

    def act_copies(step):
        slot = lax.rem(step, SLOTS)
        at = steps - 1 - step
        return [
            pltpu.make_async_copy(ref.at[at], act_buf.at[slot, i], act_sem.at[slot, i])
            for i, ref in enumerate((hid_ref, tanh_ref, sig_ref))
        ]

    def weight_copies(step):
        slot = lax.rem(step, SLOTS)
        block, layer = blocks - 1 - step // layers, layers - 1 - lax.rem(step, layers)
        conv = pltpu.make_async_copy(conv_w_ref.at[block, layer], conv_stage.at[slot], weight_sem.at[slot, 0])
        res = pltpu.make_async_copy(
            res_w_ref.at[block, jnp.minimum(layer, layers - 2)], res_stage.at[slot], weight_sem.at[slot, 1]
        )
        return [conv, res]

    def block_copies(block):
        return [
            pltpu.make_async_copy(ref.at[block], buf.at[block], block_sem.at[block, i])
            for i, (ref, buf) in enumerate(
                ((wn_ref, wn_buf), (scale_ref, scale_buf), (mixed_ref, mixed_buf), (x_ref, x_buf))
            )
        ]

    for copy in act_copies(0) + block_copies(blocks - 1) + weight_copies(0):
        copy.start()

    barrier = pltpu.get_barrier_semaphore()
    for b in range(bits):
        pl.semaphore_signal(
            barrier, inc=1, device_id=exchange.partner((exchange.value[b], 2**b)), device_id_type=MESH
        )
    grad_flow[...] = grad_out_ref[0]
    misc_buf[...] = jnp.zeros_like(misc_buf)
    columns_buf[...] = jnp.zeros_like(columns_buf)
    for high, low, rows in ((stack_high, stack_low, deep), (gated_high, gated_low, hidden_size)):
        high[rows:, :] = jnp.ones((16, frames), bf16)
        low[rows:, :] = jnp.zeros((16, frames), bf16)
    pl.semaphore_wait(barrier, bits)
    for step in range(1, SLOTS - 1):
        for copy in act_copies(step) + weight_copies(step):
            copy.start()
    for block in reversed(range(blocks - 1)):
        for copy in block_copies(block):
            copy.start()

    def run_step(step, carry):
        block = blocks - 1 - step // layers
        layer = layers - 1 - lax.rem(step, layers)
        slot = lax.rem(step, SLOTS)
        misc_at = block * MISC
        for copy in act_copies(step) + weight_copies(step):
            copy.wait()

        @pl.when(step + SLOTS - 1 < steps)
        def _():
            for copy in act_copies(step + SLOTS - 1) + weight_copies(step + SLOTS - 1):
                copy.start()

        for at in chunks(hidden_size):
            gated_high[at], gated_low[at] = split(act_buf[slot, 1, at] * act_buf[slot, 2, at])

        @pl.when(layer == layers - 1)
        def _():
            for copy in block_copies(block):
                copy.wait()
            moved_grad = grad_flow[half:] * mask
            changed_grad = moved_grad * scale_buf[block]
            grad_changed[...] = changed_grad
            logs_grad = changed_grad * mixed_buf[block, half:] + (grad_det / length.astype(f32)) * mask
            out_grad = jnp.concatenate([moved_grad, logs_grad], axis=0)
            columns_buf[:channels, 0:1] = jnp.sum(out_grad, axis=1, keepdims=True)
            out_split = split(out_grad)
            end_grad = dot3(out_split, split(wn_buf[block]), NT)
            skip = dot3(split(end_w_ref[block]), out_split, TN) * mask
            columns_buf[:, 1:2] = jnp.sum(skip, axis=1, keepdims=True)
            skip_split = split(skip)
            pair_high[hidden_size:], pair_low[hidden_size:] = skip_split
            gated = (gated_high[:hidden_size], gated_low[:hidden_size])
            unit_buf[step, deep:, :hidden_size] = dot3(skip_split, gated, NT)
            unit_buf[step, deep : deep + channels, hidden_size:] = end_grad
            grad_gated[...] = dot3(split(last_w_ref[block]), skip_split, TN)
            grad_hid[...] = jnp.zeros_like(grad_hid)

        @pl.when(layer < layers - 1)
        def _():
            masked = grad_hid[...] * mask
            grad_hid[...] = masked
            pair_high[:hidden_size], pair_low[:hidden_size] = split(masked)
            pair = (pair_high[...], pair_low[...])
            grads = dot3((gated_high[...], gated_low[...]), pair, NT)
            unit_buf[step, deep:] = grads[:hidden_size]
            misc_buf[pl.ds(misc_at + half + 8 + layers + layer, 1), :] = grads[hidden_size : hidden_size + 1]
            grad_gated[...] = dot3(split(res_stage[slot]), pair)

        tick(step, 0)
        for at in chunks(hidden_size):
            tanh_part, sig_part = act_buf[slot, 1, at], act_buf[slot, 2, at]
            inner = grad_gated[at] * sig_part
            fill_rows(inner * (1.0 - tanh_part * tanh_part), at, back_high, back_low, kernel, wide, 1)
            below = shift_by(at, hidden_size)
            fill_rows(inner * tanh_part * (1.0 - sig_part), below, back_high, back_low, kernel, wide, 1)
            fill_rows(act_buf[slot, 0, at], at, stack_high, stack_low, kernel, hidden_size, -1)
        tick(step, 1)
        center = slice(middle * wide, (middle + 1) * wide)
        for part in range(PARTS):
            at = part * part_rows
            end = at + part_rows if part < PARTS - 1 else deep + 16
            grads = dot3((stack_high[at:end], stack_low[at:end]), (back_high[center], back_low[center]), NT)
            if part < PARTS - 1:
                unit_buf[step, at:end] = grads
            else:
                unit_buf[step, at:deep] = grads[: deep - at]
                misc_buf[pl.ds(misc_at + half + 8 + layer, 1), :] = grads[deep - at : deep - at + 1]
            tick(step, 2 + part)
        for k in range(kernel):
            high, low = split(conv_stage[slot, k * hidden_size : (k + 1) * hidden_size])
            turned_high[:, k * wide : (k + 1) * wide] = high
            turned_low[:, k * wide : (k + 1) * wide] = low
        grad_hid[...] += dot3((turned_high[...], turned_low[...]), (back_high[...], back_low[...]))

        @pl.when(layer == 0)
        def _():
            hid_grad = grad_hid[...] * mask
            hid_split = split(hid_grad)
            mixed = mixed_buf[block]
            start_grad = dot3(split(mixed[:half]), hid_split, NT)
            misc_buf[pl.ds(misc_at, half), :hidden_size] = start_grad
            columns_buf[:, 2:3] = jnp.sum(hid_grad, axis=1, keepdims=True)
            passed_grad = grad_flow[:half] + dot3(split(start_w_ref[block]), hid_split)
            mixed_grad = split(jnp.concatenate([passed_grad, grad_changed[...]], axis=0))
            norm_b = jnp.transpose(jnp.broadcast_to(norm_bias_ref[pl.ds(block, 1), :], (8, channels)))[:, 0:1]
            norm_s = jnp.exp(jnp.transpose(jnp.broadcast_to(norm_logs_ref[pl.ds(block, 1), :], (8, channels)))[:, 0:1])
            scaled = norm_s * x_buf[block]
            normed = (norm_b + scaled) * mask
            mix_grad = dot3(mixed_grad, split(normed), NT)
            normed_grad = dot3(split(mix_matrix(mix_ref, block, channels)), mixed_grad, TN) * mask
            columns_buf[:channels, 3:4] = jnp.sum(normed_grad, axis=1, keepdims=True)
            columns_buf[:channels, 4:5] = jnp.sum(normed_grad * scaled, axis=1, keepdims=True) + grad_det
            grad_flow[...] = normed_grad * norm_s
            rows = columns_buf[...].T
            misc_buf[pl.ds(misc_at + half, 8), :hidden_size] = rows[:8]
            inverse, _ = inverse_logdet(mix_ref, block)
            misc_buf[pl.ds(misc_at + half + 16, 8), :] = mix_rows(
                mix_grad, inverse, grad_det * (channels // 4), wide
            )

        tick(step, POINTS - 1)
        return carry

    lax.fori_loop(0, steps, run_step, 0)
    grad_in_ref[0] = grad_flow[...]
    for unit, part, k in order:
        (misc_sum if unit == steps else reduction(unit, part)).step(k)


def mix_rows(products, inverse, factor, wide):
    channels = products.shape[0]
    half = channels // 2
    rows = lax.broadcasted_iota(jnp.int32, (channels, channels), 0)
    cols = lax.broadcasted_iota(jnp.int32, (channels, channels), 1)
    row_top, col_top = rows < half, cols < half
    row_in = jnp.where(row_top, rows, rows - half)
    col_in = jnp.where(col_top, cols, cols - half)
    row_member = jnp.where(row_top, 0, 2) + (row_in & 1)
    col_member = jnp.where(col_top, 0, 2) + (col_in & 1)
    same = (row_in >> 1) == (col_in >> 1)
    kept = jnp.where(same, products, 0.0)
    row = lax.broadcasted_iota(jnp.int32, (8, wide), 0)
    lane = lax.broadcasted_iota(jnp.int32, (8, wide), 1)
    result = jnp.zeros((8, wide), f32)
    for i in range(4):
        mine = jnp.where(row_member == i, kept, 0.0)
        for j in range(4):
            picked = jnp.where(col_member == j, mine, 0.0)
            total = jnp.sum(jnp.sum(picked, axis=0, keepdims=True), axis=1, keepdims=True)
            total = total + factor * inverse[j][i][0:1, 0:1]
            result = jnp.where((row == i) & (lane == j), total, result)
    return result


def finish_kernel(
    sizes,
    units_ref,
    misc_ref,
    grad_in_ref,
    grad_in_out,
    norm_b_out,
    norm_l_out,
    mix_out,
    start_w_out,
    start_b_out,
    conv_w_out,
    conv_b_out,
    res_w_out,
    res_b_out,
    last_w_out,
    last_b_out,
    end_w_out,
    end_b_out,
    sems,
):
    blocks, layers, kernel, hidden_size, channels, frames = sizes
    half = channels // 2
    deep = kernel * hidden_size
    steps = blocks * layers
    stores = []

    def store(source, target):
        stores.append(pltpu.make_async_copy(source, target, sems.at[len(stores)]))
        stores[-1].start()

    for step in range(steps):
        b, layer = blocks - 1 - step // layers, layers - 1 - step % layers
        store(units_ref.at[step, :deep], conv_w_out.at[b, layer])
        if layer < layers - 1:
            store(units_ref.at[step, deep:], res_w_out.at[b, layer])
    for b in range(blocks):
        at = b * MISC
        start_w_out[b] = misc_ref[at : at + half, :hidden_size]
        at += half
        for row, (out, width) in enumerate(
            ((end_b_out, channels), (last_b_out, hidden_size), (start_b_out, hidden_size), (norm_b_out, channels), (norm_l_out, channels))
        ):
            out[b : b + 1, :] = misc_ref[at + row : at + row + 1, :width]
        conv_b_out[b] = misc_ref[at + 8 : at + 8 + layers]
        for layer in range(layers - 1):
            res_b_out[layer, b : b + 1, :] = misc_ref[at + 8 + layers + layer : at + 9 + layers + layer]
        mix_out[b] = misc_ref[at + 16 : at + 20, :4]
    for b in range(blocks):
        tail = units_ref[(blocks - 1 - b) * layers, deep:]
        last_w_out[b] = tail[:, :hidden_size]
        end_w_out[b] = tail[:channels, hidden_size:]
    grad_in_out[...] = grad_in_ref[...]
    for made in stores:
        made.wait()


def finish_call(sizes, grad_in, units, misc):
    blocks, layers, kernel, hidden_size, channels, frames = sizes
    half, deep, wide = channels // 2, kernel * hidden_size, 2 * hidden_size
    vmem = pl.BlockSpec(memory_space=pltpu.VMEM)
    hbm = pl.BlockSpec(memory_space=pl.ANY)
    dims = [
        (1, channels, frames),
        (blocks, channels),
        (blocks, channels),
        (blocks, 4, 4),
        (blocks, half, hidden_size),
        (blocks, hidden_size),
        (blocks, layers, deep, wide),
        (blocks, layers, wide),
        (blocks, layers - 1, hidden_size, wide),
        (layers - 1, blocks, wide),
        (blocks, hidden_size, hidden_size),
        (blocks, hidden_size),
        (blocks, channels, hidden_size),
        (blocks, channels),
    ]
    large = (6, 8)
    return pl.pallas_call(
        functools.partial(finish_kernel, sizes),
        name="flow_finish",
        out_shape=[jax.ShapeDtypeStruct(d, f32) for d in dims],
        in_specs=[vmem, vmem, vmem],
        out_specs=[hbm if i in large else vmem for i in range(len(dims))],
        scratch_shapes=[
            pltpu.SemaphoreType.DMA((2 * blocks * layers,)),
        ],
        compiler_params=pltpu.CompilerParams(vmem_limit_bytes=32 * 2**20),
    )(units, misc, grad_in)


def backward_call(count, lengths, grad_det, grad_out, params, saved):
    (norm_bias, norm_logs, mix, start_w, _, conv_w, _, res_w, _, last_w, _, end_w, _) = params
    hid, tanh_all, sig_all, mixed, wn, scale, x_all = saved
    _, channels, frames = grad_out.shape
    conv_w, res_w, start_w = conv_w.swapaxes(2, 3), res_w.swapaxes(2, 3), start_w.swapaxes(1, 2)
    blocks, layers, deep, wide = conv_w.shape
    hidden_size = wide // 2
    kernel = deep // hidden_size
    half = channels // 2
    steps = blocks * layers
    sizes = (blocks, layers, kernel, hidden_size, channels, frames)
    bits = count.bit_length() - 1
    halvings = 4
    depth = 2
    rows = deep + hidden_size
    part_rows = rows // PARTS
    vmem = pl.BlockSpec(memory_space=pltpu.VMEM)
    smem = pl.BlockSpec(memory_space=pltpu.SMEM)
    hbm = pl.BlockSpec(memory_space=pl.ANY)
    shape = jax.ShapeDtypeStruct
    shares = [2 ** -min(hop + 1, halvings) for hop in range(bits)]
    hops = bits + halvings
    starts = [
        row if len(row) == hops + 1 else [ready + 2 * k for k in range(hops + 1)]
        for row, ready in zip(STARTS, READY)
    ]
    order = drain_order(starts, bits, halvings, depth, steps, part_rows, blocks * MISC)
    return pl.pallas_call(
        functools.partial(backward_kernel, sizes, bits, halvings, depth, starts, order),
        name="flow_backward",
        out_shape=[
            pltpu.VMEM((1, channels, frames), f32),
            pltpu.VMEM((steps, rows, wide), f32),
            pltpu.VMEM((blocks * MISC, wide), f32),
        ],
        in_specs=[smem, smem, smem] + [vmem] * 6 + [hbm] * 9,
        out_specs=[vmem, vmem, vmem],
        scratch_shapes=[
            pltpu.VMEM((SLOTS, 3, hidden_size, frames), f32),
            pltpu.VMEM((blocks, channels, frames), f32),
            pltpu.VMEM((blocks, hidden_size, frames), f32),
            pltpu.VMEM((blocks, half, frames), f32),
            pltpu.VMEM((blocks, channels, frames), f32),
            pltpu.VMEM((SLOTS, deep, wide), f32),
            pltpu.VMEM((SLOTS, hidden_size, wide), f32),
            pltpu.VMEM((deep + 16, frames), bf16),
            pltpu.VMEM((deep + 16, frames), bf16),
            pltpu.VMEM((kernel * wide, frames), bf16),
            pltpu.VMEM((kernel * wide, frames), bf16),
            pltpu.VMEM((hidden_size, kernel * wide), bf16),
            pltpu.VMEM((hidden_size, kernel * wide), bf16),
            pltpu.VMEM((hidden_size + 16, frames), bf16),
            pltpu.VMEM((hidden_size + 16, frames), bf16),
            pltpu.VMEM((wide, frames), bf16),
            pltpu.VMEM((wide, frames), bf16),
            pltpu.VMEM((hidden_size, frames), f32),
            pltpu.VMEM((hidden_size, frames), f32),
            pltpu.VMEM((hidden_size, frames), f32),
            pltpu.VMEM((channels, frames), f32),
            pltpu.VMEM((half, frames), f32),
            pltpu.VMEM((hidden_size, 128), f32),
            pltpu.SemaphoreType.DMA((SLOTS, 3)),
            pltpu.SemaphoreType.DMA((SLOTS, 2)),
            pltpu.SemaphoreType.DMA((blocks, 4)),
            pltpu.SemaphoreType.DMA((depth * PARTS + 1, 2, bits)),
            pltpu.SemaphoreType.DMA((steps * PARTS + 1, 2, halvings)),
            pltpu.SemaphoreType.REGULAR((depth * PARTS, bits)),
            pltpu.SemaphoreType.REGULAR((steps * PARTS + 1, halvings)),
        ]
        + [pltpu.VMEM((depth, PARTS, int(part_rows * s), wide), f32) for s in shares]
        + [pltpu.VMEM((int(blocks * MISC * s), wide), f32) for s in shares],
        compiler_params=pltpu.CompilerParams(
            collective_id=0, has_side_effects=True, vmem_limit_bytes=SUM_LIMIT
        ),
    )(lengths, grad_det, mix, grad_out, norm_bias, norm_logs, start_w, last_w, end_w, conv_w, res_w,
      hid, tanh_all, sig_all, mixed, wn, scale, x_all)


def shards(mesh_size, mel, lengths, *rest):
    params, grad_out, grad_det = rest[:13], rest[13], rest[14]
    flowed, logdet, *saved = forward_call(mel, lengths, params)
    blocks, layers, wide, deep = params[5].shape
    hidden_size = wide // 2
    sizes = (blocks, layers, deep // hidden_size, hidden_size, mel.shape[1], mel.shape[2])
    summed = backward_call(mesh_size, lengths, grad_det, grad_out, params, saved)
    grads = list(finish_call(sizes, *summed))
    for i in (6, 8):
        grads[i] = grads[i].swapaxes(2, 3)
    grads[4] = grads[4].swapaxes(1, 2)
    grads[9] = grads[9].swapaxes(0, 1)
    return (flowed, logdet[0, :1], *grads)


def solution(mesh):
    split_first, whole = P("dp", None, None), P()
    in_specs = (split_first, P("dp")) + (whole,) * 13 + (split_first, P("dp"))
    out_specs = (split_first, P("dp"), split_first) + (whole,) * 13
    return jax.shard_map(
        functools.partial(shards, mesh.shape["dp"]),
        mesh=mesh,
        in_specs=in_specs,
        out_specs=out_specs,
        check_vma=False,
    )
```
